32 devices in a mesh: batch: 4 (over y, x), seq: 8 (over z, core).
Axes of the slice: x: 2, y: 2, z: 4, core: 2. Of those that a mesh axis runs over, the one named last changes fastest.
Arguments:
- tokens: bfloat16 [8, 1024, 768], P('batch', 'seq'), may hold values from -6 to 6
- attn_in_weight: bfloat16 [768, 2304], replicated, may hold values from -0.21875 to 0.21875
- out_weight: bfloat16 [768, 768], replicated, may hold values from -3.5 to 3.5
- ffn_in_weight: bfloat16 [768, 3072], replicated, may hold values from -0.21875 to 0.21875
- ffn_out_weight: bfloat16 [3072, 768], replicated, may hold values from -0.109375 to 0.109375
- vera_in: bfloat16 [768, 1024], replicated, may hold values from -0.21875 to 0.21875
- vera_out: bfloat16 [1024, 768], replicated, may hold values from -0.1875 to 0.1875
- rank_scale: float32 [2, 1024], replicated, may hold values from 0.3 to 1.2
- out_scale: float32 [2, 768], replicated, may hold values from -3 to 3
- gains: float32 [2, 768], replicated, may hold values from 0.25 to 1.75
- shifts: float32 [6, 768], replicated, may hold values from -2 to 2
- ffn_bias: float32 [3072], replicated, may hold values from -2 to 2
- splits: int32 [8], P('batch'), may hold values from 1 to 1023, as said below
- out_grad: bfloat16 [8, 1024, 768], P('batch', 'seq'), may hold values from -6 to 6
Outputs:
- layer_out: bfloat16 [8, 1024, 768], P('batch', 'seq')
- in_grad: bfloat16 [8, 1024, 768], P('batch', 'seq')
- rank_scale_grad: float32 [2, 1024], replicated
- out_scale_grad: float32 [2, 768], replicated
- scale_norms: float32 [4], replicated
The draws below stay inside these ranges and needn't reach their ends.
Inputs may be any that keep to these rules, and one draw needn't show every extreme that they name: Positions below splits[s] form the first document of packed sequence s and the others the second; a token attends only within its document.
All inputs are finite; a program needn't handle non-finite values.
Results may differ from the reference program's by a relative error of at most 0.02.
Values may be sent and summed in bfloat16 or wider, within the bound.
A program may use at most 256 MiB of HBM per device.

```python
import jax
import jax.numpy as jnp
from jax import lax

D = 768
HEADS = 12
HEAD_DIM = 64
FF = 3072
RANK = 1024
SEQS = 2
SEQ_LEN = 1024
BATCH_SEQS = 8
N_SEQ = 8


def draw_splits(key, part):
    key = jax.random.fold_in(key, 7)
    subkeys = jax.random.split(key, 5)
    shard_tokens = SEQ_LEN // N_SEQ
    spread = jax.random.randint(subkeys[0], (BATCH_SEQS,), 1, SEQ_LEN)
    near_edge = jax.random.randint(subkeys[1], (BATCH_SEQS,), 1, shard_tokens)
    which_side = jax.random.randint(subkeys[2], (BATCH_SEQS,), 0, 2)
    reaching = jnp.where(which_side == 1, near_edge, SEQ_LEN - near_edge)
    chosen = jax.random.randint(subkeys[3], (BATCH_SEQS // SEQS,), 0, SEQS)
    slots = jnp.arange(BATCH_SEQS, dtype=jnp.int32) % SEQS
    result = jnp.where(slots == jnp.repeat(chosen, SEQS), reaching, spread)
    order = jax.random.permutation(subkeys[4], BATCH_SEQS)
    result = result.at[order[0]].set(1).at[order[1]].set(SEQ_LEN - 1)
    return result.astype(jnp.int32)


def shard_levels(key, shape, shards, least, largest):
    factor_of = 1.0
    for position, parts in shards:
        heights = jax.random.uniform(jax.random.fold_in(jax.random.fold_in(key, 6), position), (parts,), jnp.float32, least / len(shards), largest / len(shards))
        factor_of = factor_of * jnp.repeat(jnp.exp(heights), shape[position] // parts).reshape((-1,) + (1,) * (len(shape) - 1 - position))
    return factor_of


def gaussian(key, dims, scale, bound, pieces=(), kind=jnp.bfloat16):
    factor_of = shard_levels(key, dims, pieces, -0.22, 0.18) if pieces else 1.0
    array = jax.random.normal(key, dims, jnp.float32) * scale * factor_of
    return jnp.minimum(jnp.maximum(array, -bound), bound).astype(kind)


def setup_inputs(seed: int = 0) -> dict:
    streams_of = jax.random.split(jax.random.key(seed), 15)
    return {
        "tokens": gaussian(streams_of[0], (BATCH_SEQS, SEQ_LEN, D), 1.0, 6.0, ((0, 4), (1, 8))),
        "attn_in_weight": gaussian(streams_of[1], (D, 3 * D), D ** -0.5, 0.21875),
        "out_weight": gaussian(streams_of[2], (D, D), (max(D // 256, 1)) ** -0.5, 3.5),
        "ffn_in_weight": gaussian(streams_of[3], (D, FF), D ** -0.5, 0.21875),
        "ffn_out_weight": gaussian(streams_of[4], (FF, D), FF ** -0.5, 0.109375),
        "vera_in": gaussian(streams_of[5], (D, RANK), D ** -0.5, 0.21875),
        "vera_out": gaussian(streams_of[6], (RANK, D), RANK ** -0.5, 0.1875),
        "rank_scale": jnp.clip(jax.random.uniform(streams_of[7], (2, RANK), jnp.float32, 0.3, 1.2), 0.3, 1.2),
        "out_scale": gaussian(streams_of[8], (2, D), 0.6, 3.0, (), jnp.float32),
        "gains": jnp.clip(1.0 + 0.15 * jax.random.normal(streams_of[9], (2, D), jnp.float32), 0.25, 1.75),
        "shifts": gaussian(streams_of[10], (6, D), 0.3, 2.0, (), jnp.float32),
        "ffn_bias": gaussian(streams_of[11], (FF,), 0.3, 2.0, (), jnp.float32),
        "splits": draw_splits(jax.random.fold_in(streams_of[14], 71), 0),
        "out_grad": gaussian(streams_of[13], (BATCH_SEQS, SEQ_LEN, D), 1.0, 6.0, ((0, 4), (1, 8))),
    }


@jax.custom_vjp
def low(v):
    return lax.optimization_barrier(v.astype(jnp.bfloat16)).astype(jnp.float32)

@jax.custom_vjp
def low_back(v):
    return v

def low_keep(v):
    return (low(v), None)

def low_pass(kept, grad):
    return (grad,)

def back_keep(v):
    return (v, None)

def back_low(kept, grad):
    return (low(grad),)
low.defvjp(low_keep, low_pass)
low_back.defvjp(back_keep, back_low)

def dot_high(left_side, right_side):
    return jnp.dot(left_side, right_side, precision=lax.Precision.HIGHEST, preferred_element_type=jnp.float32)

def layer_norm(values_in, gain_row, shift_row):
    centered = values_in - lax.optimization_barrier(jnp.mean(values_in, axis=-1, keepdims=True))
    variance = lax.optimization_barrier(jnp.mean(centered * centered, axis=-1, keepdims=True))
    return centered * lax.rsqrt(variance + 1e-05) * gain_row + shift_row

def heads_first(block):
    return block.reshape(SEQS, SEQ_LEN, HEADS, HEAD_DIM).transpose(0, 2, 1, 3).reshape(SEQS * HEADS, SEQ_LEN, HEAD_DIM)

def heads_back(block):
    return block.reshape(SEQS, HEADS, SEQ_LEN, HEAD_DIM).transpose(0, 2, 1, 3).reshape(SEQS * SEQ_LEN, D)

def attend_head(head_items):
    query_head, key_head, value_head, split_point = head_items
    positions = jnp.arange(SEQ_LEN).astype(jnp.int32)
    first_part = positions < split_point
    allowed = first_part[:, None] == first_part[None, :]
    score = low_back(jnp.einsum('qe,ke->qk', query_head, key_head, precision=lax.Precision.HIGHEST) * HEAD_DIM ** (-0.5))
    score = jnp.where(allowed, score, -1e+30)
    log_total = jax.nn.logsumexp(score, axis=-1, keepdims=True)
    prob = low(jnp.exp(score - log_total))
    return jnp.einsum('qk,ke->qe', prob, value_head, precision=lax.Precision.HIGHEST)

def layer_forward(group_tokens, rank_params, out_params, group_splits, weights):
    attn_in, out_proj, ffn_in, ffn_out, vera_down, vera_up, gain_rows, shift_rows, ffn_shift = weights
    token_rows = group_tokens.reshape(-1, D)
    rank_in = low_back(dot_high(token_rows, vera_down))
    wide_q = low_back(dot_high(low(rank_in * rank_params[0]), vera_up))
    wide_v = low_back(dot_high(low(rank_in * rank_params[1]), vera_up))
    projected = dot_high(token_rows, attn_in)
    query = low(low_back(projected[:, :D] + shift_rows[0] + out_params[0] * wide_q))
    keys = low(low_back(projected[:, D:2 * D]))
    values = low(low_back(projected[:, 2 * D:] + shift_rows[1] + out_params[1] * wide_v))
    head_splits = jnp.repeat(group_splits, HEADS)
    attended = lax.map(jax.checkpoint(attend_head), (heads_first(query), heads_first(keys), heads_first(values), head_splits))
    attended = low(low_back(heads_back(attended)))
    branch = low_back(dot_high(attended, out_proj) + shift_rows[2])
    hidden = layer_norm(token_rows + branch, gain_rows[0], shift_rows[4])
    inner = low_back(dot_high(low(hidden), ffn_in) + ffn_shift)
    activated = low(jax.nn.gelu(inner, approximate=False))
    ffn_branch = low_back(dot_high(activated, ffn_out) + shift_rows[3])
    return layer_norm(hidden + ffn_branch, gain_rows[1], shift_rows[5]).reshape(group_tokens.shape)

def reference(tokens, attn_in_weight, out_weight, ffn_in_weight, ffn_out_weight, vera_in, vera_out, rank_scale, out_scale, gains, shifts, ffn_bias, splits, out_grad):
    weights = tuple((item.astype(jnp.float32) for item in (attn_in_weight, out_weight, ffn_in_weight, ffn_out_weight, vera_in, vera_out, gains, shifts, ffn_bias)))
    group_count = BATCH_SEQS // SEQS
    token_groups = tokens.astype(jnp.float32).reshape(group_count, SEQS, SEQ_LEN, D)
    grad_groups = out_grad.astype(jnp.float32).reshape(group_count, SEQS, SEQ_LEN, D)
    split_groups = splits.reshape(group_count, SEQS)
    rank_params = rank_scale.astype(jnp.float32)
    out_params = out_scale.astype(jnp.float32)

    def one_group(totals, group_items):
        group_tokens, group_grad, group_splits = group_items

        def forward(inputs, rank_values, out_values):
            return layer_forward(inputs, rank_values, out_values, group_splits, weights)
        group_out, pullback = jax.vjp(forward, group_tokens, rank_params, out_params)
        grad_tokens, grad_rank, grad_out = pullback(group_grad)
        return ((totals[0] + grad_rank, totals[1] + grad_out), (group_out.astype(jnp.bfloat16), grad_tokens.astype(jnp.bfloat16)))
    initial = (jnp.zeros((2, RANK), jnp.float32), jnp.zeros((2, D), jnp.float32))
    (rank_total, out_total), (layer_outs, input_grads) = lax.scan(one_group, initial, (token_groups, grad_groups, split_groups))
    scale_norms = jnp.concatenate([jnp.sqrt(lax.optimization_barrier(jnp.sum(rank_total * rank_total, axis=1))), jnp.sqrt(lax.optimization_barrier(jnp.sum(out_total * out_total, axis=1)))])
    return (layer_outs.reshape(BATCH_SEQS, SEQ_LEN, D), input_grads.reshape(BATCH_SEQS, SEQ_LEN, D), rank_total, out_total, scale_norms)
```

```python
import functools

import jax
import jax.numpy as jnp
from jax import lax
from jax.experimental import pallas as pl
from jax.experimental.pallas import tpu as pltpu
from jax.sharding import PartitionSpec as P

HEADS = 12


masked_score = -1e30
key_block = 512


def product(left_side, right_side):
    return jnp.dot(left_side, right_side, preferred_element_type=jnp.float32)


def product_t(left_side, right_side):
    return lax.dot_general(
        left_side, right_side, (((1,), (1,)), ((), ())), preferred_element_type=jnp.float32
    )


def gelu_exact(inputs):
    return jax.nn.gelu(inputs, approximate=False)


def norm_forward(values_in, gain_row, shift_row):
    centered = values_in - jnp.mean(values_in, axis=-1, keepdims=True)
    inverse = lax.rsqrt(jnp.mean(centered * centered, axis=-1, keepdims=True) + 1e-05)
    normed = centered * inverse
    return (normed * gain_row + shift_row, normed, inverse)


def norm_backward(grad_in, normed, inverse, gain_row):
    scaled = grad_in * gain_row
    return inverse * (
        scaled
        - jnp.mean(scaled, axis=-1, keepdims=True)
        - normed * jnp.mean(scaled * normed, axis=-1, keepdims=True)
    )


def block_width():
    return key_block


def body(
    tokens,
    attn_in_weight,
    out_weight,
    ffn_in_weight,
    ffn_out_weight,
    vera_in,
    vera_out,
    rank_scale,
    out_scale,
    gains,
    shifts,
    ffn_bias,
    splits,
    out_grad,
):
    sequences, per_device, model_width = tokens.shape
    head_dim = model_width // HEADS
    score_scale = head_dim ** (-0.5)
    cycle_place = lax.axis_index("seq")
    token_rows = tokens.reshape(-1, model_width)
    token_float = token_rows.astype(jnp.float32)
    rank_in = product(token_rows, vera_in)
    rank_q = (rank_in * rank_scale[0]).astype(jnp.bfloat16)
    rank_v = (rank_in * rank_scale[1]).astype(jnp.bfloat16)
    wide_q = product(rank_q, vera_out)
    wide_v = product(rank_v, vera_out)
    projected = product(token_rows, attn_in_weight)
    query = projected[:, :model_width] + shifts[0] + out_scale[0] * wide_q
    keys = projected[:, model_width : 2 * model_width]
    values = projected[:, 2 * model_width :] + shifts[1] + out_scale[1] * wide_v
    query_low = query.astype(jnp.bfloat16).reshape(sequences, per_device, HEADS, head_dim)
    pair_low = (
        jnp.concatenate([keys, values], axis=-1)
        .astype(jnp.bfloat16)
        .reshape(sequences, per_device, 2 * model_width)
    )
    query_pos = cycle_place * per_device + jnp.arange(per_device, dtype=jnp.int32)
    query_side = query_pos[None, :] < splits[:, None]

    def block_scores(pair_piece, block_start):
        count_keys = pair_piece.shape[1]
        key_pos = block_start + jnp.arange(count_keys, dtype=jnp.int32)
        key_side = key_pos[None, :] < splits[:, None]
        allowed = (query_side[:, :, None] == key_side[:, None, :])[:, None]
        key_heads = pair_piece[:, :, :model_width].reshape(sequences, count_keys, HEADS, head_dim)
        value_heads = pair_piece[:, :, model_width:].reshape(sequences, count_keys, HEADS, head_dim)
        raw_scores = (
            jnp.einsum("sqhe,skhe->shqk", query_low, key_heads, preferred_element_type=jnp.float32)
            * score_scale
        )
        return (raw_scores, allowed, key_heads, value_heads)

    start_max = jnp.full((sequences, HEADS, per_device), masked_score, jnp.float32)
    start_sum = jnp.zeros((sequences, HEADS, per_device), jnp.float32)
    start_acc = jnp.zeros((sequences, per_device, HEADS, head_dim), jnp.float32)
    carry = (start_max, start_sum, start_acc)
    pair_piece = lax.all_gather(pair_low, "seq", axis=1, tiled=True)
    shard_start = jnp.int32(0)
    count_keys = pair_piece.shape[1]
    block_size = block_width()
    for absorb_block_index in range(count_keys // block_size):
        absorb_pair_piece = pair_piece[
            :, absorb_block_index * block_size : (absorb_block_index + 1) * block_size
        ]
        running_max, running_sum, absorb_accumulated = carry
        absorb_raw_scores, absorb_allowed, absorb_key_heads, absorb_value_heads = block_scores(
            absorb_pair_piece, shard_start + absorb_block_index * block_size
        )
        new_max = jnp.maximum(
            running_max,
            jnp.max(jnp.where(absorb_allowed, absorb_raw_scores, masked_score), axis=-1),
        )
        block_weights = jnp.where(
            absorb_allowed, jnp.exp(absorb_raw_scores - new_max[..., None]), 0.0
        )
        rescale = jnp.exp(running_max - new_max)
        running_sum = running_sum * rescale + jnp.sum(block_weights, axis=-1)
        added = jnp.einsum(
            "shqk,skhe->sqhe",
            block_weights.astype(jnp.bfloat16),
            absorb_value_heads,
            preferred_element_type=jnp.float32,
        )
        absorb_accumulated = (
            absorb_accumulated * jnp.transpose(rescale, (0, 2, 1))[..., None] + added
        )
        carry = (new_max, running_sum, absorb_accumulated)
    final_max, final_sum, accumulated = carry
    attended = accumulated / jnp.transpose(final_sum, (0, 2, 1))[..., None]
    log_total = final_max + jnp.log(final_sum)
    branch = product(attended.reshape(-1, model_width).astype(jnp.bfloat16), out_weight) + shifts[2]
    hidden, normed_one, inverse_one = norm_forward(token_float + branch, gains[0], shifts[4])
    inner = product(hidden.astype(jnp.bfloat16), ffn_in_weight) + ffn_bias
    activated, gelu_pull = jax.vjp(gelu_exact, inner)
    ffn_branch = product(activated.astype(jnp.bfloat16), ffn_out_weight) + shifts[3]
    layer_out, normed_two, inverse_two = norm_forward(hidden + ffn_branch, gains[1], shifts[5])
    grad_two = norm_backward(
        out_grad.reshape(-1, model_width).astype(jnp.float32), normed_two, inverse_two, gains[1]
    )
    grad_act = product_t(grad_two.astype(jnp.bfloat16), ffn_out_weight)
    grad_inner = gelu_pull(grad_act)[0].astype(jnp.bfloat16)
    grad_hidden = grad_two + product_t(grad_inner, ffn_in_weight)
    grad_one = norm_backward(grad_hidden, normed_one, inverse_one, gains[0])
    grad_att = (
        product_t(grad_one.astype(jnp.bfloat16), out_weight)
        .astype(jnp.bfloat16)
        .reshape(sequences, per_device, HEADS, head_dim)
    )
    delta = jnp.transpose(jnp.sum(grad_att.astype(jnp.float32) * attended, axis=-1), (0, 2, 1))
    grad_query = jnp.zeros((sequences, per_device, HEADS, head_dim), jnp.float32)
    whole_pairs = lax.all_gather(pair_low, "seq", axis=1, tiled=True)
    whole_len = whole_pairs.shape[1]
    block_size = block_width()
    key_terms = []
    for block_index in range(whole_len // block_size):
        block_pair_piece = whole_pairs[:, block_index * block_size : (block_index + 1) * block_size]
        block_raw_scores, block_allowed, block_key_heads, block_value_heads = block_scores(
            block_pair_piece, block_index * block_size
        )
        prob = jnp.where(block_allowed, jnp.exp(block_raw_scores - log_total[..., None]), 0.0)
        grad_prob = jnp.einsum(
            "sqhe,skhe->shqk", grad_att, block_value_heads, preferred_element_type=jnp.float32
        )
        grad_score = (prob * (grad_prob - delta[..., None])).astype(jnp.bfloat16)
        grad_value = jnp.einsum(
            "shqk,sqhe->skhe",
            prob.astype(jnp.bfloat16),
            grad_att,
            preferred_element_type=jnp.float32,
        )
        grad_key = (
            jnp.einsum("shqk,sqhe->skhe", grad_score, query_low, preferred_element_type=jnp.float32)
            * score_scale
        )
        query_part = (
            jnp.einsum(
                "shqk,skhe->sqhe", grad_score, block_key_heads, preferred_element_type=jnp.float32
            )
            * score_scale
        )
        block_count_keys = block_pair_piece.shape[1]
        pair_part = jnp.concatenate(
            [
                grad_key.reshape(sequences, block_count_keys, model_width),
                grad_value.reshape(sequences, block_count_keys, model_width),
            ],
            axis=-1,
        )
        query_part, pair_part = (query_part, pair_part)
        grad_query = grad_query + query_part
        key_terms.append(pair_part)
    pair_sum = lax.psum_scatter(
        jnp.concatenate(key_terms, axis=1), "seq", scatter_dimension=1, tiled=True
    )
    pair_grad_low = pair_sum.astype(jnp.bfloat16).reshape(-1, 2 * model_width)
    query_grad_low = grad_query.reshape(-1, model_width).astype(jnp.bfloat16)
    query_grad_float = query_grad_low.astype(jnp.float32)
    value_grad_float = pair_grad_low[:, model_width:].astype(jnp.float32)
    grad_wide_q = (query_grad_float * out_scale[0]).astype(jnp.bfloat16)
    grad_wide_v = (value_grad_float * out_scale[1]).astype(jnp.bfloat16)
    grad_rank_q = product_t(grad_wide_q, vera_out)
    grad_rank_v = product_t(grad_wide_v, vera_out)
    grad_rank_in = (grad_rank_q * rank_scale[0] + grad_rank_v * rank_scale[1]).astype(jnp.bfloat16)
    grad_tokens = (
        grad_one
        + product_t(jnp.concatenate([query_grad_low, pair_grad_low], axis=-1), attn_in_weight)
        + product_t(grad_rank_in, vera_in)
    )
    rank_terms = jnp.stack(
        [jnp.sum(grad_rank_q * rank_in, axis=0), jnp.sum(grad_rank_v * rank_in, axis=0)]
    )
    out_terms = jnp.stack(
        [jnp.sum(query_grad_float * wide_q, axis=0), jnp.sum(value_grad_float * wide_v, axis=0)]
    )
    rank_total, out_total = lax.psum((rank_terms, out_terms), ("batch", "seq"))
    scale_norms = jnp.concatenate(
        [
            jnp.sqrt(jnp.sum(rank_total * rank_total, axis=1)),
            jnp.sqrt(jnp.sum(out_total * out_total, axis=1)),
        ]
    )
    return (
        layer_out.astype(jnp.bfloat16).reshape(sequences, per_device, model_width),
        grad_tokens.astype(jnp.bfloat16).reshape(sequences, per_device, model_width),
        rank_total,
        out_total,
        scale_norms,
    )


MESH = pl.DeviceIdType.MESH
BIG = 1e30
F32 = jnp.float32
BF16 = jnp.bfloat16


def fits(mesh):
    return mesh.shape["seq"] == 8 and mesh.shape["batch"] == 4


def dot(left, right):
    return lax.dot_general(left, right, (((1,), (0,)), ((), ())), preferred_element_type=F32)


def dot_nt(left, right):
    return lax.dot_general(left, right, (((1,), (1,)), ((), ())), preferred_element_type=F32)


OWN, FAR, SIB, SIB_FAR, NEAR, NEAR_FAR, SIB_NEAR, SIB_NEAR_FAR = range(8)


def layer_kernel(
    n_batch,
    tokens,
    attn_in,
    out_w,
    ffn_in,
    ffn_out,
    vera_in,
    vera_out,
    out_grad,
    rank_scale,
    out_scale,
    gains,
    shifts,
    ffn_bias,
    splits,
    layer_out,
    in_grad,
    rank_total,
    out_total,
    tok,
    og,
    w_all,
    w_out,
    w_one,
    w_two,
    v_in,
    v_out,
    v_out_t,
    k_ext,
    q_ext,
    val,
    k_t,
    v_t,
    probs,
    s_buf,
    att_t,
    inv_l,
    att_send,
    att_recv,
    hid,
    n_one,
    acc,
    gprime,
    low_rows,
    g_two,
    g_one,
    lo_buf,
    ga_send,
    ga_recv,
    ga_mine,
    go_t,
    go_m,
    delta,
    d_kv,
    dq_t,
    ta_send,
    ta_recv,
    ta_mine,
    tn_send,
    tn_recv,
    tb_send,
    tb_recv,
    ig_buf,
    sum_buf,
    sum_recv,
    send_sem,
    recv_sem,
    load_sem,
):
    s = lax.axis_index("seq")
    b = lax.axis_index("batch")
    core = s % 2
    group = s // 4
    sib = s + 1 - 2 * core
    near = s + 2 - 4 * ((s // 2) % 2)
    far = s + 4 - 8 * group
    bx = b + 1 - 2 * (b % 2)
    by = b + 2 - 4 * (b // 2)
    half = pl.multiple_of(core * 384, 384)
    other_half = pl.multiple_of(384 - core * 384, 384)

    def remote(k, src, dst, where):
        return pltpu.make_async_remote_copy(
            src_ref=src,
            dst_ref=dst,
            send_sem=send_sem.at[k],
            recv_sem=recv_sem.at[k],
            device_id=where,
            device_id_type=MESH,
        )

    def local(k, src, dst):
        return pltpu.make_async_copy(src, dst, load_sem.at[k])

    def block(ref, k, n=1):
        return ref.at[pl.ds(128 * k, 128 * n)]

    to_sib, to_near, to_far = {"seq": sib}, {"seq": near}, {"seq": far}

    loads = [
        local(0, tokens.at[group], block(tok, OWN)),
        local(1, vera_in, v_in),
        local(2, vera_out.at[:, pl.ds(half, 384)], v_out),
        local(3, attn_in.at[:, pl.ds(half, 384)], w_all.at[:, pl.ds(0, 384)]),
        local(4, attn_in.at[:, pl.ds(768 + half, 384)], w_all.at[:, pl.ds(384, 384)]),
        local(5, attn_in.at[:, pl.ds(1536 + half, 384)], w_all.at[:, pl.ds(768, 384)]),
        local(6, out_w, w_out),
        local(7, ffn_in, w_one),
        local(8, ffn_out, w_two),
        local(9, out_grad.at[group], block(og, OWN)),
    ]
    for item in loads:
        item.start()

    barrier = pltpu.get_barrier_semaphore()
    for where in (to_sib, to_near, to_far, {"batch": bx}, {"batch": by}):
        pl.semaphore_signal(barrier, inc=1, device_id=where, device_id_type=MESH)
    pl.semaphore_wait(barrier, 5)

    send_far = remote(0, tokens.at[1 - group], block(tok, FAR), to_far)
    send_near = remote(1, tokens.at[group], block(tok, NEAR), to_near)
    send_sib = remote(2, tokens.at[group], block(tok, SIB), to_sib)
    pass_far_sib = remote(3, block(tok, FAR), block(tok, SIB_FAR), to_sib)
    pass_far_near = remote(4, block(tok, FAR), block(tok, NEAR_FAR), to_near)
    pass_near_sib = remote(5, block(tok, NEAR), block(tok, SIB_NEAR), to_sib)
    pass_last = remote(6, block(tok, NEAR_FAR), block(tok, SIB_NEAR_FAR), to_sib)
    send_og = remote(7, out_grad.at[1 - group], block(og, FAR), to_far)
    send_far.start()
    send_near.start()
    send_sib.start()

    for k in range(1, 6):
        loads[k].wait()
    for row, at in ((0, 0), (1, 768)):
        scale_row = rank_scale[pl.ds(row, 1), :]
        out_row = out_scale[pl.ds(row, 1), pl.ds(half, 384)]

        def effective(t, _, at=at, scale_row=scale_row, out_row=out_row):
            rows = pl.ds(pl.multiple_of(t * 256, 256), 256)
            scaled = (v_in[rows, :].astype(F32) * scale_row).astype(BF16)
            wide = dot(scaled, v_out[...]) * out_row
            w_all[rows, at : at + 384] = (w_all[rows, at : at + 384].astype(F32) + wide).astype(BF16)
            return 0

        lax.fori_loop(0, 3, effective, 0)
    v_out_t[...] = v_out[...].astype(F32).T.astype(BF16)

    split = splits[group]
    lane = lax.broadcasted_iota(jnp.int32, (128, 128), 1)
    row_at = lax.broadcasted_iota(jnp.int32, (128, 128), 0)
    flip_one, flip_two, flip_four = sib - s, near - s, far - s
    starts = [
        s,
        s + flip_four,
        s + flip_one,
        s + flip_four + flip_one,
        s + flip_two,
        s + flip_two + flip_four,
        s + flip_two + flip_one,
        s + flip_two + flip_four + flip_one,
    ]
    for k in range(8):
        first = (starts[k] * 128 + row_at < split).astype(F32)
        second = 1.0 - first
        key_side = jnp.where(lane == 0, first, jnp.where(lane == 1, second, 0.0)).astype(BF16)
        for p in range(3):
            k_ext[p, 128 * k : 128 * k + 128, 128:256] = key_side
        if k < 4:
            query_side = (
                jnp.where(lane == 0, second, jnp.where(lane == 1, first, 0.0)) * (-BIG)
            ).astype(BF16)
            for h in range(6):
                q_ext[h, 128 * k : 128 * k + 128, 128:256] = query_side

    shift_q = shifts[0:1, pl.ds(half, 384)]
    shift_v = shifts[1:2, pl.ds(half, 384)]
    low_lane = lax.broadcasted_iota(jnp.int32, (256, 128), 1) < 64

    def project(one, two, queries):
        rows = jnp.concatenate(
            [tok[128 * one : 128 * one + 128, :], tok[128 * two : 128 * two + 128, :]], axis=0
        )
        keys = dot(rows, w_all[:, 384:768])
        values = dot(rows, w_all[:, 768:1152]) + shift_v
        low_keys = keys.astype(BF16)
        low_values = values.astype(BF16)
        keys_t = keys.T.astype(BF16)
        values_t = values.T.astype(BF16)
        for n, k in ((0, one), (1, two)):
            part = slice(128 * n, 128 * n + 128)
            to = slice(128 * k, 128 * k + 128)
            for p in range(3):
                k_ext[p, to, 0:128] = low_keys[part, 128 * p : 128 * p + 128]
                val[p, to, :] = low_values[part, 128 * p : 128 * p + 128]
            k_t[:, to] = keys_t[:, part]
            v_t[:, to] = values_t[:, part]
        if queries:
            query = dot(rows, w_all[:, 0:384]) + shift_q
            low_query = query.astype(BF16).astype(F32) * 0.125
            for h in range(6):
                p = h // 2
                mine = low_lane if h % 2 == 0 else jnp.logical_not(low_lane)
                masked = jnp.where(mine, low_query[:, 128 * p : 128 * p + 128], 0.0).astype(BF16)
                for n, k in ((0, one), (1, two)):
                    q_ext[h, 128 * k : 128 * k + 128, 0:128] = masked[128 * n : 128 * n + 128]

    loads[0].wait()
    send_sib.wait_recv()
    project(OWN, SIB, True)
    send_near.wait_recv()
    pass_near_sib.start()
    send_far.wait_recv()
    pass_far_near.start()
    pass_far_sib.start()
    pass_near_sib.wait_recv()
    project(NEAR, SIB_NEAR, False)
    pass_far_sib.wait_recv()
    project(FAR, SIB_FAR, True)
    pass_far_near.wait_recv()
    pass_last.start()
    send_og.start()
    pass_last.wait_recv()
    project(NEAR_FAR, SIB_NEAR_FAR, False)

    def forward_head(h, _):
        p = h // 2
        rows_h = pl.ds(pl.multiple_of(h * 64, 64), 64)
        top = None
        for k in range(4):
            part = dot_nt(k_ext[p, 256 * k : 256 * k + 256, :], q_ext[h])
            s_buf[256 * k : 256 * k + 256, :] = part
            peak = jnp.max(part, axis=0, keepdims=True)
            top = peak if top is None else jnp.maximum(top, peak)
        total = jnp.zeros((1, 512), F32)
        out = jnp.zeros((64, 512), F32)
        for k in range(4):
            weight = jnp.exp(s_buf[256 * k : 256 * k + 256, :] - top)
            total = total + jnp.sum(weight, axis=0, keepdims=True)
            low_weight = weight.astype(BF16)
            probs[h, 256 * k : 256 * k + 256, :] = low_weight
            out = out + dot(v_t[rows_h, 256 * k : 256 * k + 256], low_weight)
        inverse = 1.0 / total
        inv_l[h] = inverse
        att_t[rows_h, :] = out * inverse
        return 0

    lax.fori_loop(0, 6, forward_head, 0)

    swap_att = remote(8, att_send, att_recv, to_sib)
    att_send[...] = att_t[:, 256:512].T.astype(BF16)
    swap_att.start()

    def norm(values_in):
        centered = values_in - jnp.mean(values_in, axis=-1, keepdims=True)
        inverse = lax.rsqrt(jnp.mean(centered * centered, axis=-1, keepdims=True) + 1e-05)
        return centered * inverse, inverse

    def norm_back(grad_in, normed, inverse, gain_row):
        scaled = grad_in * gain_row
        return inverse * (
            scaled
            - jnp.mean(scaled, axis=-1, keepdims=True)
            - normed * jnp.mean(scaled * normed, axis=-1, keepdims=True)
        )

    loads[6].wait()
    branch = dot(att_t[:, 0:256].T.astype(BF16), w_out[pl.ds(half, 384), :])
    swap_att.wait_recv()
    branch = branch + dot(att_recv[...], w_out[pl.ds(other_half, 384), :]) + shifts[2:3, :]
    normed_one, inverse_one = norm(tok[0:256, :].astype(F32) + branch)
    n_one[...] = normed_one
    hidden = normed_one * gains[0:1, :] + shifts[4:5, :]
    hid[...] = hidden
    low_rows[...] = hidden.astype(BF16)

    loads[7].wait()
    loads[8].wait()
    acc[...] = jnp.zeros_like(acc)

    def ffn_forward(t, _):
        cols = pl.ds(pl.multiple_of(t * 512, 512), 512)
        inner = dot(low_rows[...], w_one[:, cols]) + ffn_bias[:, cols]
        phi = 0.5 * (1.0 + lax.erf(inner * 0.7071067811865476))
        density = 0.3989422804014327 * jnp.exp(-0.5 * inner * inner)
        gprime[:, cols] = phi + inner * density
        acc[...] += dot((inner * phi).astype(BF16), w_two[cols, :])
        return 0

    lax.fori_loop(0, 6, ffn_forward, 0)
    normed_two, inverse_two = norm(hid[...] + acc[...] + shifts[3:4, :])
    lo_buf[...] = (normed_two * gains[1:2, :] + shifts[5:6, :]).astype(BF16)
    send_lo = remote(10, block(lo_buf, FAR), layer_out.at[group], to_far)
    keep_lo = local(10, block(lo_buf, OWN), layer_out.at[group])
    send_lo.start()
    keep_lo.start()
    loads[9].wait()
    send_og.wait_recv()
    grad_two = norm_back(og[...].astype(F32), normed_two, inverse_two, gains[1:2, :])
    g_two[...] = grad_two
    low_rows[...] = grad_two.astype(BF16)
    acc[...] = grad_two

    def ffn_backward(t, _):
        cols = pl.ds(pl.multiple_of(t * 512, 512), 512)
        grad_act = dot_nt(low_rows[...], w_two[cols, :])
        grad_inner = (grad_act * gprime[:, cols]).astype(BF16)
        acc[...] += dot_nt(grad_inner, w_one[:, cols])
        return 0

    lax.fori_loop(0, 6, ffn_backward, 0)
    grad_one = norm_back(acc[...], n_one[...], inverse_one, gains[0:1, :])
    g_one[...] = grad_one
    low_one = grad_one.astype(BF16)
    swap_ga = remote(9, ga_send, ga_recv, to_sib)
    ga_send[...] = dot_nt(low_one, w_out[pl.ds(other_half, 384), :]).astype(BF16)
    swap_ga.start()
    ga_mine[...] = dot_nt(low_one, w_out[pl.ds(half, 384), :]).astype(BF16)
    swap_ga.wait_recv()

    go_full = jnp.concatenate([ga_mine[...], ga_recv[...]], axis=0).astype(F32).T
    top_rows = lax.broadcasted_iota(jnp.int32, (128, 512), 0) < 64
    for p in range(3):
        pair = go_full[128 * p : 128 * p + 128, :]
        attended = att_t[128 * p : 128 * p + 128, :]
        for e in range(2):
            h = 2 * p + e
            mine = top_rows if e == 0 else jnp.logical_not(top_rows)
            scaled = jnp.where(mine, pair * inv_l[h], 0.0)
            low_scaled = scaled.astype(BF16)
            rounded = low_scaled.astype(F32)
            go_t[h] = low_scaled
            go_m[h] = rounded.T.astype(BF16)
            delta[h] = jnp.sum(rounded * attended, axis=0, keepdims=True)

    def backward_pair(p, start, first):
        rows = slice(start, start + 512)
        grad_keys = None
        grad_values = None
        for e in range(2):
            h = 2 * p + e
            rows_h = pl.ds(pl.multiple_of(h * 64, 64), 64)
            weight = probs[h, rows, :]
            grad_prob = dot(val[p, rows, :], go_t[h])
            grad_score = (weight.astype(F32) * (grad_prob - delta[h])).astype(BF16)
            value_part = dot(weight, go_m[h])
            key_part = dot(grad_score, q_ext[h, :, 0:128])
            query_part = dot(k_t[rows_h, rows], grad_score)
            grad_values = value_part if e == 0 else grad_values + value_part
            grad_keys = key_part if e == 0 else grad_keys + key_part
            if first:
                dq_t[rows_h, :] = query_part
            else:
                dq_t[rows_h, :] += query_part
        d_kv[rows, pl.ds(pl.multiple_of(p * 128, 128), 128)] = grad_keys.astype(BF16)
        d_kv[rows, pl.ds(pl.multiple_of(384 + p * 128, 128), 128)] = grad_values.astype(BF16)

    def near_pair(p, _):
        backward_pair(p, 512, True)
        return 0

    def own_pair(p, _):
        backward_pair(p, 0, False)
        return 0

    lax.fori_loop(0, 3, near_pair, 0)
    swap_ta = remote(11, ta_send, ta_recv, to_sib)
    ta_send[...] = dot_nt(d_kv[768:1024, :], w_all[:, 384:1152]).astype(BF16)
    swap_ta.start()
    ta_mine[...] = dot_nt(d_kv[512:768, :], w_all[:, 384:1152])
    lax.fori_loop(0, 1, own_pair, 0)
    swap_ta.wait_recv()
    tn_send[...] = (ta_mine[...] + ta_recv[...].astype(F32)).astype(BF16)
    send_tn_far = remote(12, tn_send.at[pl.ds(128, 128)], tn_recv.at[pl.ds(128, 128)], to_near)
    send_tn_own = remote(13, tn_send.at[pl.ds(0, 128)], tn_recv.at[pl.ds(0, 128)], to_near)
    send_tn_far.start()
    send_tn_own.start()
    lax.fori_loop(1, 3, own_pair, 0)

    low_dq_t = (dq_t[...] * 0.125).astype(BF16)
    low_dq = (dq_t[...] * 0.125).T.astype(BF16)
    swap_tb = remote(14, tb_send, tb_recv, to_sib)
    tb_send[...] = (
        dot_nt(d_kv[256:512, :], w_all[:, 384:1152]) + dot_nt(low_dq[256:512, :], w_all[:, 0:384])
    ).astype(BF16)
    swap_tb.start()
    mine = (
        g_one[...]
        + dot_nt(d_kv[0:256, :], w_all[:, 384:1152])
        + dot_nt(low_dq[0:256, :], w_all[:, 0:384])
    )
    swap_tb.wait_recv()
    send_tn_far.wait_recv()
    mine = mine + tb_recv[...].astype(F32)
    ig_buf[128:256, :] = (mine[128:256] + tn_recv[128:256, :].astype(F32)).astype(BF16)
    send_ig = remote(15, block(ig_buf, FAR), in_grad.at[group], to_far)
    keep_ig = local(11, block(ig_buf, OWN), in_grad.at[group])
    send_ig.start()
    send_tn_own.wait_recv()
    ig_buf[0:128, :] = (mine[0:128] + tn_recv[0:128, :].astype(F32)).astype(BF16)
    keep_ig.start()

    grad_q_map = dot(low_dq_t, tok[0:512, :]).astype(BF16)
    grad_v_map = dot(d_kv[:, 384:768].astype(F32).T.astype(BF16), tok[...]).astype(BF16)
    sum_buf[...] = jnp.zeros_like(sum_buf)
    for row, grad_map in ((0, grad_q_map), (1, grad_v_map)):
        product_map = dot(grad_map, v_in[...]) * v_out_t[...].astype(F32)
        out_row = out_scale[pl.ds(row, 1), pl.ds(half, 384)]
        out_col = jnp.broadcast_to(out_row, (128, 384)).T[:, 0:1]
        sum_buf[row : row + 1, :] = jnp.sum(product_map * out_col, axis=0, keepdims=True)
        out_part = jnp.sum(product_map * rank_scale[pl.ds(row, 1), :], axis=1, keepdims=True)
        out_part_row = jnp.broadcast_to(out_part, (384, 128)).T[0:1, :]
        sum_buf[2 + row : 3 + row, pl.ds(half, 384)] = out_part_row

    stages = (to_sib, to_near, to_far, {"batch": bx}, {"batch": by})
    for k, where in enumerate(stages):
        swap = remote(16 + k, sum_buf.at[pl.ds(8 * k, 8)], sum_recv.at[pl.ds(8 * k, 8)], where)
        swap.start()
        swap.wait_recv()
        sum_buf[8 * k + 8 : 8 * k + 16, :] = (
            sum_buf[8 * k : 8 * k + 8, :] + sum_recv[8 * k : 8 * k + 8, :]
        )
        swap.wait_send()
    rank_total[...] = sum_buf[40:42, :]
    out_total[...] = sum_buf[42:44, 0:768]

    send_lo.wait_recv()
    send_ig.wait_recv()
    keep_lo.wait()
    keep_ig.wait()
    for item in (
        send_far,
        send_near,
        send_sib,
        pass_far_sib,
        pass_far_near,
        pass_near_sib,
        pass_last,
        send_og,
        swap_att,
        swap_ga,
        send_lo,
        swap_ta,
        send_tn_far,
        send_tn_own,
        swap_tb,
        send_ig,
    ):
        item.wait_send()


def fast_body(
    tokens,
    attn_in_weight,
    out_weight,
    ffn_in_weight,
    ffn_out_weight,
    vera_in,
    vera_out,
    rank_scale,
    out_scale,
    gains,
    shifts,
    ffn_bias,
    splits,
    out_grad,
):
    hbm = pl.BlockSpec(memory_space=pl.ANY)
    vmem = pl.BlockSpec(memory_space=pltpu.VMEM)
    smem = pl.BlockSpec(memory_space=pltpu.SMEM)
    shape = tokens.shape
    scratch = [
        ((1024, 768), BF16),
        ((256, 768), BF16),
        ((768, 1152), BF16),
        ((768, 768), BF16),
        ((768, 3072), BF16),
        ((3072, 768), BF16),
        ((768, 1024), BF16),
        ((1024, 384), BF16),
        ((384, 1024), BF16),
        ((3, 1024, 256), BF16),
        ((6, 512, 256), BF16),
        ((3, 1024, 128), BF16),
        ((384, 1024), BF16),
        ((384, 1024), BF16),
        ((6, 1024, 512), BF16),
        ((1024, 512), F32),
        ((384, 512), F32),
        ((6, 1, 512), F32),
        ((256, 384), BF16),
        ((256, 384), BF16),
        ((256, 768), F32),
        ((256, 768), F32),
        ((256, 768), F32),
        ((256, 3072), F32),
        ((256, 768), BF16),
        ((256, 768), F32),
        ((256, 768), F32),
        ((256, 768), BF16),
        ((256, 384), BF16),
        ((256, 384), BF16),
        ((256, 384), BF16),
        ((6, 128, 512), BF16),
        ((6, 512, 128), BF16),
        ((6, 1, 512), F32),
        ((1024, 768), BF16),
        ((384, 512), F32),
        ((256, 768), BF16),
        ((256, 768), BF16),
        ((256, 768), F32),
        ((256, 768), BF16),
        ((256, 768), BF16),
        ((256, 768), BF16),
        ((256, 768), BF16),
        ((256, 768), BF16),
        ((48, 1024), F32),
        ((40, 1024), F32),
    ]
    layer_out, in_grad, rank_total, out_total = pl.pallas_call(
        functools.partial(layer_kernel, 4),
        out_shape=(
            jax.ShapeDtypeStruct(shape, BF16),
            jax.ShapeDtypeStruct(shape, BF16),
            jax.ShapeDtypeStruct(rank_scale.shape, F32),
            jax.ShapeDtypeStruct(out_scale.shape, F32),
        ),
        in_specs=[hbm] * 8 + [vmem] * 5 + [smem],
        out_specs=(hbm, hbm, vmem, vmem),
        scratch_shapes=[pltpu.VMEM(dims, kind) for dims, kind in scratch]
        + [
            pltpu.SemaphoreType.DMA((21,)),
            pltpu.SemaphoreType.DMA((21,)),
            pltpu.SemaphoreType.DMA((12,)),
        ],
        compiler_params=pltpu.CompilerParams(
            collective_id=0, has_side_effects=True, vmem_limit_bytes=60 * 2**20
        ),
        name="encoder_layer",
    )(
        tokens,
        attn_in_weight,
        out_weight,
        ffn_in_weight,
        ffn_out_weight,
        vera_in,
        vera_out,
        out_grad,
        rank_scale,
        out_scale,
        gains,
        shifts,
        ffn_bias.reshape(1, -1),
        splits,
    )
    scale_norms = jnp.concatenate(
        [
            jnp.sqrt(jnp.sum(rank_total * rank_total, axis=1)),
            jnp.sqrt(jnp.sum(out_total * out_total, axis=1)),
        ]
    )
    return layer_out, in_grad, rank_total, out_total, scale_norms


def solution(mesh):
    chosen = fast_body if fits(mesh) else body
    in_specs = (
        P("batch", "seq", None),
        P(),
        P(),
        P(),
        P(),
        P(),
        P(),
        P(),
        P(),
        P(),
        P(),
        P(),
        P("batch"),
        P("batch", "seq", None),
    )
    out_specs = (P("batch", "seq", None), P("batch", "seq", None), P(), P(), P())
    return jax.shard_map(chosen, mesh=mesh, in_specs=in_specs, out_specs=out_specs, check_vma=False)
```

```python
import functools

import jax
import jax.numpy as jnp
from jax import lax
from jax.experimental import pallas as pl
from jax.experimental.pallas import tpu as pltpu
from jax.sharding import PartitionSpec as P

HEADS = 12


masked_score = -1e30
key_block = 512


def product(left_side, right_side):
    return jnp.dot(left_side, right_side, preferred_element_type=jnp.float32)


def product_t(left_side, right_side):
    return lax.dot_general(
        left_side, right_side, (((1,), (1,)), ((), ())), preferred_element_type=jnp.float32
    )


def gelu_exact(inputs):
    return jax.nn.gelu(inputs, approximate=False)


def norm_forward(values_in, gain_row, shift_row):
    centered = values_in - jnp.mean(values_in, axis=-1, keepdims=True)
    inverse = lax.rsqrt(jnp.mean(centered * centered, axis=-1, keepdims=True) + 1e-05)
    normed = centered * inverse
    return (normed * gain_row + shift_row, normed, inverse)


def norm_backward(grad_in, normed, inverse, gain_row):
    scaled = grad_in * gain_row
    return inverse * (
        scaled
        - jnp.mean(scaled, axis=-1, keepdims=True)
        - normed * jnp.mean(scaled * normed, axis=-1, keepdims=True)
    )


def block_width():
    return key_block


def body(
    tokens,
    attn_in_weight,
    out_weight,
    ffn_in_weight,
    ffn_out_weight,
    vera_in,
    vera_out,
    rank_scale,
    out_scale,
    gains,
    shifts,
    ffn_bias,
    splits,
    out_grad,
):
    sequences, per_device, model_width = tokens.shape
    head_dim = model_width // HEADS
    score_scale = head_dim ** (-0.5)
    cycle_place = lax.axis_index("seq")
    token_rows = tokens.reshape(-1, model_width)
    token_float = token_rows.astype(jnp.float32)
    rank_in = product(token_rows, vera_in)
    rank_q = (rank_in * rank_scale[0]).astype(jnp.bfloat16)
    rank_v = (rank_in * rank_scale[1]).astype(jnp.bfloat16)
    wide_q = product(rank_q, vera_out)
    wide_v = product(rank_v, vera_out)
    projected = product(token_rows, attn_in_weight)
    query = projected[:, :model_width] + shifts[0] + out_scale[0] * wide_q
    keys = projected[:, model_width : 2 * model_width]
    values = projected[:, 2 * model_width :] + shifts[1] + out_scale[1] * wide_v
    query_low = query.astype(jnp.bfloat16).reshape(sequences, per_device, HEADS, head_dim)
    pair_low = (
        jnp.concatenate([keys, values], axis=-1)
        .astype(jnp.bfloat16)
        .reshape(sequences, per_device, 2 * model_width)
    )
    query_pos = cycle_place * per_device + jnp.arange(per_device, dtype=jnp.int32)
    query_side = query_pos[None, :] < splits[:, None]

    def block_scores(pair_piece, block_start):
        count_keys = pair_piece.shape[1]
        key_pos = block_start + jnp.arange(count_keys, dtype=jnp.int32)
        key_side = key_pos[None, :] < splits[:, None]
        allowed = (query_side[:, :, None] == key_side[:, None, :])[:, None]
        key_heads = pair_piece[:, :, :model_width].reshape(sequences, count_keys, HEADS, head_dim)
        value_heads = pair_piece[:, :, model_width:].reshape(sequences, count_keys, HEADS, head_dim)
        raw_scores = (
            jnp.einsum("sqhe,skhe->shqk", query_low, key_heads, preferred_element_type=jnp.float32)
            * score_scale
        )
        return (raw_scores, allowed, key_heads, value_heads)

    start_max = jnp.full((sequences, HEADS, per_device), masked_score, jnp.float32)
    start_sum = jnp.zeros((sequences, HEADS, per_device), jnp.float32)
    start_acc = jnp.zeros((sequences, per_device, HEADS, head_dim), jnp.float32)
    carry = (start_max, start_sum, start_acc)
    pair_piece = lax.all_gather(pair_low, "seq", axis=1, tiled=True)
    shard_start = jnp.int32(0)
    count_keys = pair_piece.shape[1]
    block_size = block_width()
    for absorb_block_index in range(count_keys // block_size):
        absorb_pair_piece = pair_piece[
            :, absorb_block_index * block_size : (absorb_block_index + 1) * block_size
        ]
        running_max, running_sum, absorb_accumulated = carry
        absorb_raw_scores, absorb_allowed, absorb_key_heads, absorb_value_heads = block_scores(
            absorb_pair_piece, shard_start + absorb_block_index * block_size
        )
        new_max = jnp.maximum(
            running_max,
            jnp.max(jnp.where(absorb_allowed, absorb_raw_scores, masked_score), axis=-1),
        )
        block_weights = jnp.where(
            absorb_allowed, jnp.exp(absorb_raw_scores - new_max[..., None]), 0.0
        )
        rescale = jnp.exp(running_max - new_max)
        running_sum = running_sum * rescale + jnp.sum(block_weights, axis=-1)
        added = jnp.einsum(
            "shqk,skhe->sqhe",
            block_weights.astype(jnp.bfloat16),
            absorb_value_heads,
            preferred_element_type=jnp.float32,
        )
        absorb_accumulated = (
            absorb_accumulated * jnp.transpose(rescale, (0, 2, 1))[..., None] + added
        )
        carry = (new_max, running_sum, absorb_accumulated)
    final_max, final_sum, accumulated = carry
    attended = accumulated / jnp.transpose(final_sum, (0, 2, 1))[..., None]
    log_total = final_max + jnp.log(final_sum)
    branch = product(attended.reshape(-1, model_width).astype(jnp.bfloat16), out_weight) + shifts[2]
    hidden, normed_one, inverse_one = norm_forward(token_float + branch, gains[0], shifts[4])
    inner = product(hidden.astype(jnp.bfloat16), ffn_in_weight) + ffn_bias
    activated, gelu_pull = jax.vjp(gelu_exact, inner)
    ffn_branch = product(activated.astype(jnp.bfloat16), ffn_out_weight) + shifts[3]
    layer_out, normed_two, inverse_two = norm_forward(hidden + ffn_branch, gains[1], shifts[5])
    grad_two = norm_backward(
        out_grad.reshape(-1, model_width).astype(jnp.float32), normed_two, inverse_two, gains[1]
    )
    grad_act = product_t(grad_two.astype(jnp.bfloat16), ffn_out_weight)
    grad_inner = gelu_pull(grad_act)[0].astype(jnp.bfloat16)
    grad_hidden = grad_two + product_t(grad_inner, ffn_in_weight)
    grad_one = norm_backward(grad_hidden, normed_one, inverse_one, gains[0])
    grad_att = (
        product_t(grad_one.astype(jnp.bfloat16), out_weight)
        .astype(jnp.bfloat16)
        .reshape(sequences, per_device, HEADS, head_dim)
    )
    delta = jnp.transpose(jnp.sum(grad_att.astype(jnp.float32) * attended, axis=-1), (0, 2, 1))
    grad_query = jnp.zeros((sequences, per_device, HEADS, head_dim), jnp.float32)
    whole_pairs = lax.all_gather(pair_low, "seq", axis=1, tiled=True)
    whole_len = whole_pairs.shape[1]
    block_size = block_width()
    key_terms = []
    for block_index in range(whole_len // block_size):
        block_pair_piece = whole_pairs[:, block_index * block_size : (block_index + 1) * block_size]
        block_raw_scores, block_allowed, block_key_heads, block_value_heads = block_scores(
            block_pair_piece, block_index * block_size
        )
        prob = jnp.where(block_allowed, jnp.exp(block_raw_scores - log_total[..., None]), 0.0)
        grad_prob = jnp.einsum(
            "sqhe,skhe->shqk", grad_att, block_value_heads, preferred_element_type=jnp.float32
        )
        grad_score = (prob * (grad_prob - delta[..., None])).astype(jnp.bfloat16)
        grad_value = jnp.einsum(
            "shqk,sqhe->skhe",
            prob.astype(jnp.bfloat16),
            grad_att,
            preferred_element_type=jnp.float32,
        )
        grad_key = (
            jnp.einsum("shqk,sqhe->skhe", grad_score, query_low, preferred_element_type=jnp.float32)
            * score_scale
        )
        query_part = (
            jnp.einsum(
                "shqk,skhe->sqhe", grad_score, block_key_heads, preferred_element_type=jnp.float32
            )
            * score_scale
        )
        block_count_keys = block_pair_piece.shape[1]
        pair_part = jnp.concatenate(
            [
                grad_key.reshape(sequences, block_count_keys, model_width),
                grad_value.reshape(sequences, block_count_keys, model_width),
            ],
            axis=-1,
        )
        query_part, pair_part = (query_part, pair_part)
        grad_query = grad_query + query_part
        key_terms.append(pair_part)
    pair_sum = lax.psum_scatter(
        jnp.concatenate(key_terms, axis=1), "seq", scatter_dimension=1, tiled=True
    )
    pair_grad_low = pair_sum.astype(jnp.bfloat16).reshape(-1, 2 * model_width)
    query_grad_low = grad_query.reshape(-1, model_width).astype(jnp.bfloat16)
    query_grad_float = query_grad_low.astype(jnp.float32)
    value_grad_float = pair_grad_low[:, model_width:].astype(jnp.float32)
    grad_wide_q = (query_grad_float * out_scale[0]).astype(jnp.bfloat16)
    grad_wide_v = (value_grad_float * out_scale[1]).astype(jnp.bfloat16)
    grad_rank_q = product_t(grad_wide_q, vera_out)
    grad_rank_v = product_t(grad_wide_v, vera_out)
    grad_rank_in = (grad_rank_q * rank_scale[0] + grad_rank_v * rank_scale[1]).astype(jnp.bfloat16)
    grad_tokens = (
        grad_one
        + product_t(jnp.concatenate([query_grad_low, pair_grad_low], axis=-1), attn_in_weight)
        + product_t(grad_rank_in, vera_in)
    )
    rank_terms = jnp.stack(
        [jnp.sum(grad_rank_q * rank_in, axis=0), jnp.sum(grad_rank_v * rank_in, axis=0)]
    )
    out_terms = jnp.stack(
        [jnp.sum(query_grad_float * wide_q, axis=0), jnp.sum(value_grad_float * wide_v, axis=0)]
    )
    rank_total, out_total = lax.psum((rank_terms, out_terms), ("batch", "seq"))
    scale_norms = jnp.concatenate(
        [
            jnp.sqrt(jnp.sum(rank_total * rank_total, axis=1)),
            jnp.sqrt(jnp.sum(out_total * out_total, axis=1)),
        ]
    )
    return (
        layer_out.astype(jnp.bfloat16).reshape(sequences, per_device, model_width),
        grad_tokens.astype(jnp.bfloat16).reshape(sequences, per_device, model_width),
        rank_total,
        out_total,
        scale_norms,
    )


MESH = pl.DeviceIdType.MESH
BIG = 1e30
F32 = jnp.float32
BF16 = jnp.bfloat16


def fits(mesh):
    return mesh.shape["seq"] == 8 and mesh.shape["batch"] == 4


def dot(left, right):
    return lax.dot_general(left, right, (((1,), (0,)), ((), ())), preferred_element_type=F32)


def dot_nt(left, right):
    return lax.dot_general(left, right, (((1,), (1,)), ((), ())), preferred_element_type=F32)


OWN, SIB, FAR, SIB_FAR, NEAR_FAR, SIB_NEAR_FAR, NEAR, SIB_NEAR = range(8)
PIECES = 4


def layer_kernel(
    tokens,
    attn_in,
    out_w,
    ffn_in,
    ffn_out,
    vera_in,
    vera_out,
    out_grad,
    rank_scale,
    out_scale,
    gains,
    shifts,
    ffn_bias,
    splits,
    layer_out,
    in_grad,
    sums,
    tok,
    og,
    w_all,
    w_out,
    w_one,
    w_two,
    v_in,
    v_out,
    v_out_t,
    k_ext,
    q_ext,
    val,
    k_t,
    v_t,
    probs,
    s_buf,
    att_t,
    inv_l,
    att_send,
    att_recv,
    hid,
    n_one,
    acc,
    gprime,
    low_rows,
    g_two,
    g_one,
    lo_buf,
    ga_send,
    ga_recv,
    ga_mine,
    go_t,
    go_m,
    delta,
    d_kv,
    dq_t,
    part_send,
    part_recv,
    part_mine,
    far_terms,
    tn_send,
    tn_recv,
    ig_buf,
    sum_buf,
    sum_recv,
    send_sem,
    recv_sem,
    load_sem,
):
    s = lax.axis_index("seq")
    b = lax.axis_index("batch")
    core = s % 2
    group = s // 4
    sib = s + 1 - 2 * core
    near = s + 2 - 4 * ((s // 2) % 2)
    far = s + 4 - 8 * group
    bx = b + 1 - 2 * (b % 2)
    by = b + 2 - 4 * (b // 2)
    half = pl.multiple_of(core * 384, 384)
    other_half = pl.multiple_of(384 - core * 384, 384)

    def remote(k, src, dst, where):
        return pltpu.make_async_remote_copy(
            src_ref=src,
            dst_ref=dst,
            send_sem=send_sem.at[k],
            recv_sem=recv_sem.at[k],
            device_id=where,
            device_id_type=MESH,
        )

    def local(k, src, dst):
        return pltpu.make_async_copy(src, dst, load_sem.at[k])

    def block(ref, k, n=1):
        return ref.at[pl.ds(128 * k, 128 * n)]

    near_far = far + near - s
    to_sib, to_near, to_far = {"seq": sib}, {"seq": near}, {"seq": far}
    to_near_far = {"seq": near_far}
    to_bx, to_by, to_bxy = {"batch": bx}, {"batch": by}, {"batch": bx + by - b}

    loads = [
        local(0, tokens.at[group], block(tok, OWN)),
        local(1, vera_in, v_in),
        local(2, vera_out.at[:, pl.ds(half, 384)], v_out),
        local(3, attn_in.at[:, pl.ds(half, 384)], w_all.at[:, pl.ds(0, 384)]),
        local(4, attn_in.at[:, pl.ds(768 + half, 384)], w_all.at[:, pl.ds(384, 384)]),
        local(5, attn_in.at[:, pl.ds(1536 + half, 384)], w_all.at[:, pl.ds(768, 384)]),
        local(6, out_w, w_out),
        local(7, ffn_in, w_one),
        local(8, ffn_out, w_two),
        local(9, out_grad.at[group], og.at[pl.ds(0, 128)]),
    ]
    for item in loads:
        item.start()

    barrier = pltpu.get_barrier_semaphore()
    for where in (to_sib, to_near, to_far, to_near_far, to_bx, to_by, to_bxy):
        pl.semaphore_signal(barrier, inc=1, device_id=where, device_id_type=MESH)
    pl.semaphore_wait(barrier, 7)

    piece = 128 // PIECES
    send_far, pass_far_near, pass_last = [], [], []
    for k in range(PIECES):
        part = pl.ds(128 * FAR + piece * k, piece)
        near_part = pl.ds(128 * NEAR_FAR + piece * k, piece)
        last_part = pl.ds(128 * SIB_NEAR_FAR + piece * k, piece)
        send_far.append(
            remote(k, tokens.at[1 - group, pl.ds(piece * k, piece)], tok.at[part], to_far)
        )
        pass_far_near.append(remote(PIECES + k, tok.at[part], tok.at[near_part], to_near))
        pass_last.append(remote(2 * PIECES + k, tok.at[near_part], tok.at[last_part], to_sib))
    send_near = remote(12, tokens.at[group], block(tok, NEAR), to_near)
    send_sib = remote(13, tokens.at[group], block(tok, SIB), to_sib)
    pass_far_sib = remote(14, block(tok, FAR), block(tok, SIB_FAR), to_sib)
    pass_near_sib = remote(15, block(tok, NEAR), block(tok, SIB_NEAR), to_sib)
    send_og = remote(16, out_grad.at[1 - group], og.at[pl.ds(128, 128)], to_far)
    for item in send_far:
        item.start()
    send_near.start()
    send_sib.start()

    for k in range(1, 6):
        loads[k].wait()
    for row, at in ((0, 0), (1, 768)):
        scale_row = rank_scale[pl.ds(row, 1), :]
        out_row = out_scale[pl.ds(row, 1), pl.ds(half, 384)]

        def effective(t, _, at=at, scale_row=scale_row, out_row=out_row):
            rows = pl.ds(pl.multiple_of(t * 256, 256), 256)
            scaled = (v_in[rows, :].astype(F32) * scale_row).astype(BF16)
            wide = dot(scaled, v_out[...]) * out_row
            w_all[rows, at : at + 384] = (w_all[rows, at : at + 384].astype(F32) + wide).astype(BF16)
            return 0

        lax.fori_loop(0, 3, effective, 0)
    v_out_t[...] = v_out[...].astype(F32).T.astype(BF16)

    split = splits[group]
    lane = lax.broadcasted_iota(jnp.int32, (128, 128), 1)
    row_at = lax.broadcasted_iota(jnp.int32, (128, 128), 0)
    flip_one, flip_two, flip_four = sib - s, near - s, far - s
    starts = (
        s,
        s + flip_one,
        s + flip_four,
        s + flip_four + flip_one,
        s + flip_two + flip_four,
        s + flip_two + flip_four + flip_one,
        s + flip_two,
        s + flip_two + flip_one,
    )
    for k in range(8):
        first = (starts[k] * 128 + row_at < split).astype(F32)
        second = 1.0 - first
        key_side = jnp.where(lane == 0, first, jnp.where(lane == 1, second, 0.0)).astype(BF16)
        for p in range(3):
            k_ext[p, 128 * k : 128 * k + 128, 128:256] = key_side
        if k < 4:
            query_side = (
                jnp.where(lane == 0, second, jnp.where(lane == 1, first, 0.0)) * (-BIG)
            ).astype(BF16)
            for h in range(6):
                q_ext[h, 128 * k : 128 * k + 128, 128:256] = query_side

    shift_q = shifts[0:1, pl.ds(half, 384)]
    shift_v = shifts[1:2, pl.ds(half, 384)]
    low_lane = lax.broadcasted_iota(jnp.int32, (256, 128), 1) < 64

    def project(first, queries):
        to = slice(128 * first, 128 * first + 256)
        rows = tok[to, :]
        keys = dot(rows, w_all[:, 384:768])
        values = dot(rows, w_all[:, 768:1152]) + shift_v
        low_keys = keys.astype(BF16)
        low_values = values.astype(BF16)
        for p in range(3):
            k_ext[p, to, 0:128] = low_keys[:, 128 * p : 128 * p + 128]
            val[p, to, :] = low_values[:, 128 * p : 128 * p + 128]
        k_t[:, to] = keys.T.astype(BF16)
        v_t[:, to] = values.T.astype(BF16)
        if queries:
            query = dot(rows, w_all[:, 0:384]) + shift_q
            low_query = query.astype(BF16).astype(F32) * 0.125
            for h in range(6):
                p = h // 2
                mine = low_lane if h % 2 == 0 else jnp.logical_not(low_lane)
                masked = jnp.where(mine, low_query[:, 128 * p : 128 * p + 128], 0.0)
                q_ext[h, to, 0:128] = masked.astype(BF16)

    loads[0].wait()
    send_sib.wait_recv()
    project(OWN, True)
    for k in range(PIECES):
        if k == PIECES - 1:
            send_near.wait_recv()
            pass_near_sib.start()
            pass_near_sib.wait_recv()
            project(NEAR, False)
        send_far[k].wait_recv()
        pass_far_near[k].start()
    pass_far_sib.start()
    for k in range(PIECES):
        pass_far_near[k].wait_recv()
        pass_last[k].start()
        if k == PIECES - 2:
            pass_far_sib.wait_recv()
            project(FAR, True)
    send_og.start()
    for k in range(PIECES):
        pass_last[k].wait_recv()
    project(NEAR_FAR, False)

    def forward_head(h, _):
        p = h // 2
        rows_h = pl.ds(pl.multiple_of(h * 64, 64), 64)
        top = None
        for k in range(4):
            part = dot_nt(k_ext[p, 256 * k : 256 * k + 256, :], q_ext[h])
            s_buf[256 * k : 256 * k + 256, :] = part
            peak = jnp.max(part, axis=0, keepdims=True)
            top = peak if top is None else jnp.maximum(top, peak)
        total = jnp.zeros((1, 512), F32)
        out = jnp.zeros((64, 512), F32)
        for k in range(4):
            weight = jnp.exp(s_buf[256 * k : 256 * k + 256, :] - top)
            total = total + jnp.sum(weight, axis=0, keepdims=True)
            low_weight = weight.astype(BF16)
            probs[h, 256 * k : 256 * k + 256, :] = low_weight
            out = out + dot(v_t[rows_h, 256 * k : 256 * k + 256], low_weight)
        inverse = 1.0 / total
        inv_l[h] = inverse
        att_t[rows_h, :] = out * inverse
        return 0

    lax.fori_loop(0, 6, forward_head, 0)

    swap_att = remote(17, att_send, att_recv, to_sib)
    for k, at in ((0, 128 * SIB), (128, 128 * SIB_FAR)):
        att_send[k : k + 128, :] = att_t[:, at : at + 128].T.astype(BF16)
    swap_att.start()

    def norm(values_in):
        centered = values_in - jnp.mean(values_in, axis=-1, keepdims=True)
        inverse = lax.rsqrt(jnp.mean(centered * centered, axis=-1, keepdims=True) + 1e-05)
        return centered * inverse, inverse

    def norm_back(grad_in, normed, inverse, gain_row):
        scaled = grad_in * gain_row
        return inverse * (
            scaled
            - jnp.mean(scaled, axis=-1, keepdims=True)
            - normed * jnp.mean(scaled * normed, axis=-1, keepdims=True)
        )

    loads[6].wait()
    attended_mine = jnp.concatenate([att_t[:, 0:128], att_t[:, 256:384]], axis=1).T
    token_rows = jnp.concatenate([tok[0:128, :], tok[256:384, :]], axis=0).astype(F32)
    branch = dot(attended_mine.astype(BF16), w_out[pl.ds(half, 384), :])
    swap_att.wait_recv()
    branch = branch + dot(att_recv[...], w_out[pl.ds(other_half, 384), :]) + shifts[2:3, :]
    normed_one, inverse_one = norm(token_rows + branch)
    n_one[...] = normed_one
    hidden = normed_one * gains[0:1, :] + shifts[4:5, :]
    hid[...] = hidden
    low_rows[...] = hidden.astype(BF16)

    loads[7].wait()
    loads[8].wait()
    acc[...] = jnp.zeros_like(acc)

    def ffn_forward(t, _):
        cols = pl.ds(pl.multiple_of(t * 512, 512), 512)
        inner = dot(low_rows[...], w_one[:, cols]) + ffn_bias[:, cols]
        phi = 0.5 * (1.0 + lax.erf(inner * 0.7071067811865476))
        density = 0.3989422804014327 * jnp.exp(-0.5 * inner * inner)
        gprime[:, cols] = phi + inner * density
        acc[...] += dot((inner * phi).astype(BF16), w_two[cols, :])
        return 0

    lax.fori_loop(0, 6, ffn_forward, 0)
    normed_two, inverse_two = norm(hid[...] + acc[...] + shifts[3:4, :])
    lo_buf[...] = (normed_two * gains[1:2, :] + shifts[5:6, :]).astype(BF16)
    send_lo = remote(18, lo_buf.at[pl.ds(128, 128)], layer_out.at[group], to_far)
    keep_lo = local(10, lo_buf.at[pl.ds(0, 128)], layer_out.at[group])
    send_lo.start()
    keep_lo.start()
    loads[9].wait()
    send_og.wait_recv()
    grad_two = norm_back(og[...].astype(F32), normed_two, inverse_two, gains[1:2, :])
    g_two[...] = grad_two
    low_rows[...] = grad_two.astype(BF16)
    acc[...] = grad_two

    def ffn_backward(t, _):
        cols = pl.ds(pl.multiple_of(t * 512, 512), 512)
        grad_act = dot_nt(low_rows[...], w_two[cols, :])
        grad_inner = (grad_act * gprime[:, cols]).astype(BF16)
        acc[...] += dot_nt(grad_inner, w_one[:, cols])
        return 0

    lax.fori_loop(0, 6, ffn_backward, 0)
    grad_one = norm_back(acc[...], n_one[...], inverse_one, gains[0:1, :])
    g_one[...] = grad_one
    low_one = grad_one.astype(BF16)
    swap_ga = remote(19, ga_send, ga_recv, to_sib)
    ga_send[...] = dot_nt(low_one, w_out[pl.ds(other_half, 384), :]).astype(BF16)
    swap_ga.start()
    ga_mine[...] = dot_nt(low_one, w_out[pl.ds(half, 384), :]).astype(BF16)
    swap_ga.wait_recv()

    go_full = (
        jnp.concatenate(
            [ga_mine[0:128], ga_recv[0:128], ga_mine[128:256], ga_recv[128:256]], axis=0
        )
        .astype(F32)
        .T
    )
    top_rows = lax.broadcasted_iota(jnp.int32, (128, 512), 0) < 64
    for p in range(3):
        pair = go_full[128 * p : 128 * p + 128, :]
        attended = att_t[128 * p : 128 * p + 128, :]
        for e in range(2):
            h = 2 * p + e
            mine = top_rows if e == 0 else jnp.logical_not(top_rows)
            scaled = jnp.where(mine, pair * inv_l[h], 0.0)
            low_scaled = scaled.astype(BF16)
            rounded = low_scaled.astype(F32)
            go_t[h] = low_scaled
            go_m[h] = rounded.T.astype(BF16)
            delta[h] = jnp.sum(rounded * attended, axis=0, keepdims=True)

    def backward_pair(p, start, first):
        rows = slice(start, start + 256)
        grad_keys = None
        grad_values = None
        for e in range(2):
            h = 2 * p + e
            rows_h = pl.ds(pl.multiple_of(h * 64, 64), 64)
            weight = probs[h, rows, :]
            grad_prob = dot(val[p, rows, :], go_t[h])
            grad_score = (weight.astype(F32) * (grad_prob - delta[h])).astype(BF16)
            value_part = dot(weight, go_m[h])
            key_part = dot(grad_score, q_ext[h, :, 0:128])
            query_part = dot(k_t[rows_h, rows], grad_score)
            grad_values = value_part if e == 0 else grad_values + value_part
            grad_keys = key_part if e == 0 else grad_keys + key_part
            if first:
                dq_t[rows_h, :] = query_part
            else:
                dq_t[rows_h, :] += query_part
        d_kv[rows, pl.ds(pl.multiple_of(p * 128, 128), 128)] = grad_keys.astype(BF16)
        d_kv[rows, pl.ds(pl.multiple_of(384 + p * 128, 128), 128)] = grad_values.astype(BF16)

    def pairs(start, low, high):
        def step(p, _):
            backward_pair(p, start, start == 128 * NEAR_FAR)
            return 0

        lax.fori_loop(low, high, step, 0)

    def token_terms(start):
        return dot_nt(d_kv[start : start + 256, :], w_all[:, 384:1152])

    swap_parts = [
        remote(20 + k, part_send.at[pl.ds(128 * k, 128)], part_recv.at[pl.ds(128 * k, 128)], to_sib)
        for k in range(4)
    ]
    send_parts = [
        remote(24 + k, tn_send.at[pl.ds(128 * k, 128)], tn_recv.at[pl.ds(128 * k, 128)], to_near)
        for k in range(2)
    ]

    def share(k, terms):
        part_send[128 * k : 128 * k + 128, :] = terms[128:256].astype(BF16)
        swap_parts[k].start()
        part_mine[128 * k : 128 * k + 128, :] = terms[0:128]

    def shared(k):
        swap_parts[k].wait_recv()
        rows = slice(128 * k, 128 * k + 128)
        return part_mine[rows, :] + part_recv[rows, :].astype(F32)

    def pass_on(k):
        tn_send[128 * k : 128 * k + 128, :] = shared(k).astype(BF16)
        send_parts[k].start()

    pairs(128 * NEAR_FAR, 0, 3)
    share(0, token_terms(128 * NEAR_FAR))
    pairs(128 * NEAR, 0, 1)
    pass_on(0)
    pairs(128 * NEAR, 1, 3)
    share(1, token_terms(128 * NEAR))
    pairs(128 * FAR, 0, 1)
    pass_on(1)
    pairs(128 * FAR, 1, 3)
    far_terms[...] = token_terms(128 * FAR)
    pairs(128 * OWN, 0, 3)

    low_dq = (dq_t[...] * 0.125).T.astype(BF16)
    share(2, far_terms[...] + dot_nt(low_dq[256:512, :], w_all[:, 0:384]))
    far_part = shared(2) + g_one[128:256, :]
    send_parts[0].wait_recv()
    ig_buf[128:256, :] = (far_part + tn_recv[0:128, :].astype(F32)).astype(BF16)
    send_ig = remote(26, ig_buf.at[pl.ds(128, 128)], in_grad.at[group], to_far)
    keep_ig = local(11, ig_buf.at[pl.ds(0, 128)], in_grad.at[group])
    send_ig.start()

    low_dq_t = (dq_t[...] * 0.125).astype(BF16)
    grad_q_map = dot(low_dq_t, tok[0:512, :]).astype(BF16)
    grad_v_map = dot(d_kv[:, 384:768].astype(F32).T.astype(BF16), tok[...]).astype(BF16)
    sum_buf[0:8, :] = jnp.zeros((8, 1024), F32)
    for row, grad_map in ((0, grad_q_map), (1, grad_v_map)):
        product_map = dot(grad_map, v_in[...]) * v_out_t[...].astype(F32)
        out_row = out_scale[pl.ds(row, 1), pl.ds(half, 384)]
        out_col = jnp.broadcast_to(out_row, (128, 384)).T[:, 0:1]
        sum_buf[row : row + 1, :] = jnp.sum(product_map * out_col, axis=0, keepdims=True)
        out_part = jnp.sum(product_map * rank_scale[pl.ds(row, 1), :], axis=1, keepdims=True)
        out_part_row = jnp.broadcast_to(out_part, (384, 128)).T[0:1, :]
        sum_buf[2 + row : 3 + row, pl.ds(half, 384)] = out_part_row

    def exchange(k, stage, wheres):
        swaps = [
            remote(
                k + n,
                sum_buf.at[pl.ds(8 * stage, 8)],
                sum_recv.at[pl.ds(8 * (k - 27 + n), 8)],
                where,
            )
            for n, where in enumerate(wheres)
        ]
        for swap in swaps:
            swap.start()
        return swaps

    def received(k):
        return sum_recv[8 * k : 8 * k + 8, :]

    core_swaps = exchange(27, 0, (to_sib,))
    share(3, token_terms(128 * OWN) + dot_nt(low_dq[0:256, :], w_all[:, 0:384]))
    core_swaps[0].wait_recv()
    sum_buf[8:16, :] = sum_buf[0:8, :] + received(0)
    plane_swaps = exchange(28, 1, (to_bx, to_by, to_bxy))
    own_part = shared(3) + g_one[0:128, :]
    send_parts[1].wait_recv()
    ig_buf[0:128, :] = (own_part + tn_recv[128:256, :].astype(F32)).astype(BF16)
    keep_ig.start()
    for swap in plane_swaps:
        swap.wait_recv()
    sum_buf[16:24, :] = (sum_buf[8:16, :] + received(1)) + (received(2) + received(3))
    line_swaps = exchange(31, 2, (to_near, to_far, to_near_far))
    for swap in line_swaps:
        swap.wait_recv()
    sums[...] = (sum_buf[16:24, :] + received(4)) + (received(5) + received(6))

    send_lo.wait_recv()
    send_ig.wait_recv()
    keep_lo.wait()
    keep_ig.wait()
    for item in (
        *send_far,
        *pass_far_near,
        *pass_last,
        send_near,
        send_sib,
        pass_far_sib,
        pass_near_sib,
        send_og,
        swap_att,
        swap_ga,
        send_lo,
        *swap_parts,
        *send_parts,
        send_ig,
        *core_swaps,
        *plane_swaps,
        *line_swaps,
    ):
        item.wait_send()


def finish_kernel(layer_in, grad_in, sums, layer_out, in_grad, rank_total, out_total, norms):
    layer_out[...] = layer_in[...]
    in_grad[...] = grad_in[...]
    rank_total[...] = sums[0:2, :]
    out_total[...] = sums[2:4, 0:768]
    totals = sums[0:4, :]
    lengths = jnp.sqrt(jnp.sum(totals * totals, axis=1, keepdims=True))
    for k in range(4):
        norms[k] = lengths[k, 0]


def fast_body(
    tokens,
    attn_in_weight,
    out_weight,
    ffn_in_weight,
    ffn_out_weight,
    vera_in,
    vera_out,
    rank_scale,
    out_scale,
    gains,
    shifts,
    ffn_bias,
    splits,
    out_grad,
):
    hbm = pl.BlockSpec(memory_space=pl.ANY)
    vmem = pl.BlockSpec(memory_space=pltpu.VMEM)
    smem = pl.BlockSpec(memory_space=pltpu.SMEM)
    shape = tokens.shape
    scratch = [
        ((1024, 768), BF16),
        ((256, 768), BF16),
        ((768, 1152), BF16),
        ((768, 768), BF16),
        ((768, 3072), BF16),
        ((3072, 768), BF16),
        ((768, 1024), BF16),
        ((1024, 384), BF16),
        ((384, 1024), BF16),
        ((3, 1024, 256), BF16),
        ((6, 512, 256), BF16),
        ((3, 1024, 128), BF16),
        ((384, 1024), BF16),
        ((384, 1024), BF16),
        ((6, 1024, 512), BF16),
        ((1024, 512), F32),
        ((384, 512), F32),
        ((6, 1, 512), F32),
        ((256, 384), BF16),
        ((256, 384), BF16),
        ((256, 768), F32),
        ((256, 768), F32),
        ((256, 768), F32),
        ((256, 3072), F32),
        ((256, 768), BF16),
        ((256, 768), F32),
        ((256, 768), F32),
        ((256, 768), BF16),
        ((256, 384), BF16),
        ((256, 384), BF16),
        ((256, 384), BF16),
        ((6, 128, 512), BF16),
        ((6, 512, 128), BF16),
        ((6, 1, 512), F32),
        ((1024, 768), BF16),
        ((384, 512), F32),
        ((512, 768), BF16),
        ((512, 768), BF16),
        ((512, 768), F32),
        ((256, 768), F32),
        ((256, 768), BF16),
        ((256, 768), BF16),
        ((256, 768), BF16),
        ((24, 1024), F32),
        ((56, 1024), F32),
    ]
    rows_type = jax.ShapeDtypeStruct(shape, BF16)
    layer_rows, grad_rows, sums = pl.pallas_call(
        layer_kernel,
        out_shape=(rows_type, rows_type, jax.ShapeDtypeStruct((8, 1024), F32)),
        in_specs=[hbm] * 8 + [vmem] * 5 + [smem],
        out_specs=(hbm, hbm, vmem),
        scratch_shapes=[pltpu.VMEM(dims, kind) for dims, kind in scratch]
        + [
            pltpu.SemaphoreType.DMA((34,)),
            pltpu.SemaphoreType.DMA((34,)),
            pltpu.SemaphoreType.DMA((12,)),
        ],
        compiler_params=pltpu.CompilerParams(
            collective_id=0, has_side_effects=True, vmem_limit_bytes=60 * 2**20
        ),
        name="encoder_layer",
    )(
        tokens,
        attn_in_weight,
        out_weight,
        ffn_in_weight,
        ffn_out_weight,
        vera_in,
        vera_out,
        out_grad,
        rank_scale,
        out_scale,
        gains,
        shifts,
        ffn_bias.reshape(1, -1),
        splits,
    )
    return pl.pallas_call(
        finish_kernel,
        out_shape=(
            rows_type,
            rows_type,
            jax.ShapeDtypeStruct(rank_scale.shape, F32),
            jax.ShapeDtypeStruct(out_scale.shape, F32),
            jax.ShapeDtypeStruct((4,), F32),
        ),
        in_specs=[vmem, vmem, vmem],
        out_specs=(vmem, vmem, vmem, vmem, smem),
        name="finish",
    )(layer_rows, grad_rows, sums)


def solution(mesh):
    chosen = fast_body if fits(mesh) else body
    in_specs = (
        P("batch", "seq", None),
        P(),
        P(),
        P(),
        P(),
        P(),
        P(),
        P(),
        P(),
        P(),
        P(),
        P(),
        P("batch"),
        P("batch", "seq", None),
    )
    out_specs = (P("batch", "seq", None), P("batch", "seq", None), P(), P(), P())
    return jax.shard_map(chosen, mesh=mesh, in_specs=in_specs, out_specs=out_specs, check_vma=False)
```

```python
import functools

import jax
import jax.numpy as jnp
from jax import lax
from jax.experimental import pallas as pl
from jax.experimental.pallas import tpu as pltpu
from jax.sharding import PartitionSpec as P

HEADS = 12


masked_score = -1e30
key_block = 512


def product(left_side, right_side):
    return jnp.dot(left_side, right_side, preferred_element_type=jnp.float32)


def product_t(left_side, right_side):
    return lax.dot_general(
        left_side, right_side, (((1,), (1,)), ((), ())), preferred_element_type=jnp.float32
    )


def gelu_exact(inputs):
    return jax.nn.gelu(inputs, approximate=False)


def norm_forward(values_in, gain_row, shift_row):
    centered = values_in - jnp.mean(values_in, axis=-1, keepdims=True)
    inverse = lax.rsqrt(jnp.mean(centered * centered, axis=-1, keepdims=True) + 1e-05)
    normed = centered * inverse
    return (normed * gain_row + shift_row, normed, inverse)


def norm_backward(grad_in, normed, inverse, gain_row):
    scaled = grad_in * gain_row
    return inverse * (
        scaled
        - jnp.mean(scaled, axis=-1, keepdims=True)
        - normed * jnp.mean(scaled * normed, axis=-1, keepdims=True)
    )


def block_width():
    return key_block


def body(
    tokens,
    attn_in_weight,
    out_weight,
    ffn_in_weight,
    ffn_out_weight,
    vera_in,
    vera_out,
    rank_scale,
    out_scale,
    gains,
    shifts,
    ffn_bias,
    splits,
    out_grad,
):
    sequences, per_device, model_width = tokens.shape
    head_dim = model_width // HEADS
    score_scale = head_dim ** (-0.5)
    cycle_place = lax.axis_index("seq")
    token_rows = tokens.reshape(-1, model_width)
    token_float = token_rows.astype(jnp.float32)
    rank_in = product(token_rows, vera_in)
    rank_q = (rank_in * rank_scale[0]).astype(jnp.bfloat16)
    rank_v = (rank_in * rank_scale[1]).astype(jnp.bfloat16)
    wide_q = product(rank_q, vera_out)
    wide_v = product(rank_v, vera_out)
    projected = product(token_rows, attn_in_weight)
    query = projected[:, :model_width] + shifts[0] + out_scale[0] * wide_q
    keys = projected[:, model_width : 2 * model_width]
    values = projected[:, 2 * model_width :] + shifts[1] + out_scale[1] * wide_v
    query_low = query.astype(jnp.bfloat16).reshape(sequences, per_device, HEADS, head_dim)
    pair_low = (
        jnp.concatenate([keys, values], axis=-1)
        .astype(jnp.bfloat16)
        .reshape(sequences, per_device, 2 * model_width)
    )
    query_pos = cycle_place * per_device + jnp.arange(per_device, dtype=jnp.int32)
    query_side = query_pos[None, :] < splits[:, None]

    def block_scores(pair_piece, block_start):
        count_keys = pair_piece.shape[1]
        key_pos = block_start + jnp.arange(count_keys, dtype=jnp.int32)
        key_side = key_pos[None, :] < splits[:, None]
        allowed = (query_side[:, :, None] == key_side[:, None, :])[:, None]
        key_heads = pair_piece[:, :, :model_width].reshape(sequences, count_keys, HEADS, head_dim)
        value_heads = pair_piece[:, :, model_width:].reshape(sequences, count_keys, HEADS, head_dim)
        raw_scores = (
            jnp.einsum("sqhe,skhe->shqk", query_low, key_heads, preferred_element_type=jnp.float32)
            * score_scale
        )
        return (raw_scores, allowed, key_heads, value_heads)

    start_max = jnp.full((sequences, HEADS, per_device), masked_score, jnp.float32)
    start_sum = jnp.zeros((sequences, HEADS, per_device), jnp.float32)
    start_acc = jnp.zeros((sequences, per_device, HEADS, head_dim), jnp.float32)
    carry = (start_max, start_sum, start_acc)
    pair_piece = lax.all_gather(pair_low, "seq", axis=1, tiled=True)
    shard_start = jnp.int32(0)
    count_keys = pair_piece.shape[1]
    block_size = block_width()
    for absorb_block_index in range(count_keys // block_size):
        absorb_pair_piece = pair_piece[
            :, absorb_block_index * block_size : (absorb_block_index + 1) * block_size
        ]
        running_max, running_sum, absorb_accumulated = carry
        absorb_raw_scores, absorb_allowed, absorb_key_heads, absorb_value_heads = block_scores(
            absorb_pair_piece, shard_start + absorb_block_index * block_size
        )
        new_max = jnp.maximum(
            running_max,
            jnp.max(jnp.where(absorb_allowed, absorb_raw_scores, masked_score), axis=-1),
        )
        block_weights = jnp.where(
            absorb_allowed, jnp.exp(absorb_raw_scores - new_max[..., None]), 0.0
        )
        rescale = jnp.exp(running_max - new_max)
        running_sum = running_sum * rescale + jnp.sum(block_weights, axis=-1)
        added = jnp.einsum(
            "shqk,skhe->sqhe",
            block_weights.astype(jnp.bfloat16),
            absorb_value_heads,
            preferred_element_type=jnp.float32,
        )
        absorb_accumulated = (
            absorb_accumulated * jnp.transpose(rescale, (0, 2, 1))[..., None] + added
        )
        carry = (new_max, running_sum, absorb_accumulated)
    final_max, final_sum, accumulated = carry
    attended = accumulated / jnp.transpose(final_sum, (0, 2, 1))[..., None]
    log_total = final_max + jnp.log(final_sum)
    branch = product(attended.reshape(-1, model_width).astype(jnp.bfloat16), out_weight) + shifts[2]
    hidden, normed_one, inverse_one = norm_forward(token_float + branch, gains[0], shifts[4])
    inner = product(hidden.astype(jnp.bfloat16), ffn_in_weight) + ffn_bias
    activated, gelu_pull = jax.vjp(gelu_exact, inner)
    ffn_branch = product(activated.astype(jnp.bfloat16), ffn_out_weight) + shifts[3]
    layer_out, normed_two, inverse_two = norm_forward(hidden + ffn_branch, gains[1], shifts[5])
    grad_two = norm_backward(
        out_grad.reshape(-1, model_width).astype(jnp.float32), normed_two, inverse_two, gains[1]
    )
    grad_act = product_t(grad_two.astype(jnp.bfloat16), ffn_out_weight)
    grad_inner = gelu_pull(grad_act)[0].astype(jnp.bfloat16)
    grad_hidden = grad_two + product_t(grad_inner, ffn_in_weight)
    grad_one = norm_backward(grad_hidden, normed_one, inverse_one, gains[0])
    grad_att = (
        product_t(grad_one.astype(jnp.bfloat16), out_weight)
        .astype(jnp.bfloat16)
        .reshape(sequences, per_device, HEADS, head_dim)
    )
    delta = jnp.transpose(jnp.sum(grad_att.astype(jnp.float32) * attended, axis=-1), (0, 2, 1))
    grad_query = jnp.zeros((sequences, per_device, HEADS, head_dim), jnp.float32)
    whole_pairs = lax.all_gather(pair_low, "seq", axis=1, tiled=True)
    whole_len = whole_pairs.shape[1]
    block_size = block_width()
    key_terms = []
    for block_index in range(whole_len // block_size):
        block_pair_piece = whole_pairs[:, block_index * block_size : (block_index + 1) * block_size]
        block_raw_scores, block_allowed, block_key_heads, block_value_heads = block_scores(
            block_pair_piece, block_index * block_size
        )
        prob = jnp.where(block_allowed, jnp.exp(block_raw_scores - log_total[..., None]), 0.0)
        grad_prob = jnp.einsum(
            "sqhe,skhe->shqk", grad_att, block_value_heads, preferred_element_type=jnp.float32
        )
        grad_score = (prob * (grad_prob - delta[..., None])).astype(jnp.bfloat16)
        grad_value = jnp.einsum(
            "shqk,sqhe->skhe",
            prob.astype(jnp.bfloat16),
            grad_att,
            preferred_element_type=jnp.float32,
        )
        grad_key = (
            jnp.einsum("shqk,sqhe->skhe", grad_score, query_low, preferred_element_type=jnp.float32)
            * score_scale
        )
        query_part = (
            jnp.einsum(
                "shqk,skhe->sqhe", grad_score, block_key_heads, preferred_element_type=jnp.float32
            )
            * score_scale
        )
        block_count_keys = block_pair_piece.shape[1]
        pair_part = jnp.concatenate(
            [
                grad_key.reshape(sequences, block_count_keys, model_width),
                grad_value.reshape(sequences, block_count_keys, model_width),
            ],
            axis=-1,
        )
        query_part, pair_part = (query_part, pair_part)
        grad_query = grad_query + query_part
        key_terms.append(pair_part)
    pair_sum = lax.psum_scatter(
        jnp.concatenate(key_terms, axis=1), "seq", scatter_dimension=1, tiled=True
    )
    pair_grad_low = pair_sum.astype(jnp.bfloat16).reshape(-1, 2 * model_width)
    query_grad_low = grad_query.reshape(-1, model_width).astype(jnp.bfloat16)
    query_grad_float = query_grad_low.astype(jnp.float32)
    value_grad_float = pair_grad_low[:, model_width:].astype(jnp.float32)
    grad_wide_q = (query_grad_float * out_scale[0]).astype(jnp.bfloat16)
    grad_wide_v = (value_grad_float * out_scale[1]).astype(jnp.bfloat16)
    grad_rank_q = product_t(grad_wide_q, vera_out)
    grad_rank_v = product_t(grad_wide_v, vera_out)
    grad_rank_in = (grad_rank_q * rank_scale[0] + grad_rank_v * rank_scale[1]).astype(jnp.bfloat16)
    grad_tokens = (
        grad_one
        + product_t(jnp.concatenate([query_grad_low, pair_grad_low], axis=-1), attn_in_weight)
        + product_t(grad_rank_in, vera_in)
    )
    rank_terms = jnp.stack(
        [jnp.sum(grad_rank_q * rank_in, axis=0), jnp.sum(grad_rank_v * rank_in, axis=0)]
    )
    out_terms = jnp.stack(
        [jnp.sum(query_grad_float * wide_q, axis=0), jnp.sum(value_grad_float * wide_v, axis=0)]
    )
    rank_total, out_total = lax.psum((rank_terms, out_terms), ("batch", "seq"))
    scale_norms = jnp.concatenate(
        [
            jnp.sqrt(jnp.sum(rank_total * rank_total, axis=1)),
            jnp.sqrt(jnp.sum(out_total * out_total, axis=1)),
        ]
    )
    return (
        layer_out.astype(jnp.bfloat16).reshape(sequences, per_device, model_width),
        grad_tokens.astype(jnp.bfloat16).reshape(sequences, per_device, model_width),
        rank_total,
        out_total,
        scale_norms,
    )


MESH = pl.DeviceIdType.MESH
BIG = 1e30
F32 = jnp.float32
BF16 = jnp.bfloat16


def fits(mesh):
    return mesh.shape["seq"] == 8 and mesh.shape["batch"] == 4


def dot(left, right):
    return lax.dot_general(left, right, (((1,), (0,)), ((), ())), preferred_element_type=F32)


def dot_nt(left, right):
    return lax.dot_general(left, right, (((1,), (1,)), ((), ())), preferred_element_type=F32)


OWN, SIB, FAR, SIB_FAR, NEAR_FAR, SIB_NEAR_FAR, NEAR, SIB_NEAR = range(8)
PIECES = 4
PART_OWN, PART_FAR, PART_LAST = range(3)


def layer_kernel(
    tokens,
    attn_in,
    out_w,
    ffn_in,
    ffn_out,
    vera_in,
    vera_out,
    out_grad,
    rank_scale,
    out_scale,
    gains,
    shifts,
    ffn_bias,
    splits,
    layer_out,
    in_grad,
    sums,
    tok,
    og,
    w_all,
    w_out,
    w_one,
    w_two,
    v_in,
    v_out,
    v_out_t,
    k_ext,
    q_ext,
    val,
    k_t,
    v_t,
    probs,
    s_buf,
    att_t,
    part_top,
    part_sum,
    part_out,
    share,
    att_send,
    att_recv,
    hid,
    n_one,
    wide,
    gprime,
    low_rows,
    g_two,
    g_one,
    lo_buf,
    ga_send,
    ga_recv,
    ga_mine,
    go_t,
    go_m,
    delta,
    d_kv,
    dq_t,
    part_send,
    part_recv,
    part_mine,
    far_terms,
    tn_send,
    tn_recv,
    ig_buf,
    sum_buf,
    sum_recv,
    send_sem,
    recv_sem,
    load_sem,
):
    s = lax.axis_index("seq")
    b = lax.axis_index("batch")
    core = s % 2
    group = s // 4
    sib = s + 1 - 2 * core
    near = s + 2 - 4 * ((s // 2) % 2)
    far = s + 4 - 8 * group
    bx = b + 1 - 2 * (b % 2)
    by = b + 2 - 4 * (b // 2)
    half = pl.multiple_of(core * 384, 384)
    other_half = pl.multiple_of(384 - core * 384, 384)

    def remote(k, src, dst, where):
        return pltpu.make_async_remote_copy(
            src_ref=src,
            dst_ref=dst,
            send_sem=send_sem.at[k],
            recv_sem=recv_sem.at[k],
            device_id=where,
            device_id_type=MESH,
        )

    def local(k, src, dst):
        return pltpu.make_async_copy(src, dst, load_sem.at[k])

    def block(ref, k, n=1):
        return ref.at[pl.ds(128 * k, 128 * n)]

    near_far = far + near - s
    to_sib, to_near, to_far = {"seq": sib}, {"seq": near}, {"seq": far}
    to_near_far = {"seq": near_far}
    to_bx, to_by, to_bxy = {"batch": bx}, {"batch": by}, {"batch": bx + by - b}

    loads = [
        local(0, tokens.at[group], block(tok, OWN)),
        local(1, vera_in, v_in),
        local(2, vera_out.at[:, pl.ds(half, 384)], v_out),
        local(3, attn_in.at[:, pl.ds(half, 384)], w_all.at[:, pl.ds(0, 384)]),
        local(4, attn_in.at[:, pl.ds(768 + half, 384)], w_all.at[:, pl.ds(384, 384)]),
        local(5, attn_in.at[:, pl.ds(1536 + half, 384)], w_all.at[:, pl.ds(768, 384)]),
        local(6, out_w, w_out),
        local(7, ffn_in, w_one),
        local(8, ffn_out, w_two),
        local(9, out_grad.at[group], og.at[pl.ds(0, 128)]),
    ]
    for item in loads:
        item.start()

    barrier = pltpu.get_barrier_semaphore()
    for where in (to_sib, to_near, to_far, to_near_far, to_bx, to_by, to_bxy):
        pl.semaphore_signal(barrier, inc=1, device_id=where, device_id_type=MESH)
    pl.semaphore_wait(barrier, 7)

    piece = 128 // PIECES
    send_far, pass_far_near, pass_last = [], [], []
    for k in range(PIECES):
        part = pl.ds(128 * FAR + piece * k, piece)
        near_part = pl.ds(128 * NEAR_FAR + piece * k, piece)
        last_part = pl.ds(128 * SIB_NEAR_FAR + piece * k, piece)
        send_far.append(
            remote(k, tokens.at[1 - group, pl.ds(piece * k, piece)], tok.at[part], to_far)
        )
        pass_far_near.append(remote(PIECES + k, tok.at[part], tok.at[near_part], to_near))
        pass_last.append(remote(2 * PIECES + k, tok.at[near_part], tok.at[last_part], to_sib))
    send_near = remote(12, tokens.at[group], block(tok, NEAR), to_near)
    send_sib = remote(13, tokens.at[group], block(tok, SIB), to_sib)
    pass_far_sib = remote(14, block(tok, FAR), block(tok, SIB_FAR), to_sib)
    pass_near_sib = remote(15, block(tok, NEAR), block(tok, SIB_NEAR), to_sib)
    send_og = remote(16, out_grad.at[1 - group], og.at[pl.ds(128, 128)], to_far)
    for item in send_far:
        item.start()
    send_near.start()
    send_sib.start()

    for k in range(1, 6):
        loads[k].wait()
    for row, at in ((0, 0), (1, 768)):
        scale_row = rank_scale[pl.ds(row, 1), :]
        out_row = out_scale[pl.ds(row, 1), pl.ds(half, 384)]

        def effective(t, _, at=at, scale_row=scale_row, out_row=out_row):
            rows = pl.ds(pl.multiple_of(t * 256, 256), 256)
            scaled = (v_in[rows, :].astype(F32) * scale_row).astype(BF16)
            wide = dot(scaled, v_out[...]) * out_row
            w_all[rows, at : at + 384] = (w_all[rows, at : at + 384].astype(F32) + wide).astype(BF16)
            return 0

        lax.fori_loop(0, 3, effective, 0)
    v_out_t[...] = v_out[...].astype(F32).T.astype(BF16)

    split = splits[group]
    lane = lax.broadcasted_iota(jnp.int32, (128, 128), 1)
    row_at = lax.broadcasted_iota(jnp.int32, (128, 128), 0)
    flip_one, flip_two, flip_four = sib - s, near - s, far - s
    starts = (
        s,
        s + flip_one,
        s + flip_four,
        s + flip_four + flip_one,
        s + flip_two + flip_four,
        s + flip_two + flip_four + flip_one,
        s + flip_two,
        s + flip_two + flip_one,
    )
    for k in range(8):
        first = (starts[k] * 128 + row_at < split).astype(F32)
        second = 1.0 - first
        key_side = jnp.where(lane == 0, first, jnp.where(lane == 1, second, 0.0)).astype(BF16)
        for p in range(3):
            k_ext[p, 128 * k : 128 * k + 128, 128:256] = key_side
        if k < 4:
            query_side = (
                jnp.where(lane == 0, second, jnp.where(lane == 1, first, 0.0)) * (-BIG)
            ).astype(BF16)
            for h in range(6):
                q_ext[h, 128 * k : 128 * k + 128, 128:256] = query_side

    shift_q = shifts[0:1, pl.ds(half, 384)]
    shift_v = shifts[1:2, pl.ds(half, 384)]
    low_lane = lax.broadcasted_iota(jnp.int32, (256, 128), 1) < 64

    def project(first, queries):
        to = slice(128 * first, 128 * first + 256)
        rows = tok[to, :]
        keys = dot(rows, w_all[:, 384:768])
        values = dot(rows, w_all[:, 768:1152]) + shift_v
        low_keys = keys.astype(BF16)
        low_values = values.astype(BF16)
        for p in range(3):
            k_ext[p, to, 0:128] = low_keys[:, 128 * p : 128 * p + 128]
            val[p, to, :] = low_values[:, 128 * p : 128 * p + 128]
        k_t[:, to] = keys.T.astype(BF16)
        v_t[:, to] = values.T.astype(BF16)
        if queries:
            query = dot(rows, w_all[:, 0:384]) + shift_q
            low_query = query.astype(BF16).astype(F32) * 0.125
            for h in range(6):
                p = h // 2
                mine = low_lane if h % 2 == 0 else jnp.logical_not(low_lane)
                masked = jnp.where(mine, low_query[:, 128 * p : 128 * p + 128], 0.0)
                q_ext[h, to, 0:128] = masked.astype(BF16)

    def attend(group_at, starts_at, first_query, count):
        queries = slice(first_query, first_query + count)
        peaks, totals, outs = {}, {}, {}

        def scores(h, at):
            part = dot_nt(k_ext[h // 2, at : at + 256, :], q_ext[h, queries, :])
            s_buf[h % 2, at : at + 256, queries] = part
            peak = jnp.max(part, axis=0, keepdims=True)
            peaks[h] = jnp.maximum(peaks[h], peak) if h in peaks else peak

        def weights(h, at):
            weight = jnp.exp(s_buf[h % 2, at : at + 256, queries] - peaks[h])
            total = jnp.sum(weight, axis=0, keepdims=True)
            low_weight = weight.astype(BF16)
            probs[h, at : at + 256, queries] = low_weight
            out = dot(v_t[64 * h : 64 * h + 64, at : at + 256], low_weight)
            totals[h] = totals[h] + total if h in totals else total
            outs[h] = outs[h] + out if h in outs else out

        for at in starts_at:
            scores(0, at)
        for h in range(6):
            for at in starts_at:
                if h < 5:
                    scores(h + 1, at)
                weights(h, at)
            part_top[group_at, h, :, queries] = peaks[h]
            part_sum[group_at, h, :, queries] = totals[h]
            part_out[group_at, 64 * h : 64 * h + 64, queries] = outs[h]

    def combine(first_query, groups):
        queries = slice(first_query, first_query + 256)
        for h in range(6):
            rows_h = slice(64 * h, 64 * h + 64)
            tops = [part_top[g, h, :, queries] for g in groups]
            top = functools.reduce(jnp.maximum, tops)
            shares = [jnp.exp(one - top) for one in tops]
            total = functools.reduce(
                jnp.add, [w * part_sum[g, h, :, queries] for w, g in zip(shares, groups)]
            )
            inverse = 1.0 / total
            shares = [w * inverse for w in shares]
            att_t[rows_h, queries] = functools.reduce(
                jnp.add, [w * part_out[g, rows_h, queries] for w, g in zip(shares, groups)]
            )
            for w, g in zip(shares, groups):
                share[g, h, :, queries] = w
            if len(groups) == 2:
                share[PART_FAR, h, :, queries] = shares[0]

    loads[0].wait()
    send_sib.wait_recv()
    project(OWN, True)
    send_near.wait_recv()
    pass_near_sib.start()
    pass_near_sib.wait_recv()
    project(NEAR, False)
    attend(PART_OWN, (128 * OWN, 128 * NEAR), 0, 256)
    for k in range(PIECES):
        send_far[k].wait_recv()
        pass_far_near[k].start()
    pass_far_sib.start()
    pass_far_sib.wait_recv()
    project(FAR, True)
    attend(PART_FAR, (128 * FAR,), 0, 256)
    attend(PART_OWN, (128 * OWN, 128 * NEAR, 128 * FAR), 256, 256)
    for k in range(PIECES):
        pass_far_near[k].wait_recv()
        pass_last[k].start()
    send_og.start()
    for k in range(PIECES):
        pass_last[k].wait_recv()
    project(NEAR_FAR, False)
    attend(PART_LAST, (128 * NEAR_FAR,), 0, 512)
    combine(0, (PART_OWN, PART_FAR, PART_LAST))
    combine(256, (PART_OWN, PART_LAST))

    swap_att = remote(17, att_send, att_recv, to_sib)
    for k, at in ((0, 128 * SIB), (128, 128 * SIB_FAR)):
        att_send[k : k + 128, :] = att_t[:, at : at + 128].T.astype(BF16)
    swap_att.start()

    def norm(values_in):
        centered = values_in - jnp.mean(values_in, axis=-1, keepdims=True)
        inverse = lax.rsqrt(jnp.mean(centered * centered, axis=-1, keepdims=True) + 1e-05)
        return centered * inverse, inverse

    def norm_back(grad_in, normed, inverse, gain_row):
        scaled = grad_in * gain_row
        return inverse * (
            scaled
            - jnp.mean(scaled, axis=-1, keepdims=True)
            - normed * jnp.mean(scaled * normed, axis=-1, keepdims=True)
        )

    loads[6].wait()
    attended_mine = jnp.concatenate([att_t[:, 0:128], att_t[:, 256:384]], axis=1).T
    token_rows = jnp.concatenate([tok[0:128, :], tok[256:384, :]], axis=0).astype(F32)
    branch = dot(attended_mine.astype(BF16), w_out[pl.ds(half, 384), :])
    swap_att.wait_recv()
    branch = branch + dot(att_recv[...], w_out[pl.ds(other_half, 384), :]) + shifts[2:3, :]
    normed_one, inverse_one = norm(token_rows + branch)
    n_one[...] = normed_one
    hidden = normed_one * gains[0:1, :] + shifts[4:5, :]
    hid[...] = hidden
    low_rows[...] = hidden.astype(BF16)

    loads[7].wait()
    loads[8].wait()
    for t in range(0, 3072, 512):
        cols = slice(t, t + 512)
        inner = dot(low_rows[...], w_one[:, cols]) + ffn_bias[:, cols]
        phi = 0.5 * (1.0 + lax.erf(inner * 0.7071067811865476))
        density = 0.3989422804014327 * jnp.exp(-0.5 * inner * inner)
        gprime[:, cols] = phi + inner * density
        wide[:, cols] = (inner * phi).astype(BF16)
    ffn_branch = dot(wide[...], w_two[...])
    normed_two, inverse_two = norm(hid[...] + ffn_branch + shifts[3:4, :])
    lo_buf[...] = (normed_two * gains[1:2, :] + shifts[5:6, :]).astype(BF16)
    send_lo = remote(18, lo_buf.at[pl.ds(128, 128)], layer_out.at[group], to_far)
    keep_lo = local(10, lo_buf.at[pl.ds(0, 128)], layer_out.at[group])
    send_lo.start()
    keep_lo.start()
    loads[9].wait()
    send_og.wait_recv()
    grad_two = norm_back(og[...].astype(F32), normed_two, inverse_two, gains[1:2, :])
    g_two[...] = grad_two
    low_rows[...] = grad_two.astype(BF16)
    for t in range(0, 3072, 512):
        cols = slice(t, t + 512)
        grad_act = dot_nt(low_rows[...], w_two[cols, :])
        wide[:, cols] = (grad_act * gprime[:, cols]).astype(BF16)
    grad_hidden = g_two[...] + dot_nt(wide[...], w_one[...])
    grad_one = norm_back(grad_hidden, n_one[...], inverse_one, gains[0:1, :])
    g_one[...] = grad_one
    low_one = grad_one.astype(BF16)
    swap_ga = remote(19, ga_send, ga_recv, to_sib)
    ga_send[...] = dot_nt(low_one, w_out[pl.ds(other_half, 384), :]).astype(BF16)
    swap_ga.start()
    ga_mine[...] = dot_nt(low_one, w_out[pl.ds(half, 384), :]).astype(BF16)

    low_row = lax.broadcasted_iota(jnp.int32, (128, 128), 0) < 64
    low_col = lax.broadcasted_iota(jnp.int32, (128, 128), 1) < 64

    def spread(block_at, rows):
        to = slice(128 * block_at, 128 * block_at + 128)
        flipped = rows.T
        for p in range(3):
            cols = slice(128 * p, 128 * p + 128)
            for e in range(2):
                h = 2 * p + e
                rows_of = low_row if e == 0 else jnp.logical_not(low_row)
                cols_of = low_col if e == 0 else jnp.logical_not(low_col)
                go_m[h, to, :] = jnp.where(cols_of, rows[:, cols], 0.0).astype(BF16)
                mine = jnp.where(rows_of, flipped[cols, :], 0.0)
                go_t[h, :, to] = mine.astype(BF16)
                delta[h, :, to] = jnp.sum(mine * att_t[cols, to], axis=0, keepdims=True)

    spread(OWN, ga_mine[0:128, :].astype(F32))
    spread(FAR, ga_mine[128:256, :].astype(F32))
    swap_ga.wait_recv()
    spread(SIB, ga_recv[0:128, :].astype(F32))
    spread(SIB_FAR, ga_recv[128:256, :].astype(F32))

    def backward(first, group_at, from_head, to_head):
        rows = slice(128 * first, 128 * first + 256)

        def value_dots(h):
            return dot(val[h // 2, rows, :], go_t[h])

        grad_prob = value_dots(from_head)
        for h in range(from_head, to_head):
            following = value_dots(h + 1) if h + 1 < to_head else None
            weight = probs[h, rows, :].astype(F32) * share[group_at, h]
            grad_score = (weight * (grad_prob - delta[h])).astype(BF16)
            value_part = dot(weight.astype(BF16), go_m[h])
            key_part = dot(grad_score, q_ext[h, :, 0:128])
            rows_h = slice(64 * h, 64 * h + 64)
            query_part = dot(k_t[rows_h, rows], grad_score)
            if first == NEAR_FAR:
                dq_t[rows_h, :] = query_part
            else:
                dq_t[rows_h, :] += query_part
            if h % 2 == 0:
                grad_values, grad_keys = value_part, key_part
            else:
                cols = slice(64 * h - 64, 64 * h + 64)
                value_cols = slice(64 * h + 320, 64 * h + 448)
                d_kv[rows, cols] = (grad_keys + key_part).astype(BF16)
                d_kv[rows, value_cols] = (grad_values + value_part).astype(BF16)
            grad_prob = following

    def token_terms(start):
        return dot_nt(d_kv[start : start + 256, :], w_all[:, 384:1152])

    swap_parts = [
        remote(20 + k, part_send.at[pl.ds(128 * k, 128)], part_recv.at[pl.ds(128 * k, 128)], to_sib)
        for k in range(4)
    ]
    send_parts = [
        remote(24 + k, tn_send.at[pl.ds(128 * k, 128)], tn_recv.at[pl.ds(128 * k, 128)], to_near)
        for k in range(2)
    ]

    def share_out(k, terms):
        part_send[128 * k : 128 * k + 128, :] = terms[128:256].astype(BF16)
        swap_parts[k].start()
        part_mine[128 * k : 128 * k + 128, :] = terms[0:128]

    def shared(k):
        swap_parts[k].wait_recv()
        rows = slice(128 * k, 128 * k + 128)
        return part_mine[rows, :] + part_recv[rows, :].astype(F32)

    def pass_on(k):
        tn_send[128 * k : 128 * k + 128, :] = shared(k).astype(BF16)
        send_parts[k].start()

    backward(NEAR_FAR, PART_LAST, 0, 6)
    share_out(0, token_terms(128 * NEAR_FAR))
    backward(NEAR, PART_OWN, 0, 2)
    pass_on(0)
    backward(NEAR, PART_OWN, 2, 6)
    share_out(1, token_terms(128 * NEAR))
    backward(FAR, PART_FAR, 0, 2)
    pass_on(1)
    backward(FAR, PART_FAR, 2, 6)
    far_terms[...] = token_terms(128 * FAR)
    backward(OWN, PART_OWN, 0, 6)

    low_dq = (dq_t[...] * 0.125).T.astype(BF16)
    share_out(2, far_terms[...] + dot_nt(low_dq[256:512, :], w_all[:, 0:384]))
    far_part = shared(2) + g_one[128:256, :]
    send_parts[0].wait_recv()
    ig_buf[128:256, :] = (far_part + tn_recv[0:128, :].astype(F32)).astype(BF16)
    send_ig = remote(26, ig_buf.at[pl.ds(128, 128)], in_grad.at[group], to_far)
    keep_ig = local(11, ig_buf.at[pl.ds(0, 128)], in_grad.at[group])
    send_ig.start()

    low_dq_t = (dq_t[...] * 0.125).astype(BF16)
    grad_q_map = dot(low_dq_t, tok[0:512, :]).astype(BF16)
    grad_v_map = dot(d_kv[:, 384:768].astype(F32).T.astype(BF16), tok[...]).astype(BF16)
    sum_buf[0:8, :] = jnp.zeros((8, 1024), F32)
    for row, grad_map in ((0, grad_q_map), (1, grad_v_map)):
        product_map = dot(grad_map, v_in[...]) * v_out_t[...].astype(F32)
        out_row = out_scale[pl.ds(row, 1), pl.ds(half, 384)]
        out_col = jnp.broadcast_to(out_row, (128, 384)).T[:, 0:1]
        sum_buf[row : row + 1, :] = jnp.sum(product_map * out_col, axis=0, keepdims=True)
        out_part = jnp.sum(product_map * rank_scale[pl.ds(row, 1), :], axis=1, keepdims=True)
        out_part_row = jnp.broadcast_to(out_part, (384, 128)).T[0:1, :]
        sum_buf[2 + row : 3 + row, pl.ds(half, 384)] = out_part_row

    def exchange(k, stage, wheres):
        swaps = [
            remote(
                k + n,
                sum_buf.at[pl.ds(8 * stage, 8)],
                sum_recv.at[pl.ds(8 * (k - 27 + n), 8)],
                where,
            )
            for n, where in enumerate(wheres)
        ]
        for swap in swaps:
            swap.start()
        return swaps

    def received(k):
        return sum_recv[8 * k : 8 * k + 8, :]

    core_swaps = exchange(27, 0, (to_sib,))
    share_out(3, token_terms(128 * OWN) + dot_nt(low_dq[0:256, :], w_all[:, 0:384]))
    core_swaps[0].wait_recv()
    sum_buf[8:16, :] = sum_buf[0:8, :] + received(0)
    plane_swaps = exchange(28, 1, (to_bx, to_by, to_bxy))
    own_part = shared(3) + g_one[0:128, :]
    send_parts[1].wait_recv()
    ig_buf[0:128, :] = (own_part + tn_recv[128:256, :].astype(F32)).astype(BF16)
    keep_ig.start()
    for swap in plane_swaps:
        swap.wait_recv()
    sum_buf[16:24, :] = (sum_buf[8:16, :] + received(1)) + (received(2) + received(3))
    line_swaps = exchange(31, 2, (to_near, to_far, to_near_far))
    for swap in line_swaps:
        swap.wait_recv()
    sums[...] = (sum_buf[16:24, :] + received(4)) + (received(5) + received(6))

    send_lo.wait_recv()
    send_ig.wait_recv()
    keep_lo.wait()
    keep_ig.wait()
    for item in (
        *send_far,
        *pass_far_near,
        *pass_last,
        send_near,
        send_sib,
        pass_far_sib,
        pass_near_sib,
        send_og,
        swap_att,
        swap_ga,
        send_lo,
        *swap_parts,
        *send_parts,
        send_ig,
        *core_swaps,
        *plane_swaps,
        *line_swaps,
    ):
        item.wait_send()


def finish_kernel(layer_in, grad_in, sums, layer_out, in_grad, rank_total, out_total, norms):
    layer_out[...] = layer_in[...]
    in_grad[...] = grad_in[...]
    rank_total[...] = sums[0:2, :]
    out_total[...] = sums[2:4, 0:768]
    totals = sums[0:4, :]
    lengths = jnp.sqrt(jnp.sum(totals * totals, axis=1, keepdims=True))
    for k in range(4):
        norms[k] = lengths[k, 0]


def fast_body(
    tokens,
    attn_in_weight,
    out_weight,
    ffn_in_weight,
    ffn_out_weight,
    vera_in,
    vera_out,
    rank_scale,
    out_scale,
    gains,
    shifts,
    ffn_bias,
    splits,
    out_grad,
):
    hbm = pl.BlockSpec(memory_space=pl.ANY)
    vmem = pl.BlockSpec(memory_space=pltpu.VMEM)
    smem = pl.BlockSpec(memory_space=pltpu.SMEM)
    shape = tokens.shape
    scratch = [
        ((1024, 768), BF16),
        ((256, 768), BF16),
        ((768, 1152), BF16),
        ((768, 768), BF16),
        ((768, 3072), BF16),
        ((3072, 768), BF16),
        ((768, 1024), BF16),
        ((1024, 384), BF16),
        ((384, 1024), BF16),
        ((3, 1024, 256), BF16),
        ((6, 512, 256), BF16),
        ((3, 1024, 128), BF16),
        ((384, 1024), BF16),
        ((384, 1024), BF16),
        ((6, 1024, 512), BF16),
        ((2, 1024, 512), F32),
        ((384, 512), F32),
        ((3, 6, 1, 512), F32),
        ((3, 6, 1, 512), F32),
        ((3, 384, 512), F32),
        ((3, 6, 1, 512), F32),
        ((256, 384), BF16),
        ((256, 384), BF16),
        ((256, 768), F32),
        ((256, 768), F32),
        ((256, 3072), BF16),
        ((256, 3072), F32),
        ((256, 768), BF16),
        ((256, 768), F32),
        ((256, 768), F32),
        ((256, 768), BF16),
        ((256, 384), BF16),
        ((256, 384), BF16),
        ((256, 384), BF16),
        ((6, 128, 512), BF16),
        ((6, 512, 128), BF16),
        ((6, 1, 512), F32),
        ((1024, 768), BF16),
        ((384, 512), F32),
        ((512, 768), BF16),
        ((512, 768), BF16),
        ((512, 768), F32),
        ((256, 768), F32),
        ((256, 768), BF16),
        ((256, 768), BF16),
        ((256, 768), BF16),
        ((24, 1024), F32),
        ((56, 1024), F32),
    ]
    rows_type = jax.ShapeDtypeStruct(shape, BF16)
    layer_rows, grad_rows, sums = pl.pallas_call(
        layer_kernel,
        out_shape=(rows_type, rows_type, jax.ShapeDtypeStruct((8, 1024), F32)),
        in_specs=[hbm] * 8 + [vmem] * 5 + [smem],
        out_specs=(hbm, hbm, vmem),
        scratch_shapes=[pltpu.VMEM(dims, kind) for dims, kind in scratch]
        + [
            pltpu.SemaphoreType.DMA((34,)),
            pltpu.SemaphoreType.DMA((34,)),
            pltpu.SemaphoreType.DMA((12,)),
        ],
        compiler_params=pltpu.CompilerParams(
            collective_id=0, has_side_effects=True, vmem_limit_bytes=60 * 2**20
        ),
        name="encoder_layer",
    )(
        tokens,
        attn_in_weight,
        out_weight,
        ffn_in_weight,
        ffn_out_weight,
        vera_in,
        vera_out,
        out_grad,
        rank_scale,
        out_scale,
        gains,
        shifts,
        ffn_bias.reshape(1, -1),
        splits,
    )
    return pl.pallas_call(
        finish_kernel,
        out_shape=(
            rows_type,
            rows_type,
            jax.ShapeDtypeStruct(rank_scale.shape, F32),
            jax.ShapeDtypeStruct(out_scale.shape, F32),
            jax.ShapeDtypeStruct((4,), F32),
        ),
        in_specs=[vmem, vmem, vmem],
        out_specs=(vmem, vmem, vmem, vmem, smem),
        name="finish",
    )(layer_rows, grad_rows, sums)


def solution(mesh):
    chosen = fast_body if fits(mesh) else body
    in_specs = (
        P("batch", "seq", None),
        P(),
        P(),
        P(),
        P(),
        P(),
        P(),
        P(),
        P(),
        P(),
        P(),
        P(),
        P("batch"),
        P("batch", "seq", None),
    )
    out_specs = (P("batch", "seq", None), P("batch", "seq", None), P(), P(), P())
    return jax.shard_map(chosen, mesh=mesh, in_specs=in_specs, out_specs=out_specs, check_vma=False)
```

```python
import functools

import jax
import jax.numpy as jnp
from jax import lax
from jax.experimental import pallas as pl
from jax.experimental.pallas import tpu as pltpu
from jax.sharding import PartitionSpec as P

HEADS = 12


masked_score = -1e30
key_block = 512


def product(left_side, right_side):
    return jnp.dot(left_side, right_side, preferred_element_type=jnp.float32)


def product_t(left_side, right_side):
    return lax.dot_general(
        left_side, right_side, (((1,), (1,)), ((), ())), preferred_element_type=jnp.float32
    )


def gelu_exact(inputs):
    return jax.nn.gelu(inputs, approximate=False)


def norm_forward(values_in, gain_row, shift_row):
    centered = values_in - jnp.mean(values_in, axis=-1, keepdims=True)
    inverse = lax.rsqrt(jnp.mean(centered * centered, axis=-1, keepdims=True) + 1e-05)
    normed = centered * inverse
    return (normed * gain_row + shift_row, normed, inverse)


def norm_backward(grad_in, normed, inverse, gain_row):
    scaled = grad_in * gain_row
    return inverse * (
        scaled
        - jnp.mean(scaled, axis=-1, keepdims=True)
        - normed * jnp.mean(scaled * normed, axis=-1, keepdims=True)
    )


def block_width():
    return key_block


def body(
    tokens,
    attn_in_weight,
    out_weight,
    ffn_in_weight,
    ffn_out_weight,
    vera_in,
    vera_out,
    rank_scale,
    out_scale,
    gains,
    shifts,
    ffn_bias,
    splits,
    out_grad,
):
    sequences, per_device, model_width = tokens.shape
    head_dim = model_width // HEADS
    score_scale = head_dim ** (-0.5)
    cycle_place = lax.axis_index("seq")
    token_rows = tokens.reshape(-1, model_width)
    token_float = token_rows.astype(jnp.float32)
    rank_in = product(token_rows, vera_in)
    rank_q = (rank_in * rank_scale[0]).astype(jnp.bfloat16)
    rank_v = (rank_in * rank_scale[1]).astype(jnp.bfloat16)
    wide_q = product(rank_q, vera_out)
    wide_v = product(rank_v, vera_out)
    projected = product(token_rows, attn_in_weight)
    query = projected[:, :model_width] + shifts[0] + out_scale[0] * wide_q
    keys = projected[:, model_width : 2 * model_width]
    values = projected[:, 2 * model_width :] + shifts[1] + out_scale[1] * wide_v
    query_low = query.astype(jnp.bfloat16).reshape(sequences, per_device, HEADS, head_dim)
    pair_low = (
        jnp.concatenate([keys, values], axis=-1)
        .astype(jnp.bfloat16)
        .reshape(sequences, per_device, 2 * model_width)
    )
    query_pos = cycle_place * per_device + jnp.arange(per_device, dtype=jnp.int32)
    query_side = query_pos[None, :] < splits[:, None]

    def block_scores(pair_piece, block_start):
        count_keys = pair_piece.shape[1]
        key_pos = block_start + jnp.arange(count_keys, dtype=jnp.int32)
        key_side = key_pos[None, :] < splits[:, None]
        allowed = (query_side[:, :, None] == key_side[:, None, :])[:, None]
        key_heads = pair_piece[:, :, :model_width].reshape(sequences, count_keys, HEADS, head_dim)
        value_heads = pair_piece[:, :, model_width:].reshape(sequences, count_keys, HEADS, head_dim)
        raw_scores = (
            jnp.einsum("sqhe,skhe->shqk", query_low, key_heads, preferred_element_type=jnp.float32)
            * score_scale
        )
        return (raw_scores, allowed, key_heads, value_heads)

    start_max = jnp.full((sequences, HEADS, per_device), masked_score, jnp.float32)
    start_sum = jnp.zeros((sequences, HEADS, per_device), jnp.float32)
    start_acc = jnp.zeros((sequences, per_device, HEADS, head_dim), jnp.float32)
    carry = (start_max, start_sum, start_acc)
    pair_piece = lax.all_gather(pair_low, "seq", axis=1, tiled=True)
    shard_start = jnp.int32(0)
    count_keys = pair_piece.shape[1]
    block_size = block_width()
    for absorb_block_index in range(count_keys // block_size):
        absorb_pair_piece = pair_piece[
            :, absorb_block_index * block_size : (absorb_block_index + 1) * block_size
        ]
        running_max, running_sum, absorb_accumulated = carry
        absorb_raw_scores, absorb_allowed, absorb_key_heads, absorb_value_heads = block_scores(
            absorb_pair_piece, shard_start + absorb_block_index * block_size
        )
        new_max = jnp.maximum(
            running_max,
            jnp.max(jnp.where(absorb_allowed, absorb_raw_scores, masked_score), axis=-1),
        )
        block_weights = jnp.where(
            absorb_allowed, jnp.exp(absorb_raw_scores - new_max[..., None]), 0.0
        )
        rescale = jnp.exp(running_max - new_max)
        running_sum = running_sum * rescale + jnp.sum(block_weights, axis=-1)
        added = jnp.einsum(
            "shqk,skhe->sqhe",
            block_weights.astype(jnp.bfloat16),
            absorb_value_heads,
            preferred_element_type=jnp.float32,
        )
        absorb_accumulated = (
            absorb_accumulated * jnp.transpose(rescale, (0, 2, 1))[..., None] + added
        )
        carry = (new_max, running_sum, absorb_accumulated)
    final_max, final_sum, accumulated = carry
    attended = accumulated / jnp.transpose(final_sum, (0, 2, 1))[..., None]
    log_total = final_max + jnp.log(final_sum)
    branch = product(attended.reshape(-1, model_width).astype(jnp.bfloat16), out_weight) + shifts[2]
    hidden, normed_one, inverse_one = norm_forward(token_float + branch, gains[0], shifts[4])
    inner = product(hidden.astype(jnp.bfloat16), ffn_in_weight) + ffn_bias
    activated, gelu_pull = jax.vjp(gelu_exact, inner)
    ffn_branch = product(activated.astype(jnp.bfloat16), ffn_out_weight) + shifts[3]
    layer_out, normed_two, inverse_two = norm_forward(hidden + ffn_branch, gains[1], shifts[5])
    grad_two = norm_backward(
        out_grad.reshape(-1, model_width).astype(jnp.float32), normed_two, inverse_two, gains[1]
    )
    grad_act = product_t(grad_two.astype(jnp.bfloat16), ffn_out_weight)
    grad_inner = gelu_pull(grad_act)[0].astype(jnp.bfloat16)
    grad_hidden = grad_two + product_t(grad_inner, ffn_in_weight)
    grad_one = norm_backward(grad_hidden, normed_one, inverse_one, gains[0])
    grad_att = (
        product_t(grad_one.astype(jnp.bfloat16), out_weight)
        .astype(jnp.bfloat16)
        .reshape(sequences, per_device, HEADS, head_dim)
    )
    delta = jnp.transpose(jnp.sum(grad_att.astype(jnp.float32) * attended, axis=-1), (0, 2, 1))
    grad_query = jnp.zeros((sequences, per_device, HEADS, head_dim), jnp.float32)
    whole_pairs = lax.all_gather(pair_low, "seq", axis=1, tiled=True)
    whole_len = whole_pairs.shape[1]
    block_size = block_width()
    key_terms = []
    for block_index in range(whole_len // block_size):
        block_pair_piece = whole_pairs[:, block_index * block_size : (block_index + 1) * block_size]
        block_raw_scores, block_allowed, block_key_heads, block_value_heads = block_scores(
            block_pair_piece, block_index * block_size
        )
        prob = jnp.where(block_allowed, jnp.exp(block_raw_scores - log_total[..., None]), 0.0)
        grad_prob = jnp.einsum(
            "sqhe,skhe->shqk", grad_att, block_value_heads, preferred_element_type=jnp.float32
        )
        grad_score = (prob * (grad_prob - delta[..., None])).astype(jnp.bfloat16)
        grad_value = jnp.einsum(
            "shqk,sqhe->skhe",
            prob.astype(jnp.bfloat16),
            grad_att,
            preferred_element_type=jnp.float32,
        )
        grad_key = (
            jnp.einsum("shqk,sqhe->skhe", grad_score, query_low, preferred_element_type=jnp.float32)
            * score_scale
        )
        query_part = (
            jnp.einsum(
                "shqk,skhe->sqhe", grad_score, block_key_heads, preferred_element_type=jnp.float32
            )
            * score_scale
        )
        block_count_keys = block_pair_piece.shape[1]
        pair_part = jnp.concatenate(
            [
                grad_key.reshape(sequences, block_count_keys, model_width),
                grad_value.reshape(sequences, block_count_keys, model_width),
            ],
            axis=-1,
        )
        query_part, pair_part = (query_part, pair_part)
        grad_query = grad_query + query_part
        key_terms.append(pair_part)
    pair_sum = lax.psum_scatter(
        jnp.concatenate(key_terms, axis=1), "seq", scatter_dimension=1, tiled=True
    )
    pair_grad_low = pair_sum.astype(jnp.bfloat16).reshape(-1, 2 * model_width)
    query_grad_low = grad_query.reshape(-1, model_width).astype(jnp.bfloat16)
    query_grad_float = query_grad_low.astype(jnp.float32)
    value_grad_float = pair_grad_low[:, model_width:].astype(jnp.float32)
    grad_wide_q = (query_grad_float * out_scale[0]).astype(jnp.bfloat16)
    grad_wide_v = (value_grad_float * out_scale[1]).astype(jnp.bfloat16)
    grad_rank_q = product_t(grad_wide_q, vera_out)
    grad_rank_v = product_t(grad_wide_v, vera_out)
    grad_rank_in = (grad_rank_q * rank_scale[0] + grad_rank_v * rank_scale[1]).astype(jnp.bfloat16)
    grad_tokens = (
        grad_one
        + product_t(jnp.concatenate([query_grad_low, pair_grad_low], axis=-1), attn_in_weight)
        + product_t(grad_rank_in, vera_in)
    )
    rank_terms = jnp.stack(
        [jnp.sum(grad_rank_q * rank_in, axis=0), jnp.sum(grad_rank_v * rank_in, axis=0)]
    )
    out_terms = jnp.stack(
        [jnp.sum(query_grad_float * wide_q, axis=0), jnp.sum(value_grad_float * wide_v, axis=0)]
    )
    rank_total, out_total = lax.psum((rank_terms, out_terms), ("batch", "seq"))
    scale_norms = jnp.concatenate(
        [
            jnp.sqrt(jnp.sum(rank_total * rank_total, axis=1)),
            jnp.sqrt(jnp.sum(out_total * out_total, axis=1)),
        ]
    )
    return (
        layer_out.astype(jnp.bfloat16).reshape(sequences, per_device, model_width),
        grad_tokens.astype(jnp.bfloat16).reshape(sequences, per_device, model_width),
        rank_total,
        out_total,
        scale_norms,
    )


MESH = pl.DeviceIdType.MESH
BIG = 1e30
F32 = jnp.float32
BF16 = jnp.bfloat16


def fits(mesh):
    return mesh.shape["seq"] == 8 and mesh.shape["batch"] == 4


def dot(left, right):
    return lax.dot_general(left, right, (((1,), (0,)), ((), ())), preferred_element_type=F32)


def dot_nt(left, right):
    return lax.dot_general(left, right, (((1,), (1,)), ((), ())), preferred_element_type=F32)


OWN, SIB, FAR, SIB_FAR, NEAR_FAR, SIB_NEAR_FAR, NEAR, SIB_NEAR = range(8)
PIECES = 2
PART_OWN, PART_FAR, PART_LAST = range(3)


def layer_kernel(
    tokens,
    attn_in,
    out_w,
    ffn_in,
    ffn_out,
    vera_in,
    vera_out,
    out_grad,
    rank_scale_in,
    out_scale_in,
    gains_in,
    shifts_in,
    ffn_bias_in,
    splits_in,
    layer_out,
    in_grad,
    sums,
    rank_scale,
    out_scale,
    gains,
    shifts,
    ffn_bias,
    splits,
    tok,
    og,
    w_all,
    w_out,
    w_one,
    w_two,
    v_in,
    v_out,
    v_out_t,
    rank_in,
    k_ext,
    q_ext,
    val,
    k_t,
    v_t,
    probs,
    s_buf,
    att_t,
    part_top,
    part_sum,
    part_out,
    share,
    att_send,
    att_recv,
    hid,
    n_one,
    wide,
    gprime,
    low_rows,
    g_two,
    g_one,
    lo_buf,
    ga_send,
    ga_recv,
    ga_mine,
    go_t,
    go_m,
    delta,
    d_kv,
    d_held,
    dq_t,
    part_send,
    part_recv,
    part_mine,
    far_terms,
    tn_send,
    tn_recv,
    ig_buf,
    sum_buf,
    sum_recv,
    send_sem,
    recv_sem,
    load_sem,
):
    s = lax.axis_index("seq")
    b = lax.axis_index("batch")
    core = s % 2
    group = s // 4
    sib = s + 1 - 2 * core
    near = s + 2 - 4 * ((s // 2) % 2)
    far = s + 4 - 8 * group
    bx = b + 1 - 2 * (b % 2)
    by = b + 2 - 4 * (b // 2)
    half = pl.multiple_of(core * 384, 384)
    other_half = pl.multiple_of(384 - core * 384, 384)

    def remote(k, src, dst, where):
        return pltpu.make_async_remote_copy(
            src_ref=src,
            dst_ref=dst,
            send_sem=send_sem.at[k],
            recv_sem=recv_sem.at[k],
            device_id=where,
            device_id_type=MESH,
        )

    def local(k, src, dst):
        return pltpu.make_async_copy(src, dst, load_sem.at[k])

    def block(ref, k, n=1):
        return ref.at[pl.ds(128 * k, 128 * n)]

    near_far = far + near - s
    to_sib, to_near, to_far = {"seq": sib}, {"seq": near}, {"seq": far}
    to_near_far = {"seq": near_far}
    to_bx, to_by, to_bxy = {"batch": bx}, {"batch": by}, {"batch": bx + by - b}

    barrier = pltpu.get_barrier_semaphore()
    for where in (to_sib, to_near, to_far, to_near_far, to_bx, to_by, to_bxy):
        pl.semaphore_signal(barrier, inc=1, device_id=where, device_id_type=MESH)

    loads = [
        local(0, tokens.at[group], block(tok, OWN)),
        local(1, vera_in, v_in),
        local(2, vera_out.at[:, pl.ds(half, 384)], v_out),
        local(3, attn_in.at[:, pl.ds(half, 384)], w_all.at[:, pl.ds(0, 384)]),
        local(4, attn_in.at[:, pl.ds(768 + half, 384)], w_all.at[:, pl.ds(384, 384)]),
        local(5, attn_in.at[:, pl.ds(1536 + half, 384)], w_all.at[:, pl.ds(768, 384)]),
        local(6, out_w, w_out),
        local(7, ffn_in, w_one),
        local(8, ffn_out, w_two),
        local(9, out_grad.at[group], og.at[pl.ds(0, 128)]),
    ]
    small_loads = [
        local(12, rank_scale_in, rank_scale),
        local(13, out_scale_in, out_scale),
        local(14, gains_in, gains),
        local(15, shifts_in, shifts),
        local(16, ffn_bias_in, ffn_bias),
        local(17, splits_in, splits),
    ]
    for item in (*small_loads, *loads):
        item.start()
    pl.semaphore_wait(barrier, 7)

    piece = 128 // PIECES
    send_far, pass_far_near, pass_last = [], [], []
    for k in range(PIECES):
        part = pl.ds(128 * FAR + piece * k, piece)
        near_part = pl.ds(128 * NEAR_FAR + piece * k, piece)
        last_part = pl.ds(128 * SIB_NEAR_FAR + piece * k, piece)
        send_far.append(
            remote(k, tokens.at[1 - group, pl.ds(piece * k, piece)], tok.at[part], to_far)
        )
        pass_far_near.append(remote(PIECES + k, tok.at[part], tok.at[near_part], to_near))
        pass_last.append(remote(2 * PIECES + k, tok.at[near_part], tok.at[last_part], to_sib))
    send_near = remote(12, tokens.at[group], block(tok, NEAR), to_near)
    send_sib = remote(13, tokens.at[group], block(tok, SIB), to_sib)
    pass_far_sib = remote(14, block(tok, FAR), block(tok, SIB_FAR), to_sib)
    pass_near_sib = remote(15, block(tok, NEAR), block(tok, SIB_NEAR), to_sib)
    send_og = remote(16, out_grad.at[1 - group], og.at[pl.ds(128, 128)], to_far)
    send_near.start()
    send_sib.start()
    for item in send_far:
        item.start()

    for item in (*small_loads, *loads[1:6]):
        item.wait()
    for row, at in ((0, 0), (1, 768)):
        scale_row = rank_scale[pl.ds(row, 1), :]
        out_row = out_scale[pl.ds(row, 1), pl.ds(half, 384)]

        def effective(t, _, at=at, scale_row=scale_row, out_row=out_row):
            rows = pl.ds(pl.multiple_of(t * 256, 256), 256)
            scaled = (v_in[rows, :].astype(F32) * scale_row).astype(BF16)
            wide = dot(scaled, v_out[...]) * out_row
            w_all[rows, at : at + 384] = (w_all[rows, at : at + 384].astype(F32) + wide).astype(BF16)
            return 0

        lax.fori_loop(0, 3, effective, 0)
    v_out_t[...] = v_out[...].astype(F32).T.astype(BF16)

    split = splits[group]
    lane = lax.broadcasted_iota(jnp.int32, (128, 128), 1)
    row_at = lax.broadcasted_iota(jnp.int32, (128, 128), 0)
    flip_one, flip_two, flip_four = sib - s, near - s, far - s
    starts = (
        s,
        s + flip_one,
        s + flip_four,
        s + flip_four + flip_one,
        s + flip_two + flip_four,
        s + flip_two + flip_four + flip_one,
        s + flip_two,
        s + flip_two + flip_one,
    )
    for k in range(8):
        first = (starts[k] * 128 + row_at < split).astype(F32)
        second = 1.0 - first
        key_side = jnp.where(lane == 0, first, jnp.where(lane == 1, second, 0.0)).astype(BF16)
        for p in range(3):
            k_ext[p, 128 * k : 128 * k + 128, 128:256] = key_side
        if k < 4:
            query_side = (
                jnp.where(lane == 0, second, jnp.where(lane == 1, first, 0.0)) * (-BIG)
            ).astype(BF16)
            for h in range(6):
                q_ext[h, 128 * k : 128 * k + 128, 128:256] = query_side

    shift_q = shifts[0:1, pl.ds(half, 384)]
    shift_v = shifts[1:2, pl.ds(half, 384)]
    low_lane = lax.broadcasted_iota(jnp.int32, (256, 128), 1) < 64

    def project(first, queries):
        to = slice(128 * first, 128 * first + 256)
        rows = tok[to, :]
        keys = dot(rows, w_all[:, 384:768])
        values = dot(rows, w_all[:, 768:1152]) + shift_v
        low_keys = keys.astype(BF16)
        low_values = values.astype(BF16)
        for p in range(3):
            k_ext[p, to, 0:128] = low_keys[:, 128 * p : 128 * p + 128]
            val[p, to, :] = low_values[:, 128 * p : 128 * p + 128]
        k_t[:, to] = keys.T.astype(BF16)
        v_t[:, to] = values.T.astype(BF16)
        if queries:
            query = dot(rows, w_all[:, 0:384]) + shift_q
            low_query = query.astype(BF16).astype(F32) * 0.125
            for h in range(6):
                p = h // 2
                mine = low_lane if h % 2 == 0 else jnp.logical_not(low_lane)
                masked = jnp.where(mine, low_query[:, 128 * p : 128 * p + 128], 0.0)
                q_ext[h, to, 0:128] = masked.astype(BF16)

    def attend(group_at, starts_at, first_query, count):
        queries = slice(first_query, first_query + count)
        peaks, totals, outs = {}, {}, {}

        def scores(h, at):
            part = dot_nt(k_ext[h // 2, at : at + 256, :], q_ext[h, queries, :])
            s_buf[h % 2, at : at + 256, queries] = part
            peak = jnp.max(part, axis=0, keepdims=True)
            peaks[h] = jnp.maximum(peaks[h], peak) if h in peaks else peak

        def weights(h, at):
            weight = jnp.exp(s_buf[h % 2, at : at + 256, queries] - peaks[h])
            total = jnp.sum(weight, axis=0, keepdims=True)
            low_weight = weight.astype(BF16)
            probs[h, at : at + 256, queries] = low_weight
            out = dot(v_t[64 * h : 64 * h + 64, at : at + 256], low_weight)
            totals[h] = totals[h] + total if h in totals else total
            outs[h] = outs[h] + out if h in outs else out

        for at in starts_at:
            scores(0, at)
        for h in range(6):
            for at in starts_at:
                if h < 5:
                    scores(h + 1, at)
                weights(h, at)
            part_top[group_at, h, :, queries] = peaks[h]
            part_sum[group_at, h, :, queries] = totals[h]
            part_out[group_at, 64 * h : 64 * h + 64, queries] = outs[h]

    def combine(first_query, groups):
        queries = slice(first_query, first_query + 256)
        for h in range(6):
            rows_h = slice(64 * h, 64 * h + 64)
            tops = [part_top[g, h, :, queries] for g in groups]
            top = functools.reduce(jnp.maximum, tops)
            shares = [jnp.exp(one - top) for one in tops]
            total = functools.reduce(
                jnp.add, [w * part_sum[g, h, :, queries] for w, g in zip(shares, groups)]
            )
            inverse = 1.0 / total
            shares = [w * inverse for w in shares]
            att_t[rows_h, queries] = functools.reduce(
                jnp.add, [w * part_out[g, rows_h, queries] for w, g in zip(shares, groups)]
            )
            for w, g in zip(shares, groups):
                share[g, h, :, queries] = w
            if len(groups) == 2:
                share[PART_FAR, h, :, queries] = shares[0]

    def rank_rows(first):
        to = slice(128 * first, 128 * first + 256)
        rank_in[to, :] = dot(tok[to, :], v_in[...]).astype(BF16)

    loads[0].wait()
    send_sib.wait_recv()
    project(OWN, True)
    rank_rows(OWN)
    send_near.wait_recv()
    pass_near_sib.start()
    pass_near_sib.wait_recv()
    project(NEAR, False)
    rank_rows(NEAR)
    for k in range(PIECES):
        send_far[k].wait_recv()
        pass_far_near[k].start()
    pass_far_sib.start()
    attend(PART_OWN, (128 * OWN, 128 * NEAR), 0, 256)
    pass_far_sib.wait_recv()
    project(FAR, True)
    attend(PART_FAR, (128 * FAR,), 0, 256)
    attend(PART_OWN, (128 * OWN, 128 * NEAR, 128 * FAR), 256, 256)
    for k in range(PIECES):
        pass_far_near[k].wait_recv()
        pass_last[k].start()
    send_og.start()
    rank_rows(FAR)
    for k in range(PIECES):
        pass_last[k].wait_recv()
    project(NEAR_FAR, False)
    attend(PART_LAST, (128 * NEAR_FAR,), 0, 512)
    combine(0, (PART_OWN, PART_FAR, PART_LAST))
    combine(256, (PART_OWN, PART_LAST))

    swap_att = remote(17, att_send, att_recv, to_sib)
    for k, at in ((0, 128 * SIB), (128, 128 * SIB_FAR)):
        att_send[k : k + 128, :] = att_t[:, at : at + 128].T.astype(BF16)
    swap_att.start()

    def norm(values_in):
        centered = values_in - jnp.mean(values_in, axis=-1, keepdims=True)
        inverse = lax.rsqrt(jnp.mean(centered * centered, axis=-1, keepdims=True) + 1e-05)
        return centered * inverse, inverse

    def norm_back(grad_in, normed, inverse, gain_row):
        scaled = grad_in * gain_row
        return inverse * (
            scaled
            - jnp.mean(scaled, axis=-1, keepdims=True)
            - normed * jnp.mean(scaled * normed, axis=-1, keepdims=True)
        )

    loads[6].wait()
    attended_mine = jnp.concatenate([att_t[:, 0:128], att_t[:, 256:384]], axis=1).T
    token_rows = jnp.concatenate([tok[0:128, :], tok[256:384, :]], axis=0).astype(F32)
    branch = dot(attended_mine.astype(BF16), w_out[pl.ds(half, 384), :])
    rank_rows(NEAR_FAR)
    swap_att.wait_recv()
    branch = branch + dot(att_recv[...], w_out[pl.ds(other_half, 384), :]) + shifts[2:3, :]
    normed_one, inverse_one = norm(token_rows + branch)
    n_one[...] = normed_one
    hidden = normed_one * gains[0:1, :] + shifts[4:5, :]
    hid[...] = hidden
    low_rows[...] = hidden.astype(BF16)

    loads[7].wait()
    loads[8].wait()
    for t in range(0, 3072, 512):
        cols = slice(t, t + 512)
        inner = dot(low_rows[...], w_one[:, cols]) + ffn_bias[:, cols]
        phi = 0.5 * (1.0 + lax.erf(inner * 0.7071067811865476))
        density = 0.3989422804014327 * jnp.exp(-0.5 * inner * inner)
        gprime[:, cols] = phi + inner * density
        wide[:, cols] = (inner * phi).astype(BF16)
    ffn_branch = dot(wide[...], w_two[...])
    normed_two, inverse_two = norm(hid[...] + ffn_branch + shifts[3:4, :])
    lo_buf[...] = (normed_two * gains[1:2, :] + shifts[5:6, :]).astype(BF16)
    send_lo = remote(18, lo_buf.at[pl.ds(128, 128)], layer_out.at[group], to_far)
    keep_lo = local(10, lo_buf.at[pl.ds(0, 128)], layer_out.at[group])
    send_lo.start()
    keep_lo.start()
    loads[9].wait()
    send_og.wait_recv()
    grad_two = norm_back(og[...].astype(F32), normed_two, inverse_two, gains[1:2, :])
    g_two[...] = grad_two
    low_rows[...] = grad_two.astype(BF16)
    for t in range(0, 3072, 512):
        cols = slice(t, t + 512)
        grad_act = dot_nt(low_rows[...], w_two[cols, :])
        wide[:, cols] = (grad_act * gprime[:, cols]).astype(BF16)
    grad_hidden = g_two[...] + dot_nt(wide[...], w_one[...])
    grad_one = norm_back(grad_hidden, n_one[...], inverse_one, gains[0:1, :])
    g_one[...] = grad_one
    low_one = grad_one.astype(BF16)
    swap_ga = remote(19, ga_send, ga_recv, to_sib)
    ga_send[...] = dot_nt(low_one, w_out[pl.ds(other_half, 384), :]).astype(BF16)
    swap_ga.start()
    ga_mine[...] = dot_nt(low_one, w_out[pl.ds(half, 384), :]).astype(BF16)

    low_row = lax.broadcasted_iota(jnp.int32, (128, 128), 0) < 64
    low_col = lax.broadcasted_iota(jnp.int32, (128, 128), 1) < 64

    def spread(block_at, rows):
        to = slice(128 * block_at, 128 * block_at + 128)
        flipped = rows.T
        for p in range(3):
            cols = slice(128 * p, 128 * p + 128)
            for e in range(2):
                h = 2 * p + e
                rows_of = low_row if e == 0 else jnp.logical_not(low_row)
                cols_of = low_col if e == 0 else jnp.logical_not(low_col)
                go_m[h, to, :] = jnp.where(cols_of, rows[:, cols], 0.0).astype(BF16)
                mine = jnp.where(rows_of, flipped[cols, :], 0.0)
                go_t[h, :, to] = mine.astype(BF16)
                delta[h, :, to] = jnp.sum(mine * att_t[cols, to], axis=0, keepdims=True)

    spread(OWN, ga_mine[0:128, :].astype(F32))
    spread(FAR, ga_mine[128:256, :].astype(F32))
    swap_ga.wait_recv()
    spread(SIB, ga_recv[0:128, :].astype(F32))
    spread(SIB_FAR, ga_recv[128:256, :].astype(F32))

    def backward(first, group_at, first_query, count, heads=range(6)):
        rows = slice(128 * first, 128 * first + 256)
        queries = slice(first_query, first_query + count)

        def value_dots(h):
            return dot(val[h // 2, rows, :], go_t[h, :, queries])

        grad_prob = value_dots(heads[0])
        for h in heads:
            following = value_dots(h + 1) if h + 1 in heads else None
            weight = probs[h, rows, queries].astype(F32) * share[group_at, h, :, queries]
            grad_score = (weight * (grad_prob - delta[h, :, queries])).astype(BF16)
            value_part = dot(weight.astype(BF16), go_m[h, queries, :])
            key_part = dot(grad_score, q_ext[h, queries, 0:128])
            rows_h = slice(64 * h, 64 * h + 64)
            query_part = dot(k_t[rows_h, rows], grad_score)
            if first == NEAR_FAR:
                dq_t[rows_h, queries] = query_part
            else:
                dq_t[rows_h, queries] += query_part
            if h % 2 == 0:
                grad_values, grad_keys = value_part, key_part
            else:
                grad_values, grad_keys = grad_values + value_part, grad_keys + key_part
                cols = slice(64 * h - 64, 64 * h + 64)
                value_cols = slice(64 * h + 320, 64 * h + 448)
                if count == 512:
                    d_kv[rows, cols] = grad_keys.astype(BF16)
                    d_kv[rows, value_cols] = grad_values.astype(BF16)
                elif first_query == 256:
                    d_held[:, cols] = grad_keys
                    d_held[:, value_cols] = grad_values
                else:
                    d_kv[rows, cols] = (d_held[:, cols] + grad_keys).astype(BF16)
                    d_kv[rows, value_cols] = (d_held[:, value_cols] + grad_values).astype(BF16)
            grad_prob = following

    def token_terms(start):
        return dot_nt(d_kv[start : start + 256, :], w_all[:, 384:1152])

    swap_parts = [
        remote(20 + k, part_send.at[pl.ds(128 * k, 128)], part_recv.at[pl.ds(128 * k, 128)], to_sib)
        for k in range(4)
    ]
    send_parts = [
        remote(24 + k, tn_send.at[pl.ds(128 * k, 128)], tn_recv.at[pl.ds(128 * k, 128)], to_near)
        for k in range(2)
    ]

    def share_out(k, terms):
        part_send[128 * k : 128 * k + 128, :] = terms[128:256].astype(BF16)
        swap_parts[k].start()
        part_mine[128 * k : 128 * k + 128, :] = terms[0:128]

    def shared(k):
        swap_parts[k].wait_recv()
        rows = slice(128 * k, 128 * k + 128)
        return part_mine[rows, :] + part_recv[rows, :].astype(F32)

    def pass_on(k):
        tn_send[128 * k : 128 * k + 128, :] = shared(k).astype(BF16)
        send_parts[k].start()

    backward(NEAR_FAR, PART_LAST, 0, 512)
    share_out(0, token_terms(128 * NEAR_FAR))
    backward(NEAR, PART_OWN, 0, 512, range(0, 4))
    pass_on(0)
    backward(NEAR, PART_OWN, 0, 512, range(4, 6))
    share_out(1, token_terms(128 * NEAR))
    backward(FAR, PART_FAR, 0, 512)
    pass_on(1)
    far_terms[...] = token_terms(128 * FAR)
    backward(OWN, PART_OWN, 256, 256)
    low_dq_far = (dq_t[:, 256:512] * 0.125).T.astype(BF16)
    share_out(2, far_terms[...] + dot_nt(low_dq_far, w_all[:, 0:384]))
    backward(OWN, PART_OWN, 0, 256)
    far_part = shared(2) + g_one[128:256, :]
    send_parts[0].wait_recv()
    ig_buf[128:256, :] = (far_part + tn_recv[0:128, :].astype(F32)).astype(BF16)
    send_ig = remote(26, ig_buf.at[pl.ds(128, 128)], in_grad.at[group], to_far)
    keep_ig = local(11, ig_buf.at[pl.ds(0, 128)], in_grad.at[group])
    send_ig.start()

    low_dq_t = (dq_t[...] * 0.125).astype(BF16)
    low_dv_t = d_kv[:, 384:768].astype(F32).T.astype(BF16)
    rank_parts, out_parts = [], []
    for row, product_map in (
        (0, dot(low_dq_t, rank_in[0:512, :])),
        (1, dot(low_dv_t, rank_in[...])),
    ):
        product_map = product_map * v_out_t[...].astype(F32)
        out_row = out_scale[pl.ds(row, 1), pl.ds(half, 384)]
        out_col = jnp.broadcast_to(out_row, (128, 384)).T[:, 0:1]
        rank_part = jnp.sum(product_map * out_col, axis=0, keepdims=True)
        rank_parts += [rank_part[:, 0:512], rank_part[:, 512:1024]]
        out_part = jnp.sum(product_map * rank_scale[pl.ds(row, 1), :], axis=1, keepdims=True)
        out_part = jnp.broadcast_to(out_part, (384, 128)).T[0:1, :]
        out_part = jnp.concatenate([out_part, jnp.zeros((1, 128), F32)], axis=1)
        out_parts += [jnp.where(core == 0, out_part, 0.0), jnp.where(core == 1, out_part, 0.0)]
    for k, part in enumerate(rank_parts + out_parts):
        sum_buf[k : k + 1, :] = part

    def exchange(k, stage, wheres):
        swaps = [
            remote(
                k + n,
                sum_buf.at[pl.ds(8 * stage, 8)],
                sum_recv.at[pl.ds(8 * (k - 27 + n), 8)],
                where,
            )
            for n, where in enumerate(wheres)
        ]
        for swap in swaps:
            swap.start()
        return swaps

    def received(k):
        return sum_recv[8 * k : 8 * k + 8, :]

    core_swaps = exchange(27, 0, (to_sib,))
    low_dq = (dq_t[:, 0:256] * 0.125).T.astype(BF16)
    share_out(3, token_terms(128 * OWN) + dot_nt(low_dq, w_all[:, 0:384]))
    core_swaps[0].wait_recv()
    sum_buf[8:16, :] = sum_buf[0:8, :] + received(0)
    plane_swaps = exchange(28, 1, (to_bx, to_by, to_bxy))
    own_part = shared(3) + g_one[0:128, :]
    for swap in plane_swaps:
        swap.wait_recv()
    sum_buf[16:24, :] = (sum_buf[8:16, :] + received(1)) + (received(2) + received(3))
    line_swaps = exchange(31, 2, (to_near, to_far, to_near_far))
    send_parts[1].wait_recv()
    ig_buf[0:128, :] = (own_part + tn_recv[128:256, :].astype(F32)).astype(BF16)
    keep_ig.start()
    for swap in line_swaps:
        swap.wait_recv()
    sums[...] = (sum_buf[16:24, :] + received(4)) + (received(5) + received(6))

    send_lo.wait_recv()
    send_ig.wait_recv()
    keep_lo.wait()
    keep_ig.wait()
    for item in (
        *send_far,
        *pass_far_near,
        *pass_last,
        send_near,
        send_sib,
        pass_far_sib,
        pass_near_sib,
        send_og,
        swap_att,
        swap_ga,
        send_lo,
        *swap_parts,
        *send_parts,
        send_ig,
        *core_swaps,
        *plane_swaps,
        *line_swaps,
    ):
        item.wait_send()


def finish_kernel(layer_in, grad_in, sums, layer_out, in_grad, rank_total, out_total, norms):
    layer_out[...] = layer_in[...]
    in_grad[...] = grad_in[...]
    rank_rows = [jnp.concatenate([sums[k : k + 1], sums[k + 1 : k + 2]], axis=1) for k in (0, 2)]
    out_rows = [
        jnp.concatenate([sums[k : k + 1, 0:384], sums[k + 1 : k + 2, 0:384]], axis=1) for k in (4, 6)
    ]
    for k in range(2):
        rank_total[k : k + 1, :] = rank_rows[k]
        out_total[k : k + 1, :] = out_rows[k]
    for k, row in enumerate(rank_rows + out_rows):
        norms[k] = jnp.sqrt(jnp.sum(row * row, axis=1, keepdims=True))[0, 0]


def fast_body(
    tokens,
    attn_in_weight,
    out_weight,
    ffn_in_weight,
    ffn_out_weight,
    vera_in,
    vera_out,
    rank_scale,
    out_scale,
    gains,
    shifts,
    ffn_bias,
    splits,
    out_grad,
):
    hbm = pl.BlockSpec(memory_space=pl.ANY)
    vmem = pl.BlockSpec(memory_space=pltpu.VMEM)
    smem = pl.BlockSpec(memory_space=pltpu.SMEM)
    shape = tokens.shape
    small = (rank_scale, out_scale, gains, shifts, ffn_bias.reshape(1, -1))
    scratch = [
        ((1024, 768), BF16),
        ((256, 768), BF16),
        ((768, 1152), BF16),
        ((768, 768), BF16),
        ((768, 3072), BF16),
        ((3072, 768), BF16),
        ((768, 1024), BF16),
        ((1024, 384), BF16),
        ((384, 1024), BF16),
        ((1024, 1024), BF16),
        ((3, 1024, 256), BF16),
        ((6, 512, 256), BF16),
        ((3, 1024, 128), BF16),
        ((384, 1024), BF16),
        ((384, 1024), BF16),
        ((6, 1024, 512), BF16),
        ((2, 1024, 512), F32),
        ((384, 512), F32),
        ((3, 6, 1, 512), F32),
        ((3, 6, 1, 512), F32),
        ((3, 384, 512), F32),
        ((3, 6, 1, 512), F32),
        ((256, 384), BF16),
        ((256, 384), BF16),
        ((256, 768), F32),
        ((256, 768), F32),
        ((256, 3072), BF16),
        ((256, 3072), F32),
        ((256, 768), BF16),
        ((256, 768), F32),
        ((256, 768), F32),
        ((256, 768), BF16),
        ((256, 384), BF16),
        ((256, 384), BF16),
        ((256, 384), BF16),
        ((6, 128, 512), BF16),
        ((6, 512, 128), BF16),
        ((6, 1, 512), F32),
        ((1024, 768), BF16),
        ((256, 768), F32),
        ((384, 512), F32),
        ((512, 768), BF16),
        ((512, 768), BF16),
        ((512, 768), F32),
        ((256, 768), F32),
        ((256, 768), BF16),
        ((256, 768), BF16),
        ((256, 768), BF16),
        ((24, 512), F32),
        ((56, 512), F32),
    ]
    rows_type = jax.ShapeDtypeStruct(shape, BF16)
    layer_rows, grad_rows, sums = pl.pallas_call(
        layer_kernel,
        out_shape=(rows_type, rows_type, jax.ShapeDtypeStruct((8, 512), F32)),
        in_specs=[hbm] * 14,
        out_specs=(hbm, hbm, vmem),
        scratch_shapes=[pltpu.VMEM(item.shape, F32) for item in small]
        + [pltpu.SMEM(splits.shape, jnp.int32)]
        + [pltpu.VMEM(dims, kind) for dims, kind in scratch]
        + [
            pltpu.SemaphoreType.DMA((34,)),
            pltpu.SemaphoreType.DMA((34,)),
            pltpu.SemaphoreType.DMA((18,)),
        ],
        compiler_params=pltpu.CompilerParams(
            collective_id=0, has_side_effects=True, vmem_limit_bytes=60 * 2**20
        ),
        name="encoder_layer",
    )(
        tokens,
        attn_in_weight,
        out_weight,
        ffn_in_weight,
        ffn_out_weight,
        vera_in,
        vera_out,
        out_grad,
        *small,
        splits,
    )
    return pl.pallas_call(
        finish_kernel,
        out_shape=(
            rows_type,
            rows_type,
            jax.ShapeDtypeStruct(rank_scale.shape, F32),
            jax.ShapeDtypeStruct(out_scale.shape, F32),
            jax.ShapeDtypeStruct((4,), F32),
        ),
        in_specs=[vmem, vmem, vmem],
        out_specs=(vmem, vmem, vmem, vmem, smem),
        name="finish",
    )(layer_rows, grad_rows, sums)


def solution(mesh):
    chosen = fast_body if fits(mesh) else body
    in_specs = (
        P("batch", "seq", None),
        P(),
        P(),
        P(),
        P(),
        P(),
        P(),
        P(),
        P(),
        P(),
        P(),
        P(),
        P("batch"),
        P("batch", "seq", None),
    )
    out_specs = (P("batch", "seq", None), P("batch", "seq", None), P(), P(), P())
    return jax.shard_map(chosen, mesh=mesh, in_specs=in_specs, out_specs=out_specs, check_vma=False)
```

```python
import functools

import jax
import jax.numpy as jnp
from jax import lax
from jax.experimental import pallas as pl
from jax.experimental.pallas import tpu as pltpu
from jax.sharding import PartitionSpec as P

HEADS = 12


masked_score = -1e30
key_block = 512


def product(left_side, right_side):
    return jnp.dot(left_side, right_side, preferred_element_type=jnp.float32)


def product_t(left_side, right_side):
    return lax.dot_general(
        left_side, right_side, (((1,), (1,)), ((), ())), preferred_element_type=jnp.float32
    )


def gelu_exact(inputs):
    return jax.nn.gelu(inputs, approximate=False)


def norm_forward(values_in, gain_row, shift_row):
    centered = values_in - jnp.mean(values_in, axis=-1, keepdims=True)
    inverse = lax.rsqrt(jnp.mean(centered * centered, axis=-1, keepdims=True) + 1e-05)
    normed = centered * inverse
    return (normed * gain_row + shift_row, normed, inverse)


def norm_backward(grad_in, normed, inverse, gain_row):
    scaled = grad_in * gain_row
    return inverse * (
        scaled
        - jnp.mean(scaled, axis=-1, keepdims=True)
        - normed * jnp.mean(scaled * normed, axis=-1, keepdims=True)
    )


def block_width():
    return key_block


def body(
    tokens,
    attn_in_weight,
    out_weight,
    ffn_in_weight,
    ffn_out_weight,
    vera_in,
    vera_out,
    rank_scale,
    out_scale,
    gains,
    shifts,
    ffn_bias,
    splits,
    out_grad,
):
    sequences, per_device, model_width = tokens.shape
    head_dim = model_width // HEADS
    score_scale = head_dim ** (-0.5)
    cycle_place = lax.axis_index("seq")
    token_rows = tokens.reshape(-1, model_width)
    token_float = token_rows.astype(jnp.float32)
    rank_in = product(token_rows, vera_in)
    rank_q = (rank_in * rank_scale[0]).astype(jnp.bfloat16)
    rank_v = (rank_in * rank_scale[1]).astype(jnp.bfloat16)
    wide_q = product(rank_q, vera_out)
    wide_v = product(rank_v, vera_out)
    projected = product(token_rows, attn_in_weight)
    query = projected[:, :model_width] + shifts[0] + out_scale[0] * wide_q
    keys = projected[:, model_width : 2 * model_width]
    values = projected[:, 2 * model_width :] + shifts[1] + out_scale[1] * wide_v
    query_low = query.astype(jnp.bfloat16).reshape(sequences, per_device, HEADS, head_dim)
    pair_low = (
        jnp.concatenate([keys, values], axis=-1)
        .astype(jnp.bfloat16)
        .reshape(sequences, per_device, 2 * model_width)
    )
    query_pos = cycle_place * per_device + jnp.arange(per_device, dtype=jnp.int32)
    query_side = query_pos[None, :] < splits[:, None]

    def block_scores(pair_piece, block_start):
        count_keys = pair_piece.shape[1]
        key_pos = block_start + jnp.arange(count_keys, dtype=jnp.int32)
        key_side = key_pos[None, :] < splits[:, None]
        allowed = (query_side[:, :, None] == key_side[:, None, :])[:, None]
        key_heads = pair_piece[:, :, :model_width].reshape(sequences, count_keys, HEADS, head_dim)
        value_heads = pair_piece[:, :, model_width:].reshape(sequences, count_keys, HEADS, head_dim)
        raw_scores = (
            jnp.einsum("sqhe,skhe->shqk", query_low, key_heads, preferred_element_type=jnp.float32)
            * score_scale
        )
        return (raw_scores, allowed, key_heads, value_heads)

    start_max = jnp.full((sequences, HEADS, per_device), masked_score, jnp.float32)
    start_sum = jnp.zeros((sequences, HEADS, per_device), jnp.float32)
    start_acc = jnp.zeros((sequences, per_device, HEADS, head_dim), jnp.float32)
    carry = (start_max, start_sum, start_acc)
    pair_piece = lax.all_gather(pair_low, "seq", axis=1, tiled=True)
    shard_start = jnp.int32(0)
    count_keys = pair_piece.shape[1]
    block_size = block_width()
    for absorb_block_index in range(count_keys // block_size):
        absorb_pair_piece = pair_piece[
            :, absorb_block_index * block_size : (absorb_block_index + 1) * block_size
        ]
        running_max, running_sum, absorb_accumulated = carry
        absorb_raw_scores, absorb_allowed, absorb_key_heads, absorb_value_heads = block_scores(
            absorb_pair_piece, shard_start + absorb_block_index * block_size
        )
        new_max = jnp.maximum(
            running_max,
            jnp.max(jnp.where(absorb_allowed, absorb_raw_scores, masked_score), axis=-1),
        )
        block_weights = jnp.where(
            absorb_allowed, jnp.exp(absorb_raw_scores - new_max[..., None]), 0.0
        )
        rescale = jnp.exp(running_max - new_max)
        running_sum = running_sum * rescale + jnp.sum(block_weights, axis=-1)
        added = jnp.einsum(
            "shqk,skhe->sqhe",
            block_weights.astype(jnp.bfloat16),
            absorb_value_heads,
            preferred_element_type=jnp.float32,
        )
        absorb_accumulated = (
            absorb_accumulated * jnp.transpose(rescale, (0, 2, 1))[..., None] + added
        )
        carry = (new_max, running_sum, absorb_accumulated)
    final_max, final_sum, accumulated = carry
    attended = accumulated / jnp.transpose(final_sum, (0, 2, 1))[..., None]
    log_total = final_max + jnp.log(final_sum)
    branch = product(attended.reshape(-1, model_width).astype(jnp.bfloat16), out_weight) + shifts[2]
    hidden, normed_one, inverse_one = norm_forward(token_float + branch, gains[0], shifts[4])
    inner = product(hidden.astype(jnp.bfloat16), ffn_in_weight) + ffn_bias
    activated, gelu_pull = jax.vjp(gelu_exact, inner)
    ffn_branch = product(activated.astype(jnp.bfloat16), ffn_out_weight) + shifts[3]
    layer_out, normed_two, inverse_two = norm_forward(hidden + ffn_branch, gains[1], shifts[5])
    grad_two = norm_backward(
        out_grad.reshape(-1, model_width).astype(jnp.float32), normed_two, inverse_two, gains[1]
    )
    grad_act = product_t(grad_two.astype(jnp.bfloat16), ffn_out_weight)
    grad_inner = gelu_pull(grad_act)[0].astype(jnp.bfloat16)
    grad_hidden = grad_two + product_t(grad_inner, ffn_in_weight)
    grad_one = norm_backward(grad_hidden, normed_one, inverse_one, gains[0])
    grad_att = (
        product_t(grad_one.astype(jnp.bfloat16), out_weight)
        .astype(jnp.bfloat16)
        .reshape(sequences, per_device, HEADS, head_dim)
    )
    delta = jnp.transpose(jnp.sum(grad_att.astype(jnp.float32) * attended, axis=-1), (0, 2, 1))
    grad_query = jnp.zeros((sequences, per_device, HEADS, head_dim), jnp.float32)
    whole_pairs = lax.all_gather(pair_low, "seq", axis=1, tiled=True)
    whole_len = whole_pairs.shape[1]
    block_size = block_width()
    key_terms = []
    for block_index in range(whole_len // block_size):
        block_pair_piece = whole_pairs[:, block_index * block_size : (block_index + 1) * block_size]
        block_raw_scores, block_allowed, block_key_heads, block_value_heads = block_scores(
            block_pair_piece, block_index * block_size
        )
        prob = jnp.where(block_allowed, jnp.exp(block_raw_scores - log_total[..., None]), 0.0)
        grad_prob = jnp.einsum(
            "sqhe,skhe->shqk", grad_att, block_value_heads, preferred_element_type=jnp.float32
        )
        grad_score = (prob * (grad_prob - delta[..., None])).astype(jnp.bfloat16)
        grad_value = jnp.einsum(
            "shqk,sqhe->skhe",
            prob.astype(jnp.bfloat16),
            grad_att,
            preferred_element_type=jnp.float32,
        )
        grad_key = (
            jnp.einsum("shqk,sqhe->skhe", grad_score, query_low, preferred_element_type=jnp.float32)
            * score_scale
        )
        query_part = (
            jnp.einsum(
                "shqk,skhe->sqhe", grad_score, block_key_heads, preferred_element_type=jnp.float32
            )
            * score_scale
        )
        block_count_keys = block_pair_piece.shape[1]
        pair_part = jnp.concatenate(
            [
                grad_key.reshape(sequences, block_count_keys, model_width),
                grad_value.reshape(sequences, block_count_keys, model_width),
            ],
            axis=-1,
        )
        query_part, pair_part = (query_part, pair_part)
        grad_query = grad_query + query_part
        key_terms.append(pair_part)
    pair_sum = lax.psum_scatter(
        jnp.concatenate(key_terms, axis=1), "seq", scatter_dimension=1, tiled=True
    )
    pair_grad_low = pair_sum.astype(jnp.bfloat16).reshape(-1, 2 * model_width)
    query_grad_low = grad_query.reshape(-1, model_width).astype(jnp.bfloat16)
    query_grad_float = query_grad_low.astype(jnp.float32)
    value_grad_float = pair_grad_low[:, model_width:].astype(jnp.float32)
    grad_wide_q = (query_grad_float * out_scale[0]).astype(jnp.bfloat16)
    grad_wide_v = (value_grad_float * out_scale[1]).astype(jnp.bfloat16)
    grad_rank_q = product_t(grad_wide_q, vera_out)
    grad_rank_v = product_t(grad_wide_v, vera_out)
    grad_rank_in = (grad_rank_q * rank_scale[0] + grad_rank_v * rank_scale[1]).astype(jnp.bfloat16)
    grad_tokens = (
        grad_one
        + product_t(jnp.concatenate([query_grad_low, pair_grad_low], axis=-1), attn_in_weight)
        + product_t(grad_rank_in, vera_in)
    )
    rank_terms = jnp.stack(
        [jnp.sum(grad_rank_q * rank_in, axis=0), jnp.sum(grad_rank_v * rank_in, axis=0)]
    )
    out_terms = jnp.stack(
        [jnp.sum(query_grad_float * wide_q, axis=0), jnp.sum(value_grad_float * wide_v, axis=0)]
    )
    rank_total, out_total = lax.psum((rank_terms, out_terms), ("batch", "seq"))
    scale_norms = jnp.concatenate(
        [
            jnp.sqrt(jnp.sum(rank_total * rank_total, axis=1)),
            jnp.sqrt(jnp.sum(out_total * out_total, axis=1)),
        ]
    )
    return (
        layer_out.astype(jnp.bfloat16).reshape(sequences, per_device, model_width),
        grad_tokens.astype(jnp.bfloat16).reshape(sequences, per_device, model_width),
        rank_total,
        out_total,
        scale_norms,
    )


MESH = pl.DeviceIdType.MESH
BIG = 1e30
F32 = jnp.float32
BF16 = jnp.bfloat16


def fits(mesh):
    return mesh.shape["seq"] == 8 and mesh.shape["batch"] == 4


def dot(left, right):
    return lax.dot_general(left, right, (((1,), (0,)), ((), ())), preferred_element_type=F32)


def dot_nt(left, right):
    return lax.dot_general(left, right, (((1,), (1,)), ((), ())), preferred_element_type=F32)


OWN, SIB, FAR, SIB_FAR, NEAR_FAR, SIB_NEAR_FAR, NEAR, SIB_NEAR = range(8)
PIECES = 2


def layer_kernel(
    tokens,
    attn_in,
    out_w,
    ffn_in,
    ffn_out,
    vera_in,
    vera_out,
    out_grad,
    rank_scale_in,
    out_scale_in,
    gains_in,
    shifts_in,
    ffn_bias_in,
    splits_in,
    layer_out,
    in_grad,
    sums,
    rank_scale,
    out_scale,
    gains,
    shifts,
    ffn_bias,
    splits,
    tok,
    og,
    w_all,
    w_out,
    w_one,
    w_two,
    v_in,
    v_out,
    v_out_t,
    rank_in,
    k_ext,
    q_ext,
    val,
    k_t,
    v_t,
    probs,
    s_buf,
    att_t,
    part_top,
    part_sum,
    part_out,
    share,
    att_send,
    att_recv,
    hid,
    n_one,
    wide,
    low_rows,
    g_two,
    g_one,
    lo_buf,
    ga_send,
    ga_recv,
    ga_mine,
    go_t,
    go_m,
    delta,
    d_kv,
    d_held,
    part_send,
    part_recv,
    part_mine,
    far_terms,
    tn_send,
    tn_recv,
    ig_buf,
    sum_buf,
    sum_recv,
    send_sem,
    recv_sem,
    load_sem,
):
    s = lax.axis_index("seq")
    b = lax.axis_index("batch")
    core = s % 2
    group = s // 4
    sib = s + 1 - 2 * core
    near = s + 2 - 4 * ((s // 2) % 2)
    far = s + 4 - 8 * group
    bx = b + 1 - 2 * (b % 2)
    by = b + 2 - 4 * (b // 2)
    half = pl.multiple_of(core * 384, 384)
    other_half = pl.multiple_of(384 - core * 384, 384)

    def remote(k, src, dst, where):
        return pltpu.make_async_remote_copy(
            src_ref=src,
            dst_ref=dst,
            send_sem=send_sem.at[k],
            recv_sem=recv_sem.at[k],
            device_id=where,
            device_id_type=MESH,
        )

    def local(k, src, dst):
        return pltpu.make_async_copy(src, dst, load_sem.at[k])

    def block(ref, k, n=1):
        return ref.at[pl.ds(128 * k, 128 * n)]

    near_far = far + near - s
    to_sib, to_near, to_far = {"seq": sib}, {"seq": near}, {"seq": far}
    to_near_far = {"seq": near_far}
    to_bx, to_by, to_bxy = {"batch": bx}, {"batch": by}, {"batch": bx + by - b}

    barrier = pltpu.get_barrier_semaphore()
    for where in (to_sib, to_near, to_far, to_near_far, to_bx, to_by, to_bxy):
        pl.semaphore_signal(barrier, inc=1, device_id=where, device_id_type=MESH)

    loads = [
        local(0, tokens.at[group], block(tok, OWN)),
        local(1, vera_in, v_in),
        local(2, vera_out.at[:, pl.ds(half, 384)], v_out),
        local(3, attn_in.at[:, pl.ds(half, 384)], w_all.at[:, pl.ds(0, 384)]),
        local(4, attn_in.at[:, pl.ds(768 + half, 384)], w_all.at[:, pl.ds(384, 384)]),
        local(5, attn_in.at[:, pl.ds(1536 + half, 384)], w_all.at[:, pl.ds(768, 384)]),
        local(6, out_w, w_out),
        local(7, ffn_in, w_one),
        local(8, ffn_out, w_two),
        local(9, out_grad.at[group], og.at[pl.ds(0, 128)]),
    ]
    small_loads = [
        local(12, rank_scale_in, rank_scale),
        local(13, out_scale_in, out_scale),
        local(14, gains_in, gains),
        local(15, shifts_in, shifts),
        local(16, ffn_bias_in, ffn_bias),
        local(17, splits_in, splits),
    ]
    for item in (*small_loads, *loads):
        item.start()
    pl.semaphore_wait(barrier, 7)

    piece = 128 // PIECES
    send_far, pass_far_near, pass_last = [], [], []
    for k in range(PIECES):
        part = pl.ds(128 * FAR + piece * k, piece)
        near_part = pl.ds(128 * NEAR_FAR + piece * k, piece)
        last_part = pl.ds(128 * SIB_NEAR_FAR + piece * k, piece)
        send_far.append(
            remote(k, tokens.at[1 - group, pl.ds(piece * k, piece)], tok.at[part], to_far)
        )
        pass_far_near.append(remote(PIECES + k, tok.at[part], tok.at[near_part], to_near))
        pass_last.append(remote(2 * PIECES + k, tok.at[near_part], tok.at[last_part], to_sib))
    send_near = remote(12, tokens.at[group], block(tok, NEAR), to_near)
    send_sib = remote(13, tokens.at[group], block(tok, SIB), to_sib)
    pass_far_sib = remote(14, block(tok, FAR), block(tok, SIB_FAR), to_sib)
    pass_near_sib = remote(15, block(tok, NEAR), block(tok, SIB_NEAR), to_sib)
    send_og = remote(16, out_grad.at[1 - group], og.at[pl.ds(128, 128)], to_far)
    outer = (s // 2) % 2 == group
    inner = jnp.logical_not(outer)

    def start_far():
        for item in send_far:
            item.start()

    pl.when(outer)(start_far)
    pl.when(inner)(send_near.start)
    send_sib.start()

    for item in (*small_loads, *loads[1:6]):
        item.wait()
    for row, at in ((0, 0), (1, 768)):
        scale_row = rank_scale[pl.ds(row, 1), :]
        out_row = out_scale[pl.ds(row, 1), pl.ds(half, 384)]

        def effective(t, _, at=at, scale_row=scale_row, out_row=out_row):
            rows = pl.ds(pl.multiple_of(t * 256, 256), 256)
            scaled = (v_in[rows, :].astype(F32) * scale_row).astype(BF16)
            wide = dot(scaled, v_out[...]) * out_row
            w_all[rows, at : at + 384] = (w_all[rows, at : at + 384].astype(F32) + wide).astype(BF16)
            return 0

        lax.fori_loop(0, 3, effective, 0)
    v_out_t[...] = v_out[...].astype(F32).T.astype(BF16)

    split = splits[group]
    lane = lax.broadcasted_iota(jnp.int32, (128, 128), 1)
    row_at = lax.broadcasted_iota(jnp.int32, (128, 128), 0)
    flip_one, flip_two, flip_four = sib - s, near - s, far - s
    starts = (
        s,
        s + flip_one,
        s + flip_four,
        s + flip_four + flip_one,
        s + flip_two + flip_four,
        s + flip_two + flip_four + flip_one,
        s + flip_two,
        s + flip_two + flip_one,
    )
    for k in range(8):
        first = (starts[k] * 128 + row_at < split).astype(F32)
        second = 1.0 - first
        key_side = jnp.where(lane == 0, first, jnp.where(lane == 1, second, 0.0)).astype(BF16)
        for p in range(3):
            k_ext[p, 128 * k : 128 * k + 128, 128:256] = key_side
        if k < 4:
            query_side = (
                jnp.where(lane == 0, second, jnp.where(lane == 1, first, 0.0)) * (-BIG)
            ).astype(BF16)
            for h in range(6):
                q_ext[h, 128 * k : 128 * k + 128, 128:256] = query_side

    pl.when(inner)(start_far)
    pl.when(outer)(send_near.start)

    shift_q = shifts[0:1, pl.ds(half, 384)]
    shift_v = shifts[1:2, pl.ds(half, 384)]
    low_lane = lax.broadcasted_iota(jnp.int32, (256, 128), 1) < 64

    def project(first, queries):
        to = slice(128 * first, 128 * first + 256)
        rows = tok[to, :]
        keys = dot(rows, w_all[:, 384:768])
        values = dot(rows, w_all[:, 768:1152]) + shift_v
        low_keys = keys.astype(BF16)
        low_values = values.astype(BF16)
        for p in range(3):
            k_ext[p, to, 0:128] = low_keys[:, 128 * p : 128 * p + 128]
            val[p, to, :] = low_values[:, 128 * p : 128 * p + 128]
        k_t[:, to] = keys.T.astype(BF16)
        v_t[:, to] = values.T.astype(BF16)
        if queries:
            query = dot(rows, w_all[:, 0:384]) + shift_q
            low_query = query.astype(BF16).astype(F32) * 0.125
            for h in range(6):
                p = h // 2
                mine = low_lane if h % 2 == 0 else jnp.logical_not(low_lane)
                masked = jnp.where(mine, low_query[:, 128 * p : 128 * p + 128], 0.0)
                q_ext[h, to, 0:128] = masked.astype(BF16)

    def attend(blocks, first_query, count):
        queries = slice(first_query, first_query + count)
        part_at = blocks[0] // 2
        starts_at = [128 * first for first in blocks]
        peaks, totals, outs = {}, {}, {}

        def scores(h, at):
            part = dot_nt(k_ext[h // 2, at : at + 256, :], q_ext[h, queries, :])
            s_buf[h % 2, at : at + 256, queries] = part
            peak = jnp.max(part, axis=0, keepdims=True)
            peaks[h] = jnp.maximum(peaks[h], peak) if h in peaks else peak

        def weights(h, at):
            weight = jnp.exp(s_buf[h % 2, at : at + 256, queries] - peaks[h])
            total = jnp.sum(weight, axis=0, keepdims=True)
            low_weight = weight.astype(BF16)
            probs[h, at : at + 256, queries] = low_weight
            out = dot(v_t[64 * h : 64 * h + 64, at : at + 256], low_weight)
            totals[h] = totals[h] + total if h in totals else total
            outs[h] = outs[h] + out if h in outs else out

        for at in starts_at:
            scores(0, at)
        for h in range(6):
            for at in starts_at:
                if h < 5:
                    scores(h + 1, at)
                weights(h, at)
            part_top[part_at, h, :, queries] = peaks[h]
            part_sum[part_at, h, :, queries] = totals[h]
            part_out[part_at, 64 * h : 64 * h + 64, queries] = outs[h]

    def combine(first_query, groups):
        queries = slice(first_query, first_query + 256)
        for h in range(6):
            rows_h = slice(64 * h, 64 * h + 64)
            parts = [group_of[0] // 2 for group_of in groups]
            tops = [part_top[k, h, :, queries] for k in parts]
            top = functools.reduce(jnp.maximum, tops)
            shares = [jnp.exp(one - top) for one in tops]
            total = functools.reduce(
                jnp.add, [w * part_sum[k, h, :, queries] for w, k in zip(shares, parts)]
            )
            inverse = 1.0 / total
            shares = [w * inverse for w in shares]
            att_t[rows_h, queries] = functools.reduce(
                jnp.add, [w * part_out[k, rows_h, queries] for w, k in zip(shares, parts)]
            )
            for w, group_of in zip(shares, groups):
                for first in group_of:
                    share[first // 2, h, :, queries] = w

    def rank_rows(first):
        to = slice(128 * first, 128 * first + 256)
        rank_in[to, :] = dot(tok[to, :], v_in[...]).astype(BF16)

    def pass_far():
        for k in range(PIECES):
            send_far[k].wait_recv()
            pass_far_near[k].start()
        pass_far_sib.start()

    def near_blocks():
        send_near.wait_recv()
        pass_near_sib.start()
        pass_near_sib.wait_recv()
        project(NEAR, False)

    def far_blocks():
        pass_far_sib.wait_recv()
        project(FAR, True)

    def pass_last_on():
        for k in range(PIECES):
            pass_far_near[k].wait_recv()
            pass_last[k].start()

    def last_blocks():
        for k in range(PIECES):
            pass_last[k].wait_recv()
        project(NEAR_FAR, False)

    loads[0].wait()
    send_sib.wait_recv()
    project(OWN, True)
    rank_rows(OWN)
    attend((OWN,), 0, 256)

    @pl.when(inner)
    def _():
        pass_far()
        far_blocks()
        attend((FAR,), 0, 256)
        attend((OWN, FAR), 256, 256)
        near_blocks()
        attend((NEAR,), 0, 512)
        rank_rows(NEAR)
        pass_last_on()
        send_og.start()
        last_blocks()
        attend((NEAR_FAR,), 0, 512)
        combine(0, ((OWN,), (FAR,), (NEAR,), (NEAR_FAR,)))
        combine(256, ((OWN, FAR), (NEAR,), (NEAR_FAR,)))

    @pl.when(outer)
    def _():
        near_blocks()
        attend((NEAR,), 0, 256)
        pass_far()
        rank_rows(NEAR)
        far_blocks()
        attend((FAR,), 0, 256)
        attend((OWN, FAR, NEAR), 256, 256)
        pass_last_on()
        send_og.start()
        last_blocks()
        attend((NEAR_FAR,), 0, 512)
        combine(0, ((OWN,), (FAR,), (NEAR,), (NEAR_FAR,)))
        combine(256, ((OWN, FAR, NEAR), (NEAR_FAR,)))

    swap_att = remote(17, att_send, att_recv, to_sib)
    for k, at in ((0, 128 * SIB), (128, 128 * SIB_FAR)):
        att_send[k : k + 128, :] = att_t[:, at : at + 128].T.astype(BF16)
    swap_att.start()

    def norm(values_in):
        centered = values_in - jnp.mean(values_in, axis=-1, keepdims=True)
        inverse = lax.rsqrt(jnp.mean(centered * centered, axis=-1, keepdims=True) + 1e-05)
        return centered * inverse, inverse

    def norm_back(grad_in, normed, inverse, gain_row):
        scaled = grad_in * gain_row
        return inverse * (
            scaled
            - jnp.mean(scaled, axis=-1, keepdims=True)
            - normed * jnp.mean(scaled * normed, axis=-1, keepdims=True)
        )

    loads[6].wait()
    attended_mine = jnp.concatenate([att_t[:, 0:128], att_t[:, 256:384]], axis=1).T
    token_rows = jnp.concatenate([tok[0:128, :], tok[256:384, :]], axis=0).astype(F32)
    branch = dot(attended_mine.astype(BF16), w_out[pl.ds(half, 384), :])
    rank_rows(FAR)
    rank_rows(NEAR_FAR)
    swap_att.wait_recv()
    branch = branch + dot(att_recv[...], w_out[pl.ds(other_half, 384), :]) + shifts[2:3, :]
    normed_one, inverse_one = norm(token_rows + branch)
    n_one[...] = normed_one
    hidden = normed_one * gains[0:1, :] + shifts[4:5, :]
    hid[...] = hidden
    low_rows[...] = hidden.astype(BF16)

    loads[7].wait()
    loads[8].wait()
    def slope(t):
        return s_buf.at[t // 2048, pl.ds(t % 2048 // 2, 256)]

    for t in range(0, 3072, 512):
        cols = slice(t, t + 512)
        inner = dot(low_rows[...], w_one[:, cols]) + ffn_bias[:, cols]
        phi = 0.5 * (1.0 + lax.erf(inner * 0.7071067811865476))
        density = 0.3989422804014327 * jnp.exp(-0.5 * inner * inner)
        slope(t)[...] = phi + inner * density
        wide[:, cols] = (inner * phi).astype(BF16)
    ffn_branch = dot(wide[...], w_two[...])
    normed_two, inverse_two = norm(hid[...] + ffn_branch + shifts[3:4, :])
    lo_buf[...] = (normed_two * gains[1:2, :] + shifts[5:6, :]).astype(BF16)
    send_lo = remote(18, lo_buf.at[pl.ds(128, 128)], layer_out.at[group], to_far)
    keep_lo = local(10, lo_buf.at[pl.ds(0, 128)], layer_out.at[group])
    send_lo.start()
    keep_lo.start()
    loads[9].wait()
    send_og.wait_recv()
    grad_two = norm_back(og[...].astype(F32), normed_two, inverse_two, gains[1:2, :])
    g_two[...] = grad_two
    low_rows[...] = grad_two.astype(BF16)
    for t in range(0, 3072, 512):
        cols = slice(t, t + 512)
        grad_act = dot_nt(low_rows[...], w_two[cols, :])
        wide[:, cols] = (grad_act * slope(t)[...]).astype(BF16)
    grad_hidden = g_two[...] + dot_nt(wide[...], w_one[...])
    grad_one = norm_back(grad_hidden, n_one[...], inverse_one, gains[0:1, :])
    g_one[...] = grad_one
    low_one = grad_one.astype(BF16)
    swap_ga = remote(19, ga_send, ga_recv, to_sib)
    ga_send[...] = dot_nt(low_one, w_out[pl.ds(other_half, 384), :]).astype(BF16)
    swap_ga.start()
    ga_mine[...] = dot_nt(low_one, w_out[pl.ds(half, 384), :]).astype(BF16)

    low_row = lax.broadcasted_iota(jnp.int32, (128, 128), 0) < 64
    low_col = lax.broadcasted_iota(jnp.int32, (128, 128), 1) < 64

    def spread(block_at, rows):
        to = slice(128 * block_at, 128 * block_at + 128)
        flipped = rows.T
        for p in range(3):
            cols = slice(128 * p, 128 * p + 128)
            for e in range(2):
                h = 2 * p + e
                rows_of = low_row if e == 0 else jnp.logical_not(low_row)
                cols_of = low_col if e == 0 else jnp.logical_not(low_col)
                go_m[h, to, :] = jnp.where(cols_of, rows[:, cols], 0.0).astype(BF16)
                mine = jnp.where(rows_of, flipped[cols, :], 0.0)
                go_t[h, :, to] = mine.astype(BF16)
                delta[h, :, to] = jnp.sum(mine * att_t[cols, to], axis=0, keepdims=True)

    spread(OWN, ga_mine[0:128, :].astype(F32))
    spread(FAR, ga_mine[128:256, :].astype(F32))
    swap_ga.wait_recv()
    spread(SIB, ga_recv[0:128, :].astype(F32))
    spread(SIB_FAR, ga_recv[128:256, :].astype(F32))

    dq_t = part_out.at[0]

    def backward(first, first_query, count, heads=range(6)):
        rows = slice(128 * first, 128 * first + 256)
        queries = slice(first_query, first_query + count)

        def value_dots(h):
            return dot(val[h // 2, rows, :], go_t[h, :, queries])

        grad_prob = value_dots(heads[0])
        for h in heads:
            following = value_dots(h + 1) if h + 1 in heads else None
            weight = probs[h, rows, queries].astype(F32) * share[first // 2, h, :, queries]
            grad_score = (weight * (grad_prob - delta[h, :, queries])).astype(BF16)
            value_part = dot(weight.astype(BF16), go_m[h, queries, :])
            key_part = dot(grad_score, q_ext[h, queries, 0:128])
            rows_h = slice(64 * h, 64 * h + 64)
            query_part = dot(k_t[rows_h, rows], grad_score)
            if first == NEAR_FAR:
                dq_t[rows_h, queries] = query_part
            else:
                dq_t[rows_h, queries] += query_part
            if h % 2 == 0:
                grad_values, grad_keys = value_part, key_part
            else:
                grad_values, grad_keys = grad_values + value_part, grad_keys + key_part
                cols = slice(64 * h - 64, 64 * h + 64)
                value_cols = slice(64 * h + 320, 64 * h + 448)
                if count == 512:
                    d_kv[rows, cols] = grad_keys.astype(BF16)
                    d_kv[rows, value_cols] = grad_values.astype(BF16)
                elif first_query == 256:
                    d_held[:, cols] = grad_keys
                    d_held[:, value_cols] = grad_values
                else:
                    d_kv[rows, cols] = (d_held[:, cols] + grad_keys).astype(BF16)
                    d_kv[rows, value_cols] = (d_held[:, value_cols] + grad_values).astype(BF16)
            grad_prob = following

    def token_terms(start):
        return dot_nt(d_kv[start : start + 256, :], w_all[:, 384:1152])

    swap_parts = [
        remote(20 + k, part_send.at[pl.ds(128 * k, 128)], part_recv.at[pl.ds(128 * k, 128)], to_sib)
        for k in range(4)
    ]
    send_parts = [
        remote(24 + k, tn_send.at[pl.ds(128 * k, 128)], tn_recv.at[pl.ds(128 * k, 128)], to_near)
        for k in range(2)
    ]

    def share_out(k, terms):
        part_send[128 * k : 128 * k + 128, :] = terms[128:256].astype(BF16)
        swap_parts[k].start()
        part_mine[128 * k : 128 * k + 128, :] = terms[0:128]

    def shared(k):
        swap_parts[k].wait_recv()
        rows = slice(128 * k, 128 * k + 128)
        return part_mine[rows, :] + part_recv[rows, :].astype(F32)

    def pass_on(k):
        tn_send[128 * k : 128 * k + 128, :] = shared(k).astype(BF16)
        send_parts[k].start()

    backward(NEAR_FAR, 0, 512)
    share_out(0, token_terms(128 * NEAR_FAR))
    backward(NEAR, 0, 512, range(0, 4))
    pass_on(0)
    backward(NEAR, 0, 512, range(4, 6))
    share_out(1, token_terms(128 * NEAR))
    backward(FAR, 0, 512)
    pass_on(1)
    far_terms[...] = token_terms(128 * FAR)
    backward(OWN, 256, 256)
    low_dq_far = (dq_t[:, 256:512] * 0.125).T.astype(BF16)
    share_out(2, far_terms[...] + dot_nt(low_dq_far, w_all[:, 0:384]))
    backward(OWN, 0, 256)
    far_part = shared(2) + g_one[128:256, :]
    send_parts[0].wait_recv()
    ig_buf[128:256, :] = (far_part + tn_recv[0:128, :].astype(F32)).astype(BF16)
    send_ig = remote(26, ig_buf.at[pl.ds(128, 128)], in_grad.at[group], to_far)
    keep_ig = local(11, ig_buf.at[pl.ds(0, 128)], in_grad.at[group])
    send_ig.start()

    low_dq_t = (dq_t[...] * 0.125).astype(BF16)
    low_dv_t = d_kv[:, 384:768].astype(F32).T.astype(BF16)
    rank_parts, out_parts = [], []
    for row, product_map in (
        (0, dot(low_dq_t, rank_in[0:512, :])),
        (1, dot(low_dv_t, rank_in[...])),
    ):
        product_map = product_map * v_out_t[...].astype(F32)
        out_row = out_scale[pl.ds(row, 1), pl.ds(half, 384)]
        out_col = jnp.broadcast_to(out_row, (128, 384)).T[:, 0:1]
        rank_part = jnp.sum(product_map * out_col, axis=0, keepdims=True)
        rank_parts += [rank_part[:, 0:512], rank_part[:, 512:1024]]
        out_part = jnp.sum(product_map * rank_scale[pl.ds(row, 1), :], axis=1, keepdims=True)
        out_part = jnp.broadcast_to(out_part, (384, 128)).T[0:1, :]
        out_part = jnp.concatenate([out_part, jnp.zeros((1, 128), F32)], axis=1)
        out_parts += [jnp.where(core == 0, out_part, 0.0), jnp.where(core == 1, out_part, 0.0)]
    for k, part in enumerate(rank_parts + out_parts):
        sum_buf[k : k + 1, :] = part

    def exchange(k, stage, wheres):
        swaps = [
            remote(
                k + n,
                sum_buf.at[pl.ds(8 * stage, 8)],
                sum_recv.at[pl.ds(8 * (k - 27 + n), 8)],
                where,
            )
            for n, where in enumerate(wheres)
        ]
        for swap in swaps:
            swap.start()
        return swaps

    def received(k):
        return sum_recv[8 * k : 8 * k + 8, :]

    core_swaps = exchange(27, 0, (to_sib,))
    low_dq = (dq_t[:, 0:256] * 0.125).T.astype(BF16)
    share_out(3, token_terms(128 * OWN) + dot_nt(low_dq, w_all[:, 0:384]))
    core_swaps[0].wait_recv()
    sum_buf[8:16, :] = sum_buf[0:8, :] + received(0)
    plane_swaps = exchange(28, 1, (to_bx, to_by, to_bxy))
    own_part = shared(3) + g_one[0:128, :]
    for swap in plane_swaps:
        swap.wait_recv()
    sum_buf[16:24, :] = (sum_buf[8:16, :] + received(1)) + (received(2) + received(3))
    line_swaps = exchange(31, 2, (to_near, to_far, to_near_far))
    send_parts[1].wait_recv()
    ig_buf[0:128, :] = (own_part + tn_recv[128:256, :].astype(F32)).astype(BF16)
    keep_ig.start()
    for swap in line_swaps:
        swap.wait_recv()
    sums[...] = (sum_buf[16:24, :] + received(4)) + (received(5) + received(6))

    send_lo.wait_recv()
    send_ig.wait_recv()
    keep_lo.wait()
    keep_ig.wait()
    for item in (
        *send_far,
        *pass_far_near,
        *pass_last,
        send_near,
        send_sib,
        pass_far_sib,
        pass_near_sib,
        send_og,
        swap_att,
        swap_ga,
        send_lo,
        *swap_parts,
        *send_parts,
        send_ig,
        *core_swaps,
        *plane_swaps,
        *line_swaps,
    ):
        item.wait_send()


def finish_kernel(layer_in, grad_in, sums, layer_out, in_grad, rank_total, out_total, norms):
    layer_out[...] = layer_in[...]
    in_grad[...] = grad_in[...]
    rank_rows = [jnp.concatenate([sums[k : k + 1], sums[k + 1 : k + 2]], axis=1) for k in (0, 2)]
    out_rows = [
        jnp.concatenate([sums[k : k + 1, 0:384], sums[k + 1 : k + 2, 0:384]], axis=1) for k in (4, 6)
    ]
    for k in range(2):
        rank_total[k : k + 1, :] = rank_rows[k]
        out_total[k : k + 1, :] = out_rows[k]
    for k, row in enumerate(rank_rows + out_rows):
        norms[k] = jnp.sqrt(jnp.sum(row * row, axis=1, keepdims=True))[0, 0]


def fast_body(
    tokens,
    attn_in_weight,
    out_weight,
    ffn_in_weight,
    ffn_out_weight,
    vera_in,
    vera_out,
    rank_scale,
    out_scale,
    gains,
    shifts,
    ffn_bias,
    splits,
    out_grad,
):
    hbm = pl.BlockSpec(memory_space=pl.ANY)
    vmem = pl.BlockSpec(memory_space=pltpu.VMEM)
    smem = pl.BlockSpec(memory_space=pltpu.SMEM)
    shape = tokens.shape
    small = (rank_scale, out_scale, gains, shifts, ffn_bias.reshape(1, -1))
    scratch = [
        ((1024, 768), BF16),
        ((256, 768), BF16),
        ((768, 1152), BF16),
        ((768, 768), BF16),
        ((768, 3072), BF16),
        ((3072, 768), BF16),
        ((768, 1024), BF16),
        ((1024, 384), BF16),
        ((384, 1024), BF16),
        ((1024, 1024), BF16),
        ((3, 1024, 256), BF16),
        ((6, 512, 256), BF16),
        ((3, 1024, 128), BF16),
        ((384, 1024), BF16),
        ((384, 1024), BF16),
        ((6, 1024, 512), BF16),
        ((2, 1024, 512), F32),
        ((384, 512), F32),
        ((4, 6, 1, 512), F32),
        ((4, 6, 1, 512), F32),
        ((4, 384, 512), F32),
        ((4, 6, 1, 512), F32),
        ((256, 384), BF16),
        ((256, 384), BF16),
        ((256, 768), F32),
        ((256, 768), F32),
        ((256, 3072), BF16),
        ((256, 768), BF16),
        ((256, 768), F32),
        ((256, 768), F32),
        ((256, 768), BF16),
        ((256, 384), BF16),
        ((256, 384), BF16),
        ((256, 384), BF16),
        ((6, 128, 512), BF16),
        ((6, 512, 128), BF16),
        ((6, 1, 512), F32),
        ((1024, 768), BF16),
        ((256, 768), F32),
        ((512, 768), BF16),
        ((512, 768), BF16),
        ((512, 768), F32),
        ((256, 768), F32),
        ((256, 768), BF16),
        ((256, 768), BF16),
        ((256, 768), BF16),
        ((24, 512), F32),
        ((56, 512), F32),
    ]
    rows_type = jax.ShapeDtypeStruct(shape, BF16)
    held_rows = pltpu.VMEM(shape, BF16)
    layer_rows, grad_rows, sums = pl.pallas_call(
        layer_kernel,
        out_shape=(held_rows, held_rows, pltpu.VMEM((8, 512), F32)),
        in_specs=[hbm] * 14,
        out_specs=(vmem, vmem, vmem),
        scratch_shapes=[pltpu.VMEM(item.shape, F32) for item in small]
        + [pltpu.SMEM(splits.shape, jnp.int32)]
        + [pltpu.VMEM(dims, kind) for dims, kind in scratch]
        + [
            pltpu.SemaphoreType.DMA((34,)),
            pltpu.SemaphoreType.DMA((34,)),
            pltpu.SemaphoreType.DMA((18,)),
        ],
        compiler_params=pltpu.CompilerParams(
            collective_id=0, has_side_effects=True, vmem_limit_bytes=60 * 2**20
        ),
        name="encoder_layer",
    )(
        tokens,
        attn_in_weight,
        out_weight,
        ffn_in_weight,
        ffn_out_weight,
        vera_in,
        vera_out,
        out_grad,
        *small,
        splits,
    )
    return pl.pallas_call(
        finish_kernel,
        out_shape=(
            rows_type,
            rows_type,
            jax.ShapeDtypeStruct(rank_scale.shape, F32),
            jax.ShapeDtypeStruct(out_scale.shape, F32),
            jax.ShapeDtypeStruct((4,), F32),
        ),
        in_specs=[vmem, vmem, vmem],
        out_specs=(vmem, vmem, vmem, vmem, smem),
        name="finish",
    )(*[pltpu.with_memory_space_constraint(x, pltpu.VMEM) for x in (layer_rows, grad_rows, sums)])


def solution(mesh):
    chosen = fast_body if fits(mesh) else body
    in_specs = (
        P("batch", "seq", None),
        P(),
        P(),
        P(),
        P(),
        P(),
        P(),
        P(),
        P(),
        P(),
        P(),
        P(),
        P("batch"),
        P("batch", "seq", None),
    )
    out_specs = (P("batch", "seq", None), P("batch", "seq", None), P(), P(), P())
    return jax.shard_map(chosen, mesh=mesh, in_specs=in_specs, out_specs=out_specs, check_vma=False)
```

```python
import functools

import jax
import jax.numpy as jnp
from jax import lax
from jax.experimental import pallas as pl
from jax.experimental.pallas import tpu as pltpu
from jax.sharding import PartitionSpec as P

HEADS = 12


masked_score = -1e30
key_block = 512


def product(left_side, right_side):
    return jnp.dot(left_side, right_side, preferred_element_type=jnp.float32)


def product_t(left_side, right_side):
    return lax.dot_general(
        left_side, right_side, (((1,), (1,)), ((), ())), preferred_element_type=jnp.float32
    )


def gelu_exact(inputs):
    return jax.nn.gelu(inputs, approximate=False)


def norm_forward(values_in, gain_row, shift_row):
    centered = values_in - jnp.mean(values_in, axis=-1, keepdims=True)
    inverse = lax.rsqrt(jnp.mean(centered * centered, axis=-1, keepdims=True) + 1e-05)
    normed = centered * inverse
    return (normed * gain_row + shift_row, normed, inverse)


def norm_backward(grad_in, normed, inverse, gain_row):
    scaled = grad_in * gain_row
    return inverse * (
        scaled
        - jnp.mean(scaled, axis=-1, keepdims=True)
        - normed * jnp.mean(scaled * normed, axis=-1, keepdims=True)
    )


def block_width():
    return key_block


def body(
    tokens,
    attn_in_weight,
    out_weight,
    ffn_in_weight,
    ffn_out_weight,
    vera_in,
    vera_out,
    rank_scale,
    out_scale,
    gains,
    shifts,
    ffn_bias,
    splits,
    out_grad,
):
    sequences, per_device, model_width = tokens.shape
    head_dim = model_width // HEADS
    score_scale = head_dim ** (-0.5)
    cycle_place = lax.axis_index("seq")
    token_rows = tokens.reshape(-1, model_width)
    token_float = token_rows.astype(jnp.float32)
    rank_in = product(token_rows, vera_in)
    rank_q = (rank_in * rank_scale[0]).astype(jnp.bfloat16)
    rank_v = (rank_in * rank_scale[1]).astype(jnp.bfloat16)
    wide_q = product(rank_q, vera_out)
    wide_v = product(rank_v, vera_out)
    projected = product(token_rows, attn_in_weight)
    query = projected[:, :model_width] + shifts[0] + out_scale[0] * wide_q
    keys = projected[:, model_width : 2 * model_width]
    values = projected[:, 2 * model_width :] + shifts[1] + out_scale[1] * wide_v
    query_low = query.astype(jnp.bfloat16).reshape(sequences, per_device, HEADS, head_dim)
    pair_low = (
        jnp.concatenate([keys, values], axis=-1)
        .astype(jnp.bfloat16)
        .reshape(sequences, per_device, 2 * model_width)
    )
    query_pos = cycle_place * per_device + jnp.arange(per_device, dtype=jnp.int32)
    query_side = query_pos[None, :] < splits[:, None]

    def block_scores(pair_piece, block_start):
        count_keys = pair_piece.shape[1]
        key_pos = block_start + jnp.arange(count_keys, dtype=jnp.int32)
        key_side = key_pos[None, :] < splits[:, None]
        allowed = (query_side[:, :, None] == key_side[:, None, :])[:, None]
        key_heads = pair_piece[:, :, :model_width].reshape(sequences, count_keys, HEADS, head_dim)
        value_heads = pair_piece[:, :, model_width:].reshape(sequences, count_keys, HEADS, head_dim)
        raw_scores = (
            jnp.einsum("sqhe,skhe->shqk", query_low, key_heads, preferred_element_type=jnp.float32)
            * score_scale
        )
        return (raw_scores, allowed, key_heads, value_heads)

    start_max = jnp.full((sequences, HEADS, per_device), masked_score, jnp.float32)
    start_sum = jnp.zeros((sequences, HEADS, per_device), jnp.float32)
    start_acc = jnp.zeros((sequences, per_device, HEADS, head_dim), jnp.float32)
    carry = (start_max, start_sum, start_acc)
    pair_piece = lax.all_gather(pair_low, "seq", axis=1, tiled=True)
    shard_start = jnp.int32(0)
    count_keys = pair_piece.shape[1]
    block_size = block_width()
    for absorb_block_index in range(count_keys // block_size):
        absorb_pair_piece = pair_piece[
            :, absorb_block_index * block_size : (absorb_block_index + 1) * block_size
        ]
        running_max, running_sum, absorb_accumulated = carry
        absorb_raw_scores, absorb_allowed, absorb_key_heads, absorb_value_heads = block_scores(
            absorb_pair_piece, shard_start + absorb_block_index * block_size
        )
        new_max = jnp.maximum(
            running_max,
            jnp.max(jnp.where(absorb_allowed, absorb_raw_scores, masked_score), axis=-1),
        )
        block_weights = jnp.where(
            absorb_allowed, jnp.exp(absorb_raw_scores - new_max[..., None]), 0.0
        )
        rescale = jnp.exp(running_max - new_max)
        running_sum = running_sum * rescale + jnp.sum(block_weights, axis=-1)
        added = jnp.einsum(
            "shqk,skhe->sqhe",
            block_weights.astype(jnp.bfloat16),
            absorb_value_heads,
            preferred_element_type=jnp.float32,
        )
        absorb_accumulated = (
            absorb_accumulated * jnp.transpose(rescale, (0, 2, 1))[..., None] + added
        )
        carry = (new_max, running_sum, absorb_accumulated)
    final_max, final_sum, accumulated = carry
    attended = accumulated / jnp.transpose(final_sum, (0, 2, 1))[..., None]
    log_total = final_max + jnp.log(final_sum)
    branch = product(attended.reshape(-1, model_width).astype(jnp.bfloat16), out_weight) + shifts[2]
    hidden, normed_one, inverse_one = norm_forward(token_float + branch, gains[0], shifts[4])
    inner = product(hidden.astype(jnp.bfloat16), ffn_in_weight) + ffn_bias
    activated, gelu_pull = jax.vjp(gelu_exact, inner)
    ffn_branch = product(activated.astype(jnp.bfloat16), ffn_out_weight) + shifts[3]
    layer_out, normed_two, inverse_two = norm_forward(hidden + ffn_branch, gains[1], shifts[5])
    grad_two = norm_backward(
        out_grad.reshape(-1, model_width).astype(jnp.float32), normed_two, inverse_two, gains[1]
    )
    grad_act = product_t(grad_two.astype(jnp.bfloat16), ffn_out_weight)
    grad_inner = gelu_pull(grad_act)[0].astype(jnp.bfloat16)
    grad_hidden = grad_two + product_t(grad_inner, ffn_in_weight)
    grad_one = norm_backward(grad_hidden, normed_one, inverse_one, gains[0])
    grad_att = (
        product_t(grad_one.astype(jnp.bfloat16), out_weight)
        .astype(jnp.bfloat16)
        .reshape(sequences, per_device, HEADS, head_dim)
    )
    delta = jnp.transpose(jnp.sum(grad_att.astype(jnp.float32) * attended, axis=-1), (0, 2, 1))
    grad_query = jnp.zeros((sequences, per_device, HEADS, head_dim), jnp.float32)
    whole_pairs = lax.all_gather(pair_low, "seq", axis=1, tiled=True)
    whole_len = whole_pairs.shape[1]
    block_size = block_width()
    key_terms = []
    for block_index in range(whole_len // block_size):
        block_pair_piece = whole_pairs[:, block_index * block_size : (block_index + 1) * block_size]
        block_raw_scores, block_allowed, block_key_heads, block_value_heads = block_scores(
            block_pair_piece, block_index * block_size
        )
        prob = jnp.where(block_allowed, jnp.exp(block_raw_scores - log_total[..., None]), 0.0)
        grad_prob = jnp.einsum(
            "sqhe,skhe->shqk", grad_att, block_value_heads, preferred_element_type=jnp.float32
        )
        grad_score = (prob * (grad_prob - delta[..., None])).astype(jnp.bfloat16)
        grad_value = jnp.einsum(
            "shqk,sqhe->skhe",
            prob.astype(jnp.bfloat16),
            grad_att,
            preferred_element_type=jnp.float32,
        )
        grad_key = (
            jnp.einsum("shqk,sqhe->skhe", grad_score, query_low, preferred_element_type=jnp.float32)
            * score_scale
        )
        query_part = (
            jnp.einsum(
                "shqk,skhe->sqhe", grad_score, block_key_heads, preferred_element_type=jnp.float32
            )
            * score_scale
        )
        block_count_keys = block_pair_piece.shape[1]
        pair_part = jnp.concatenate(
            [
                grad_key.reshape(sequences, block_count_keys, model_width),
                grad_value.reshape(sequences, block_count_keys, model_width),
            ],
            axis=-1,
        )
        query_part, pair_part = (query_part, pair_part)
        grad_query = grad_query + query_part
        key_terms.append(pair_part)
    pair_sum = lax.psum_scatter(
        jnp.concatenate(key_terms, axis=1), "seq", scatter_dimension=1, tiled=True
    )
    pair_grad_low = pair_sum.astype(jnp.bfloat16).reshape(-1, 2 * model_width)
    query_grad_low = grad_query.reshape(-1, model_width).astype(jnp.bfloat16)
    query_grad_float = query_grad_low.astype(jnp.float32)
    value_grad_float = pair_grad_low[:, model_width:].astype(jnp.float32)
    grad_wide_q = (query_grad_float * out_scale[0]).astype(jnp.bfloat16)
    grad_wide_v = (value_grad_float * out_scale[1]).astype(jnp.bfloat16)
    grad_rank_q = product_t(grad_wide_q, vera_out)
    grad_rank_v = product_t(grad_wide_v, vera_out)
    grad_rank_in = (grad_rank_q * rank_scale[0] + grad_rank_v * rank_scale[1]).astype(jnp.bfloat16)
    grad_tokens = (
        grad_one
        + product_t(jnp.concatenate([query_grad_low, pair_grad_low], axis=-1), attn_in_weight)
        + product_t(grad_rank_in, vera_in)
    )
    rank_terms = jnp.stack(
        [jnp.sum(grad_rank_q * rank_in, axis=0), jnp.sum(grad_rank_v * rank_in, axis=0)]
    )
    out_terms = jnp.stack(
        [jnp.sum(query_grad_float * wide_q, axis=0), jnp.sum(value_grad_float * wide_v, axis=0)]
    )
    rank_total, out_total = lax.psum((rank_terms, out_terms), ("batch", "seq"))
    scale_norms = jnp.concatenate(
        [
            jnp.sqrt(jnp.sum(rank_total * rank_total, axis=1)),
            jnp.sqrt(jnp.sum(out_total * out_total, axis=1)),
        ]
    )
    return (
        layer_out.astype(jnp.bfloat16).reshape(sequences, per_device, model_width),
        grad_tokens.astype(jnp.bfloat16).reshape(sequences, per_device, model_width),
        rank_total,
        out_total,
        scale_norms,
    )


MESH = pl.DeviceIdType.MESH
BIG = 1e30
F32 = jnp.float32
BF16 = jnp.bfloat16


def fits(mesh):
    return mesh.shape["seq"] == 8 and mesh.shape["batch"] == 4


def dot(left, right):
    return lax.dot_general(left, right, (((1,), (0,)), ((), ())), preferred_element_type=F32)


def dot_nt(left, right):
    return lax.dot_general(left, right, (((1,), (1,)), ((), ())), preferred_element_type=F32)


OWN, SIB, FAR, SIB_FAR, NEAR_FAR, SIB_NEAR_FAR, NEAR, SIB_NEAR = range(8)
PIECES = 4


def layer_kernel(
    tokens,
    attn_in,
    out_w,
    ffn_in,
    ffn_out,
    vera_in,
    vera_out,
    out_grad,
    rank_scale_in,
    out_scale_in,
    gains_in,
    shifts_in,
    ffn_bias_in,
    splits_in,
    layer_out,
    in_grad,
    sums,
    rank_scale,
    out_scale,
    gains,
    shifts,
    ffn_bias,
    splits,
    tok,
    og,
    w_all,
    w_out,
    w_one,
    w_two,
    v_in,
    v_out,
    v_out_t,
    rank_in,
    k_ext,
    q_ext,
    val,
    k_t,
    v_t,
    probs,
    s_buf,
    att_t,
    part_top,
    part_sum,
    part_out,
    share,
    att_send,
    att_recv,
    hid,
    n_one,
    wide,
    low_rows,
    g_two,
    g_one,
    lo_buf,
    ga_send,
    ga_recv,
    ga_mine,
    go_t,
    go_m,
    delta,
    d_kv,
    d_held,
    part_send,
    part_recv,
    part_mine,
    far_terms,
    tn_send,
    tn_recv,
    ig_buf,
    sum_buf,
    sum_recv,
    send_sem,
    recv_sem,
    load_sem,
):
    s = lax.axis_index("seq")
    b = lax.axis_index("batch")
    core = s % 2
    group = s // 4
    sib = s + 1 - 2 * core
    near = s + 2 - 4 * ((s // 2) % 2)
    far = s + 4 - 8 * group
    bx = b + 1 - 2 * (b % 2)
    by = b + 2 - 4 * (b // 2)
    half = pl.multiple_of(core * 384, 384)
    other_half = pl.multiple_of(384 - core * 384, 384)

    def remote(k, src, dst, where):
        return pltpu.make_async_remote_copy(
            src_ref=src,
            dst_ref=dst,
            send_sem=send_sem.at[k],
            recv_sem=recv_sem.at[k],
            device_id=where,
            device_id_type=MESH,
        )

    def local(k, src, dst):
        return pltpu.make_async_copy(src, dst, load_sem.at[k])

    def block(ref, k, n=1):
        return ref.at[pl.ds(128 * k, 128 * n)]

    near_far = far + near - s
    to_sib, to_near, to_far = {"seq": sib}, {"seq": near}, {"seq": far}
    to_near_far = {"seq": near_far}
    to_bx, to_by, to_bxy = {"batch": bx}, {"batch": by}, {"batch": bx + by - b}

    barrier = pltpu.get_barrier_semaphore()
    for where in (to_sib, to_near, to_far, to_near_far, to_bx, to_by, to_bxy):
        pl.semaphore_signal(barrier, inc=1, device_id=where, device_id_type=MESH)

    loads = [
        local(0, tokens.at[group], block(tok, OWN)),
        local(1, vera_in, v_in),
        local(2, vera_out.at[:, pl.ds(half, 384)], v_out),
        local(3, attn_in.at[:, pl.ds(half, 384)], w_all.at[:, pl.ds(0, 384)]),
        local(4, attn_in.at[:, pl.ds(768 + half, 384)], w_all.at[:, pl.ds(384, 384)]),
        local(5, attn_in.at[:, pl.ds(1536 + half, 384)], w_all.at[:, pl.ds(768, 384)]),
        local(6, out_w, w_out),
        local(7, ffn_in, w_one),
        local(8, ffn_out, w_two),
        local(9, out_grad.at[group], og.at[pl.ds(0, 128)]),
    ]
    small_loads = [
        local(12, rank_scale_in, rank_scale),
        local(13, out_scale_in, out_scale),
        local(14, gains_in, gains),
        local(15, shifts_in, shifts),
        local(16, ffn_bias_in, ffn_bias),
        local(17, splits_in, splits),
    ]
    for item in (*loads[1:6], *small_loads, loads[0]):
        item.start()
    pl.semaphore_wait(barrier, 7)

    piece = 128 // PIECES
    send_far, pass_far_near, pass_last = [], [], []
    for k in range(PIECES):
        part = pl.ds(128 * FAR + piece * k, piece)
        near_part = pl.ds(128 * NEAR_FAR + piece * k, piece)
        last_part = pl.ds(128 * SIB_NEAR_FAR + piece * k, piece)
        send_far.append(
            remote(k, tokens.at[1 - group, pl.ds(piece * k, piece)], tok.at[part], to_far)
        )
        pass_far_near.append(remote(PIECES + k, tok.at[part], tok.at[near_part], to_near))
        pass_last.append(remote(2 * PIECES + k, tok.at[near_part], tok.at[last_part], to_sib))
    send_near = remote(12, tokens.at[group], block(tok, NEAR), to_near)
    send_sib = remote(13, tokens.at[group], block(tok, SIB), to_sib)
    pass_far_sib = remote(14, block(tok, FAR), block(tok, SIB_FAR), to_sib)
    pass_near_sib = remote(15, block(tok, NEAR), block(tok, SIB_NEAR), to_sib)
    send_og = remote(16, out_grad.at[1 - group], og.at[pl.ds(128, 128)], to_far)
    outer = (s // 2) % 2 == group
    inner = jnp.logical_not(outer)

    def start_far():
        for item in send_far:
            item.start()

    pl.when(outer)(start_far)
    pl.when(inner)(send_near.start)
    send_sib.start()

    for item in (*small_loads, *loads[1:6]):
        item.wait()
    for item in loads[6:10]:
        item.start()
    for row, at in ((0, 0), (1, 768)):
        scale_row = rank_scale[pl.ds(row, 1), :]
        out_row = out_scale[pl.ds(row, 1), pl.ds(half, 384)]

        def effective(t, _, at=at, scale_row=scale_row, out_row=out_row):
            rows = pl.ds(pl.multiple_of(t * 256, 256), 256)
            scaled = (v_in[rows, :].astype(F32) * scale_row).astype(BF16)
            wide = dot(scaled, v_out[...]) * out_row
            w_all[rows, at : at + 384] = (w_all[rows, at : at + 384].astype(F32) + wide).astype(BF16)
            return 0

        lax.fori_loop(0, 3, effective, 0)
    v_out_t[...] = v_out[...].astype(F32).T.astype(BF16)

    split = splits[group]
    lane = lax.broadcasted_iota(jnp.int32, (128, 128), 1)
    row_at = lax.broadcasted_iota(jnp.int32, (128, 128), 0)
    flip_one, flip_two, flip_four = sib - s, near - s, far - s
    starts = (
        s,
        s + flip_one,
        s + flip_four,
        s + flip_four + flip_one,
        s + flip_two + flip_four,
        s + flip_two + flip_four + flip_one,
        s + flip_two,
        s + flip_two + flip_one,
    )
    for k in range(8):
        first = (starts[k] * 128 + row_at < split).astype(F32)
        second = 1.0 - first
        key_side = jnp.where(lane == 0, first, jnp.where(lane == 1, second, 0.0)).astype(BF16)
        for p in range(3):
            k_ext[p, 128 * k : 128 * k + 128, 128:256] = key_side
        if k < 4:
            query_side = (
                jnp.where(lane == 0, second, jnp.where(lane == 1, first, 0.0)) * (-BIG)
            ).astype(BF16)
            for h in range(6):
                q_ext[h, 128 * k : 128 * k + 128, 128:256] = query_side

    pl.when(inner)(start_far)
    pl.when(outer)(send_near.start)

    shift_q = shifts[0:1, pl.ds(half, 384)]
    shift_v = shifts[1:2, pl.ds(half, 384)]
    low_lane = lax.broadcasted_iota(jnp.int32, (256, 128), 1) < 64

    def project(first, queries, count=256):
        to = slice(128 * first, 128 * first + count)
        rows = tok[to, :]
        keys = dot(rows, w_all[:, 384:768])
        values = dot(rows, w_all[:, 768:1152]) + shift_v
        low_keys = keys.astype(BF16)
        low_values = values.astype(BF16)
        for p in range(3):
            k_ext[p, to, 0:128] = low_keys[:, 128 * p : 128 * p + 128]
            val[p, to, :] = low_values[:, 128 * p : 128 * p + 128]
        k_t[:, to] = keys.T.astype(BF16)
        v_t[:, to] = values.T.astype(BF16)
        if queries:
            query = dot(rows, w_all[:, 0:384]) + shift_q
            low_query = query.astype(BF16).astype(F32) * 0.125
            for h in range(6):
                p = h // 2
                mine = low_lane if h % 2 == 0 else jnp.logical_not(low_lane)
                masked = jnp.where(mine, low_query[:, 128 * p : 128 * p + 128], 0.0)
                q_ext[h, to, 0:128] = masked.astype(BF16)

    def attend(blocks, first_query, count):
        queries = slice(first_query, first_query + count)
        part_at = blocks[0] // 2
        starts_at = [128 * first for first in blocks]
        peaks, totals, outs = {}, {}, {}

        def scores(h, at):
            part = dot_nt(k_ext[h // 2, at : at + 256, :], q_ext[h, queries, :])
            s_buf[h % 2, at : at + 256, queries] = part
            peak = jnp.max(part, axis=0, keepdims=True)
            peaks[h] = jnp.maximum(peaks[h], peak) if h in peaks else peak

        def weights(h, at):
            weight = jnp.exp(s_buf[h % 2, at : at + 256, queries] - peaks[h])
            total = jnp.sum(weight, axis=0, keepdims=True)
            low_weight = weight.astype(BF16)
            probs[h, at : at + 256, queries] = low_weight
            out = dot(v_t[64 * h : 64 * h + 64, at : at + 256], low_weight)
            totals[h] = totals[h] + total if h in totals else total
            outs[h] = outs[h] + out if h in outs else out

        for at in starts_at:
            scores(0, at)
        for h in range(6):
            for at in starts_at:
                if h < 5:
                    scores(h + 1, at)
                weights(h, at)
            part_top[part_at, h, :, queries] = peaks[h]
            part_sum[part_at, h, :, queries] = totals[h]
            part_out[part_at, 64 * h : 64 * h + 64, queries] = outs[h]

    def combine(first_query, groups):
        queries = slice(first_query, first_query + 256)
        for h in range(6):
            rows_h = slice(64 * h, 64 * h + 64)
            parts = [group_of[0] // 2 for group_of in groups]
            tops = [part_top[k, h, :, queries] for k in parts]
            top = functools.reduce(jnp.maximum, tops)
            shares = [jnp.exp(one - top) for one in tops]
            total = functools.reduce(
                jnp.add, [w * part_sum[k, h, :, queries] for w, k in zip(shares, parts)]
            )
            inverse = 1.0 / total
            shares = [w * inverse for w in shares]
            att_t[rows_h, queries] = functools.reduce(
                jnp.add, [w * part_out[k, rows_h, queries] for w, k in zip(shares, parts)]
            )
            for w, group_of in zip(shares, groups):
                for first in group_of:
                    share[first // 2, h, :, queries] = w

    def rank_rows(first):
        to = slice(128 * first, 128 * first + 256)
        rank_in[to, :] = dot(tok[to, :], v_in[...]).astype(BF16)

    def pass_far():
        for k in range(PIECES):
            send_far[k].wait_recv()
            pass_far_near[k].start()
        pass_far_sib.start()

    def near_blocks():
        send_near.wait_recv()
        pass_near_sib.start()
        pass_near_sib.wait_recv()
        project(NEAR, False)

    def far_blocks():
        pass_far_sib.wait_recv()
        project(FAR, True)

    def pass_last_on():
        for k in range(PIECES):
            pass_far_near[k].wait_recv()
            pass_last[k].start()

    def last_blocks():
        project(NEAR_FAR, False, 128)
        for k in range(PIECES):
            pass_last[k].wait_recv()
        project(SIB_NEAR_FAR, False, 128)

    loads[0].wait()
    send_sib.wait_recv()
    project(OWN, True)
    rank_rows(OWN)
    attend((OWN,), 0, 256)

    @pl.when(inner)
    def _():
        pass_far()
        far_blocks()
        attend((FAR,), 0, 256)
        attend((OWN, FAR), 256, 256)
        near_blocks()
        attend((NEAR,), 0, 512)
        rank_rows(NEAR)
        pass_last_on()
        send_og.start()
        last_blocks()
        attend((NEAR_FAR,), 0, 512)
        combine(0, ((OWN,), (FAR,), (NEAR,), (NEAR_FAR,)))
        combine(256, ((OWN, FAR), (NEAR,), (NEAR_FAR,)))

    @pl.when(outer)
    def _():
        near_blocks()
        attend((NEAR,), 0, 256)
        pass_far()
        rank_rows(NEAR)
        far_blocks()
        attend((FAR,), 0, 256)
        attend((OWN, FAR, NEAR), 256, 256)
        pass_last_on()
        send_og.start()
        last_blocks()
        attend((NEAR_FAR,), 0, 512)
        combine(0, ((OWN,), (FAR,), (NEAR,), (NEAR_FAR,)))
        combine(256, ((OWN, FAR, NEAR), (NEAR_FAR,)))

    swap_att = remote(17, att_send, att_recv, to_sib)
    for k, at in ((0, 128 * SIB), (128, 128 * SIB_FAR)):
        att_send[k : k + 128, :] = att_t[:, at : at + 128].T.astype(BF16)
    swap_att.start()

    def norm(values_in):
        centered = values_in - jnp.mean(values_in, axis=-1, keepdims=True)
        inverse = lax.rsqrt(jnp.mean(centered * centered, axis=-1, keepdims=True) + 1e-05)
        return centered * inverse, inverse

    def norm_back(grad_in, normed, inverse, gain_row):
        scaled = grad_in * gain_row
        return inverse * (
            scaled
            - jnp.mean(scaled, axis=-1, keepdims=True)
            - normed * jnp.mean(scaled * normed, axis=-1, keepdims=True)
        )

    loads[6].wait()
    attended_mine = jnp.concatenate([att_t[:, 0:128], att_t[:, 256:384]], axis=1).T
    token_rows = jnp.concatenate([tok[0:128, :], tok[256:384, :]], axis=0).astype(F32)
    branch = dot(attended_mine.astype(BF16), w_out[pl.ds(half, 384), :])
    rank_rows(FAR)
    rank_rows(NEAR_FAR)
    swap_att.wait_recv()
    branch = branch + dot(att_recv[...], w_out[pl.ds(other_half, 384), :]) + shifts[2:3, :]
    normed_one, inverse_one = norm(token_rows + branch)
    n_one[...] = normed_one
    hidden = normed_one * gains[0:1, :] + shifts[4:5, :]
    hid[...] = hidden
    low_rows[...] = hidden.astype(BF16)

    loads[7].wait()
    loads[8].wait()
    def slope(t):
        return s_buf.at[t // 2048, pl.ds(t % 2048 // 2, 256)]

    for t in range(0, 3072, 512):
        cols = slice(t, t + 512)
        inner = dot(low_rows[...], w_one[:, cols]) + ffn_bias[:, cols]
        phi = 0.5 * (1.0 + lax.erf(inner * 0.7071067811865476))
        density = 0.3989422804014327 * jnp.exp(-0.5 * inner * inner)
        slope(t)[...] = phi + inner * density
        wide[:, cols] = (inner * phi).astype(BF16)
    ffn_branch = dot(wide[...], w_two[...])
    normed_two, inverse_two = norm(hid[...] + ffn_branch + shifts[3:4, :])
    out_rows = (normed_two * gains[1:2, :] + shifts[5:6, :]).astype(BF16)
    lo_buf[...] = out_rows[128:256]
    send_lo = remote(18, lo_buf, layer_out.at[group], to_far)
    send_lo.start()
    layer_out[group] = out_rows[0:128]
    loads[9].wait()
    send_og.wait_recv()
    grad_two = norm_back(og[...].astype(F32), normed_two, inverse_two, gains[1:2, :])
    g_two[...] = grad_two
    low_rows[...] = grad_two.astype(BF16)
    for t in range(0, 3072, 512):
        cols = slice(t, t + 512)
        grad_act = dot_nt(low_rows[...], w_two[cols, :])
        wide[:, cols] = (grad_act * slope(t)[...]).astype(BF16)
    grad_hidden = g_two[...] + dot_nt(wide[...], w_one[...])
    grad_one = norm_back(grad_hidden, n_one[...], inverse_one, gains[0:1, :])
    g_one[...] = grad_one
    low_one = grad_one.astype(BF16)
    swap_ga = remote(19, ga_send, ga_recv, to_sib)
    ga_send[...] = dot_nt(low_one, w_out[pl.ds(other_half, 384), :]).astype(BF16)
    swap_ga.start()
    ga_mine[...] = dot_nt(low_one, w_out[pl.ds(half, 384), :]).astype(BF16)

    low_row = lax.broadcasted_iota(jnp.int32, (128, 128), 0) < 64
    low_col = lax.broadcasted_iota(jnp.int32, (128, 128), 1) < 64

    def spread(block_at, rows):
        to = slice(128 * block_at, 128 * block_at + 128)
        flipped = rows.T
        for p in range(3):
            cols = slice(128 * p, 128 * p + 128)
            for e in range(2):
                h = 2 * p + e
                rows_of = low_row if e == 0 else jnp.logical_not(low_row)
                cols_of = low_col if e == 0 else jnp.logical_not(low_col)
                go_m[h, to, :] = jnp.where(cols_of, rows[:, cols], 0.0).astype(BF16)
                mine = jnp.where(rows_of, flipped[cols, :], 0.0)
                go_t[h, :, to] = mine.astype(BF16)
                delta[h, :, to] = jnp.sum(mine * att_t[cols, to], axis=0, keepdims=True)

    spread(OWN, ga_mine[0:128, :].astype(F32))
    spread(FAR, ga_mine[128:256, :].astype(F32))
    swap_ga.wait_recv()
    spread(SIB, ga_recv[0:128, :].astype(F32))
    spread(SIB_FAR, ga_recv[128:256, :].astype(F32))

    dq_t = part_out.at[0]

    def backward(first, first_query, count, heads=range(6)):
        rows = slice(128 * first, 128 * first + 256)
        queries = slice(first_query, first_query + count)

        def value_dots(h):
            return dot(val[h // 2, rows, :], go_t[h, :, queries])

        grad_prob = value_dots(heads[0])
        for h in heads:
            following = value_dots(h + 1) if h + 1 in heads else None
            weight = probs[h, rows, queries].astype(F32) * share[first // 2, h, :, queries]
            grad_score = (weight * (grad_prob - delta[h, :, queries])).astype(BF16)
            value_part = dot(weight.astype(BF16), go_m[h, queries, :])
            key_part = dot(grad_score, q_ext[h, queries, 0:128])
            rows_h = slice(64 * h, 64 * h + 64)
            query_part = dot(k_t[rows_h, rows], grad_score)
            if first == NEAR_FAR:
                dq_t[rows_h, queries] = query_part
            else:
                dq_t[rows_h, queries] += query_part
            if h % 2 == 0:
                grad_values, grad_keys = value_part, key_part
            else:
                grad_values, grad_keys = grad_values + value_part, grad_keys + key_part
                cols = slice(64 * h - 64, 64 * h + 64)
                value_cols = slice(64 * h + 320, 64 * h + 448)
                if count == 512:
                    d_kv[rows, cols] = grad_keys.astype(BF16)
                    d_kv[rows, value_cols] = grad_values.astype(BF16)
                elif first_query == 256:
                    d_held[:, cols] = grad_keys
                    d_held[:, value_cols] = grad_values
                else:
                    d_kv[rows, cols] = (d_held[:, cols] + grad_keys).astype(BF16)
                    d_kv[rows, value_cols] = (d_held[:, value_cols] + grad_values).astype(BF16)
            grad_prob = following

    def token_terms(start):
        return dot_nt(d_kv[start : start + 256, :], w_all[:, 384:1152])

    swap_parts = [
        remote(20 + k, part_send.at[pl.ds(128 * k, 128)], part_recv.at[pl.ds(128 * k, 128)], to_sib)
        for k in range(4)
    ]
    send_parts = [
        remote(24 + k, tn_send.at[pl.ds(128 * k, 128)], tn_recv.at[pl.ds(128 * k, 128)], to_near)
        for k in range(2)
    ]

    def share_out(k, terms):
        part_send[128 * k : 128 * k + 128, :] = terms[128:256].astype(BF16)
        swap_parts[k].start()
        part_mine[128 * k : 128 * k + 128, :] = terms[0:128]

    def shared(k):
        swap_parts[k].wait_recv()
        rows = slice(128 * k, 128 * k + 128)
        return part_mine[rows, :] + part_recv[rows, :].astype(F32)

    def pass_on(k):
        tn_send[128 * k : 128 * k + 128, :] = shared(k).astype(BF16)
        send_parts[k].start()

    backward(NEAR_FAR, 0, 512)
    share_out(0, token_terms(128 * NEAR_FAR))
    backward(NEAR, 0, 512, range(0, 2))
    pass_on(0)
    backward(NEAR, 0, 512, range(2, 6))
    share_out(1, token_terms(128 * NEAR))
    backward(FAR, 0, 512)
    pass_on(1)
    far_terms[...] = token_terms(128 * FAR)
    backward(OWN, 256, 256)
    low_dq_far = (dq_t[:, 256:512] * 0.125).T.astype(BF16)
    share_out(2, far_terms[...] + dot_nt(low_dq_far, w_all[:, 0:384]))
    backward(OWN, 0, 256)
    far_part = shared(2) + g_one[128:256, :]
    send_parts[0].wait_recv()
    ig_buf[...] = (far_part + tn_recv[0:128, :].astype(F32)).astype(BF16)
    send_ig = remote(26, ig_buf, in_grad.at[group], to_far)
    send_ig.start()

    low_dq_t = (dq_t[...] * 0.125).astype(BF16)
    low_dv_t = d_kv[:, 384:768].astype(F32).T.astype(BF16)
    rank_parts, out_parts = [], []
    for row, product_map in (
        (0, dot(low_dq_t, rank_in[0:512, :])),
        (1, dot(low_dv_t, rank_in[...])),
    ):
        product_map = product_map * v_out_t[...].astype(F32)
        out_row = out_scale[pl.ds(row, 1), pl.ds(half, 384)]
        out_col = jnp.broadcast_to(out_row, (128, 384)).T[:, 0:1]
        rank_part = jnp.sum(product_map * out_col, axis=0, keepdims=True)
        rank_parts += [rank_part[:, 0:512], rank_part[:, 512:1024]]
        out_part = jnp.sum(product_map * rank_scale[pl.ds(row, 1), :], axis=1, keepdims=True)
        out_part = jnp.broadcast_to(out_part, (384, 128)).T[0:1, :]
        out_part = jnp.concatenate([out_part, jnp.zeros((1, 128), F32)], axis=1)
        out_parts += [jnp.where(core == 0, out_part, 0.0), jnp.where(core == 1, out_part, 0.0)]
    for k, part in enumerate(rank_parts + out_parts):
        sum_buf[k : k + 1, :] = part

    def exchange(k, stage, wheres):
        swaps = [
            remote(
                k + n,
                sum_buf.at[pl.ds(8 * stage, 8)],
                sum_recv.at[pl.ds(8 * (k - 27 + n), 8)],
                where,
            )
            for n, where in enumerate(wheres)
        ]
        for swap in swaps:
            swap.start()
        return swaps

    def received(k):
        return sum_recv[8 * k : 8 * k + 8, :]

    core_swaps = exchange(27, 0, (to_sib,))
    low_dq = (dq_t[:, 0:256] * 0.125).T.astype(BF16)
    share_out(3, token_terms(128 * OWN) + dot_nt(low_dq, w_all[:, 0:384]))
    core_swaps[0].wait_recv()
    sum_buf[8:16, :] = sum_buf[0:8, :] + received(0)
    plane_swaps = exchange(28, 1, (to_bx, to_by, to_bxy))
    own_part = shared(3) + g_one[0:128, :]
    for swap in plane_swaps:
        swap.wait_recv()
    sum_buf[16:24, :] = (sum_buf[8:16, :] + received(1)) + (received(2) + received(3))
    line_swaps = exchange(31, 2, (to_near, to_far, to_near_far))
    send_parts[1].wait_recv()
    in_grad[group] = (own_part + tn_recv[128:256, :].astype(F32)).astype(BF16)
    for swap in line_swaps:
        swap.wait_recv()
    sums[...] = (sum_buf[16:24, :] + received(4)) + (received(5) + received(6))

    send_lo.wait_recv()
    send_ig.wait_recv()
    for item in (
        *send_far,
        *pass_far_near,
        *pass_last,
        send_near,
        send_sib,
        pass_far_sib,
        pass_near_sib,
        send_og,
        swap_att,
        swap_ga,
        send_lo,
        *swap_parts,
        *send_parts,
        send_ig,
        *core_swaps,
        *plane_swaps,
        *line_swaps,
    ):
        item.wait_send()


def finish_kernel(layer_in, grad_in, sums, layer_out, in_grad, rank_total, out_total, norms):
    layer_out[...] = layer_in[...]
    in_grad[...] = grad_in[...]
    rank_rows = [jnp.concatenate([sums[k : k + 1], sums[k + 1 : k + 2]], axis=1) for k in (0, 2)]
    out_rows = [
        jnp.concatenate([sums[k : k + 1, 0:384], sums[k + 1 : k + 2, 0:384]], axis=1) for k in (4, 6)
    ]
    for k in range(2):
        rank_total[k : k + 1, :] = rank_rows[k]
        out_total[k : k + 1, :] = out_rows[k]
    for k, row in enumerate(rank_rows + out_rows):
        norms[k] = jnp.sqrt(jnp.sum(row * row, axis=1, keepdims=True))[0, 0]


def fast_body(
    tokens,
    attn_in_weight,
    out_weight,
    ffn_in_weight,
    ffn_out_weight,
    vera_in,
    vera_out,
    rank_scale,
    out_scale,
    gains,
    shifts,
    ffn_bias,
    splits,
    out_grad,
):
    hbm = pl.BlockSpec(memory_space=pl.ANY)
    vmem = pl.BlockSpec(memory_space=pltpu.VMEM)
    smem = pl.BlockSpec(memory_space=pltpu.SMEM)
    shape = tokens.shape
    small = (rank_scale, out_scale, gains, shifts, ffn_bias.reshape(1, -1))
    scratch = [
        ((1024, 768), BF16),
        ((256, 768), BF16),
        ((768, 1152), BF16),
        ((768, 768), BF16),
        ((768, 3072), BF16),
        ((3072, 768), BF16),
        ((768, 1024), BF16),
        ((1024, 384), BF16),
        ((384, 1024), BF16),
        ((1024, 1024), BF16),
        ((3, 1024, 256), BF16),
        ((6, 512, 256), BF16),
        ((3, 1024, 128), BF16),
        ((384, 1024), BF16),
        ((384, 1024), BF16),
        ((6, 1024, 512), BF16),
        ((2, 1024, 512), F32),
        ((384, 512), F32),
        ((4, 6, 1, 512), F32),
        ((4, 6, 1, 512), F32),
        ((4, 384, 512), F32),
        ((4, 6, 1, 512), F32),
        ((256, 384), BF16),
        ((256, 384), BF16),
        ((256, 768), F32),
        ((256, 768), F32),
        ((256, 3072), BF16),
        ((256, 768), BF16),
        ((256, 768), F32),
        ((256, 768), F32),
        ((128, 768), BF16),
        ((256, 384), BF16),
        ((256, 384), BF16),
        ((256, 384), BF16),
        ((6, 128, 512), BF16),
        ((6, 512, 128), BF16),
        ((6, 1, 512), F32),
        ((1024, 768), BF16),
        ((256, 768), F32),
        ((512, 768), BF16),
        ((512, 768), BF16),
        ((512, 768), F32),
        ((256, 768), F32),
        ((256, 768), BF16),
        ((256, 768), BF16),
        ((128, 768), BF16),
        ((24, 512), F32),
        ((56, 512), F32),
    ]
    rows_type = jax.ShapeDtypeStruct(shape, BF16)
    held_rows = pltpu.VMEM(shape, BF16)
    layer_rows, grad_rows, sums = pl.pallas_call(
        layer_kernel,
        out_shape=(held_rows, held_rows, pltpu.VMEM((8, 512), F32)),
        in_specs=[hbm] * 14,
        out_specs=(vmem, vmem, vmem),
        scratch_shapes=[pltpu.VMEM(item.shape, F32) for item in small]
        + [pltpu.SMEM(splits.shape, jnp.int32)]
        + [pltpu.VMEM(dims, kind) for dims, kind in scratch]
        + [
            pltpu.SemaphoreType.DMA((34,)),
            pltpu.SemaphoreType.DMA((34,)),
            pltpu.SemaphoreType.DMA((18,)),
        ],
        compiler_params=pltpu.CompilerParams(
            collective_id=0, has_side_effects=True, vmem_limit_bytes=60 * 2**20
        ),
        name="encoder_layer",
    )(
        tokens,
        attn_in_weight,
        out_weight,
        ffn_in_weight,
        ffn_out_weight,
        vera_in,
        vera_out,
        out_grad,
        *small,
        splits,
    )
    return pl.pallas_call(
        finish_kernel,
        out_shape=(
            rows_type,
            rows_type,
            jax.ShapeDtypeStruct(rank_scale.shape, F32),
            jax.ShapeDtypeStruct(out_scale.shape, F32),
            jax.ShapeDtypeStruct((4,), F32),
        ),
        in_specs=[vmem, vmem, vmem],
        out_specs=(vmem, vmem, vmem, vmem, smem),
        name="finish",
    )(*[pltpu.with_memory_space_constraint(x, pltpu.VMEM) for x in (layer_rows, grad_rows, sums)])


def solution(mesh):
    chosen = fast_body if fits(mesh) else body
    in_specs = (
        P("batch", "seq", None),
        P(),
        P(),
        P(),
        P(),
        P(),
        P(),
        P(),
        P(),
        P(),
        P(),
        P(),
        P("batch"),
        P("batch", "seq", None),
    )
    out_specs = (P("batch", "seq", None), P("batch", "seq", None), P(), P(), P())
    return jax.shard_map(chosen, mesh=mesh, in_specs=in_specs, out_specs=out_specs, check_vma=False)
```

```python
import functools

import jax
import jax.numpy as jnp
from jax import lax
from jax.experimental import pallas as pl
from jax.experimental.pallas import tpu as pltpu
from jax.sharding import PartitionSpec as P

HEADS = 12


masked_score = -1e30
key_block = 512


def product(left_side, right_side):
    return jnp.dot(left_side, right_side, preferred_element_type=jnp.float32)


def product_t(left_side, right_side):
    return lax.dot_general(
        left_side, right_side, (((1,), (1,)), ((), ())), preferred_element_type=jnp.float32
    )


def gelu_exact(inputs):
    return jax.nn.gelu(inputs, approximate=False)


def norm_forward(values_in, gain_row, shift_row):
    centered = values_in - jnp.mean(values_in, axis=-1, keepdims=True)
    inverse = lax.rsqrt(jnp.mean(centered * centered, axis=-1, keepdims=True) + 1e-05)
    normed = centered * inverse
    return (normed * gain_row + shift_row, normed, inverse)


def norm_backward(grad_in, normed, inverse, gain_row):
    scaled = grad_in * gain_row
    return inverse * (
        scaled
        - jnp.mean(scaled, axis=-1, keepdims=True)
        - normed * jnp.mean(scaled * normed, axis=-1, keepdims=True)
    )


def block_width():
    return key_block


def body(
    tokens,
    attn_in_weight,
    out_weight,
    ffn_in_weight,
    ffn_out_weight,
    vera_in,
    vera_out,
    rank_scale,
    out_scale,
    gains,
    shifts,
    ffn_bias,
    splits,
    out_grad,
):
    sequences, per_device, model_width = tokens.shape
    head_dim = model_width // HEADS
    score_scale = head_dim ** (-0.5)
    cycle_place = lax.axis_index("seq")
    token_rows = tokens.reshape(-1, model_width)
    token_float = token_rows.astype(jnp.float32)
    rank_in = product(token_rows, vera_in)
    rank_q = (rank_in * rank_scale[0]).astype(jnp.bfloat16)
    rank_v = (rank_in * rank_scale[1]).astype(jnp.bfloat16)
    wide_q = product(rank_q, vera_out)
    wide_v = product(rank_v, vera_out)
    projected = product(token_rows, attn_in_weight)
    query = projected[:, :model_width] + shifts[0] + out_scale[0] * wide_q
    keys = projected[:, model_width : 2 * model_width]
    values = projected[:, 2 * model_width :] + shifts[1] + out_scale[1] * wide_v
    query_low = query.astype(jnp.bfloat16).reshape(sequences, per_device, HEADS, head_dim)
    pair_low = (
        jnp.concatenate([keys, values], axis=-1)
        .astype(jnp.bfloat16)
        .reshape(sequences, per_device, 2 * model_width)
    )
    query_pos = cycle_place * per_device + jnp.arange(per_device, dtype=jnp.int32)
    query_side = query_pos[None, :] < splits[:, None]

    def block_scores(pair_piece, block_start):
        count_keys = pair_piece.shape[1]
        key_pos = block_start + jnp.arange(count_keys, dtype=jnp.int32)
        key_side = key_pos[None, :] < splits[:, None]
        allowed = (query_side[:, :, None] == key_side[:, None, :])[:, None]
        key_heads = pair_piece[:, :, :model_width].reshape(sequences, count_keys, HEADS, head_dim)
        value_heads = pair_piece[:, :, model_width:].reshape(sequences, count_keys, HEADS, head_dim)
        raw_scores = (
            jnp.einsum("sqhe,skhe->shqk", query_low, key_heads, preferred_element_type=jnp.float32)
            * score_scale
        )
        return (raw_scores, allowed, key_heads, value_heads)

    start_max = jnp.full((sequences, HEADS, per_device), masked_score, jnp.float32)
    start_sum = jnp.zeros((sequences, HEADS, per_device), jnp.float32)
    start_acc = jnp.zeros((sequences, per_device, HEADS, head_dim), jnp.float32)
    carry = (start_max, start_sum, start_acc)
    pair_piece = lax.all_gather(pair_low, "seq", axis=1, tiled=True)
    shard_start = jnp.int32(0)
    count_keys = pair_piece.shape[1]
    block_size = block_width()
    for absorb_block_index in range(count_keys // block_size):
        absorb_pair_piece = pair_piece[
            :, absorb_block_index * block_size : (absorb_block_index + 1) * block_size
        ]
        running_max, running_sum, absorb_accumulated = carry
        absorb_raw_scores, absorb_allowed, absorb_key_heads, absorb_value_heads = block_scores(
            absorb_pair_piece, shard_start + absorb_block_index * block_size
        )
        new_max = jnp.maximum(
            running_max,
            jnp.max(jnp.where(absorb_allowed, absorb_raw_scores, masked_score), axis=-1),
        )
        block_weights = jnp.where(
            absorb_allowed, jnp.exp(absorb_raw_scores - new_max[..., None]), 0.0
        )
        rescale = jnp.exp(running_max - new_max)
        running_sum = running_sum * rescale + jnp.sum(block_weights, axis=-1)
        added = jnp.einsum(
            "shqk,skhe->sqhe",
            block_weights.astype(jnp.bfloat16),
            absorb_value_heads,
            preferred_element_type=jnp.float32,
        )
        absorb_accumulated = (
            absorb_accumulated * jnp.transpose(rescale, (0, 2, 1))[..., None] + added
        )
        carry = (new_max, running_sum, absorb_accumulated)
    final_max, final_sum, accumulated = carry
    attended = accumulated / jnp.transpose(final_sum, (0, 2, 1))[..., None]
    log_total = final_max + jnp.log(final_sum)
    branch = product(attended.reshape(-1, model_width).astype(jnp.bfloat16), out_weight) + shifts[2]
    hidden, normed_one, inverse_one = norm_forward(token_float + branch, gains[0], shifts[4])
    inner = product(hidden.astype(jnp.bfloat16), ffn_in_weight) + ffn_bias
    activated, gelu_pull = jax.vjp(gelu_exact, inner)
    ffn_branch = product(activated.astype(jnp.bfloat16), ffn_out_weight) + shifts[3]
    layer_out, normed_two, inverse_two = norm_forward(hidden + ffn_branch, gains[1], shifts[5])
    grad_two = norm_backward(
        out_grad.reshape(-1, model_width).astype(jnp.float32), normed_two, inverse_two, gains[1]
    )
    grad_act = product_t(grad_two.astype(jnp.bfloat16), ffn_out_weight)
    grad_inner = gelu_pull(grad_act)[0].astype(jnp.bfloat16)
    grad_hidden = grad_two + product_t(grad_inner, ffn_in_weight)
    grad_one = norm_backward(grad_hidden, normed_one, inverse_one, gains[0])
    grad_att = (
        product_t(grad_one.astype(jnp.bfloat16), out_weight)
        .astype(jnp.bfloat16)
        .reshape(sequences, per_device, HEADS, head_dim)
    )
    delta = jnp.transpose(jnp.sum(grad_att.astype(jnp.float32) * attended, axis=-1), (0, 2, 1))
    grad_query = jnp.zeros((sequences, per_device, HEADS, head_dim), jnp.float32)
    whole_pairs = lax.all_gather(pair_low, "seq", axis=1, tiled=True)
    whole_len = whole_pairs.shape[1]
    block_size = block_width()
    key_terms = []
    for block_index in range(whole_len // block_size):
        block_pair_piece = whole_pairs[:, block_index * block_size : (block_index + 1) * block_size]
        block_raw_scores, block_allowed, block_key_heads, block_value_heads = block_scores(
            block_pair_piece, block_index * block_size
        )
        prob = jnp.where(block_allowed, jnp.exp(block_raw_scores - log_total[..., None]), 0.0)
        grad_prob = jnp.einsum(
            "sqhe,skhe->shqk", grad_att, block_value_heads, preferred_element_type=jnp.float32
        )
        grad_score = (prob * (grad_prob - delta[..., None])).astype(jnp.bfloat16)
        grad_value = jnp.einsum(
            "shqk,sqhe->skhe",
            prob.astype(jnp.bfloat16),
            grad_att,
            preferred_element_type=jnp.float32,
        )
        grad_key = (
            jnp.einsum("shqk,sqhe->skhe", grad_score, query_low, preferred_element_type=jnp.float32)
            * score_scale
        )
        query_part = (
            jnp.einsum(
                "shqk,skhe->sqhe", grad_score, block_key_heads, preferred_element_type=jnp.float32
            )
            * score_scale
        )
        block_count_keys = block_pair_piece.shape[1]
        pair_part = jnp.concatenate(
            [
                grad_key.reshape(sequences, block_count_keys, model_width),
                grad_value.reshape(sequences, block_count_keys, model_width),
            ],
            axis=-1,
        )
        query_part, pair_part = (query_part, pair_part)
        grad_query = grad_query + query_part
        key_terms.append(pair_part)
    pair_sum = lax.psum_scatter(
        jnp.concatenate(key_terms, axis=1), "seq", scatter_dimension=1, tiled=True
    )
    pair_grad_low = pair_sum.astype(jnp.bfloat16).reshape(-1, 2 * model_width)
    query_grad_low = grad_query.reshape(-1, model_width).astype(jnp.bfloat16)
    query_grad_float = query_grad_low.astype(jnp.float32)
    value_grad_float = pair_grad_low[:, model_width:].astype(jnp.float32)
    grad_wide_q = (query_grad_float * out_scale[0]).astype(jnp.bfloat16)
    grad_wide_v = (value_grad_float * out_scale[1]).astype(jnp.bfloat16)
    grad_rank_q = product_t(grad_wide_q, vera_out)
    grad_rank_v = product_t(grad_wide_v, vera_out)
    grad_rank_in = (grad_rank_q * rank_scale[0] + grad_rank_v * rank_scale[1]).astype(jnp.bfloat16)
    grad_tokens = (
        grad_one
        + product_t(jnp.concatenate([query_grad_low, pair_grad_low], axis=-1), attn_in_weight)
        + product_t(grad_rank_in, vera_in)
    )
    rank_terms = jnp.stack(
        [jnp.sum(grad_rank_q * rank_in, axis=0), jnp.sum(grad_rank_v * rank_in, axis=0)]
    )
    out_terms = jnp.stack(
        [jnp.sum(query_grad_float * wide_q, axis=0), jnp.sum(value_grad_float * wide_v, axis=0)]
    )
    rank_total, out_total = lax.psum((rank_terms, out_terms), ("batch", "seq"))
    scale_norms = jnp.concatenate(
        [
            jnp.sqrt(jnp.sum(rank_total * rank_total, axis=1)),
            jnp.sqrt(jnp.sum(out_total * out_total, axis=1)),
        ]
    )
    return (
        layer_out.astype(jnp.bfloat16).reshape(sequences, per_device, model_width),
        grad_tokens.astype(jnp.bfloat16).reshape(sequences, per_device, model_width),
        rank_total,
        out_total,
        scale_norms,
    )


MESH = pl.DeviceIdType.MESH
BIG = 1e30
F32 = jnp.float32
BF16 = jnp.bfloat16


def fits(mesh):
    return mesh.shape["seq"] == 8 and mesh.shape["batch"] == 4


def dot(left, right):
    return lax.dot_general(left, right, (((1,), (0,)), ((), ())), preferred_element_type=F32)


def dot_nt(left, right):
    return lax.dot_general(left, right, (((1,), (1,)), ((), ())), preferred_element_type=F32)


OWN, SIB, FAR, SIB_FAR, NEAR_FAR, SIB_NEAR_FAR, NEAR, SIB_NEAR = range(8)
PIECES = 4


def layer_kernel(
    tokens,
    attn_in,
    out_w,
    ffn_in,
    ffn_out,
    vera_in,
    vera_out,
    out_grad,
    rank_scale_in,
    out_scale_in,
    gains_in,
    shifts_in,
    ffn_bias_in,
    splits_in,
    layer_out,
    in_grad,
    sums,
    rank_scale,
    out_scale,
    gains,
    shifts,
    ffn_bias,
    splits,
    tok,
    og,
    w_all,
    w_out,
    w_one,
    w_two,
    v_in,
    v_out,
    v_out_t,
    rank_in,
    k_ext,
    q_ext,
    val,
    k_t,
    v_t,
    probs,
    s_buf,
    att_t,
    part_top,
    part_sum,
    part_out,
    share,
    att_send,
    att_recv,
    hid,
    n_one,
    wide,
    low_rows,
    g_two,
    g_one,
    lo_buf,
    ga_send,
    ga_recv,
    ga_mine,
    go_t,
    go_m,
    delta,
    d_kv,
    d_held,
    part_send,
    part_recv,
    part_mine,
    far_terms,
    tn_send,
    tn_recv,
    ig_buf,
    sum_buf,
    sum_recv,
    send_sem,
    recv_sem,
    load_sem,
):
    s = lax.axis_index("seq")
    b = lax.axis_index("batch")
    core = s % 2
    group = s // 4
    sib = s + 1 - 2 * core
    near = s + 2 - 4 * ((s // 2) % 2)
    far = s + 4 - 8 * group
    bx = b + 1 - 2 * (b % 2)
    by = b + 2 - 4 * (b // 2)
    half = pl.multiple_of(core * 384, 384)
    other_half = pl.multiple_of(384 - core * 384, 384)

    def remote(k, src, dst, where):
        return pltpu.make_async_remote_copy(
            src_ref=src,
            dst_ref=dst,
            send_sem=send_sem.at[k],
            recv_sem=recv_sem.at[k],
            device_id=where,
            device_id_type=MESH,
        )

    def local(k, src, dst):
        return pltpu.make_async_copy(src, dst, load_sem.at[k])

    def block(ref, k, n=1):
        return ref.at[pl.ds(128 * k, 128 * n)]

    near_far = far + near - s
    to_sib, to_near, to_far = {"seq": sib}, {"seq": near}, {"seq": far}
    to_near_far = {"seq": near_far}
    to_bx, to_by, to_bxy = {"batch": bx}, {"batch": by}, {"batch": bx + by - b}

    barrier = pltpu.get_barrier_semaphore()
    for where in (to_sib, to_near, to_far, to_near_far, to_bx, to_by, to_bxy):
        pl.semaphore_signal(barrier, inc=1, device_id=where, device_id_type=MESH)

    loads = [
        local(0, tokens.at[group], block(tok, OWN)),
        local(1, vera_in, v_in),
        local(2, vera_out.at[:, pl.ds(half, 384)], v_out),
        local(3, attn_in.at[:, pl.ds(half, 384)], w_all.at[:, pl.ds(0, 384)]),
        local(4, attn_in.at[:, pl.ds(768 + half, 384)], w_all.at[:, pl.ds(384, 384)]),
        local(5, attn_in.at[:, pl.ds(1536 + half, 384)], w_all.at[:, pl.ds(768, 384)]),
        local(6, out_w, w_out),
        local(7, ffn_in, w_one),
        local(8, ffn_out, w_two),
        local(9, out_grad.at[group], og.at[pl.ds(0, 128)]),
    ]
    small_loads = [
        local(12, rank_scale_in, rank_scale),
        local(13, out_scale_in, out_scale),
        local(14, gains_in, gains),
        local(15, shifts_in, shifts),
        local(16, ffn_bias_in, ffn_bias),
        local(17, splits_in, splits),
    ]
    for item in (*loads[1:6], *small_loads, loads[0]):
        item.start()
    pl.semaphore_wait(barrier, 7)

    piece = 128 // PIECES
    send_far, pass_far_near, pass_last = [], [], []
    for k in range(PIECES):
        part = pl.ds(128 * FAR + piece * k, piece)
        near_part = pl.ds(128 * NEAR_FAR + piece * k, piece)
        last_part = pl.ds(128 * SIB_NEAR_FAR + piece * k, piece)
        send_far.append(
            remote(k, tokens.at[1 - group, pl.ds(piece * k, piece)], tok.at[part], to_far)
        )
        pass_far_near.append(remote(PIECES + k, tok.at[part], tok.at[near_part], to_near))
        pass_last.append(remote(2 * PIECES + k, tok.at[near_part], tok.at[last_part], to_sib))
    send_near = remote(12, tokens.at[group], block(tok, NEAR), to_near)
    send_sib = remote(13, tokens.at[group], block(tok, SIB), to_sib)
    pass_far_sib = remote(14, block(tok, FAR), block(tok, SIB_FAR), to_sib)
    pass_near_sib = remote(15, block(tok, NEAR), block(tok, SIB_NEAR), to_sib)
    send_og = remote(16, out_grad.at[1 - group], og.at[pl.ds(128, 128)], to_far)
    outer = (s // 2) % 2 == group
    inner = jnp.logical_not(outer)

    def start_far():
        for item in send_far:
            item.start()

    pl.when(outer)(start_far)
    pl.when(inner)(send_near.start)
    send_sib.start()

    for item in (*small_loads, *loads[1:6]):
        item.wait()
    for item in loads[6:10]:
        item.start()
    for row, at in ((0, 0), (1, 768)):
        scale_row = rank_scale[pl.ds(row, 1), :]
        out_row = out_scale[pl.ds(row, 1), pl.ds(half, 384)]

        def effective(t, _, at=at, scale_row=scale_row, out_row=out_row):
            rows = pl.ds(pl.multiple_of(t * 256, 256), 256)
            scaled = (v_in[rows, :].astype(F32) * scale_row).astype(BF16)
            wide = dot(scaled, v_out[...]) * out_row
            w_all[rows, at : at + 384] = (w_all[rows, at : at + 384].astype(F32) + wide).astype(BF16)
            return 0

        lax.fori_loop(0, 3, effective, 0)
    v_out_t[...] = v_out[...].astype(F32).T.astype(BF16)

    split = splits[group]
    lane = lax.broadcasted_iota(jnp.int32, (128, 128), 1)
    row_at = lax.broadcasted_iota(jnp.int32, (128, 128), 0)
    flip_one, flip_two, flip_four = sib - s, near - s, far - s
    starts = (
        s,
        s + flip_one,
        s + flip_four,
        s + flip_four + flip_one,
        s + flip_two + flip_four,
        s + flip_two + flip_four + flip_one,
        s + flip_two,
        s + flip_two + flip_one,
    )
    for k in range(8):
        first = (starts[k] * 128 + row_at < split).astype(F32)
        second = 1.0 - first
        key_side = jnp.where(lane == 0, first, jnp.where(lane == 1, second, 0.0)).astype(BF16)
        for p in range(3):
            k_ext[p, 128 * k : 128 * k + 128, 128:256] = key_side
        if k < 4:
            query_side = (
                jnp.where(lane == 0, second, jnp.where(lane == 1, first, 0.0)) * (-BIG)
            ).astype(BF16)
            for h in range(6):
                q_ext[h, 128 * k : 128 * k + 128, 128:256] = query_side

    pl.when(outer)(send_near.start)

    shift_q = shifts[0:1, pl.ds(half, 384)]
    shift_v = shifts[1:2, pl.ds(half, 384)]
    low_lane = lax.broadcasted_iota(jnp.int32, (256, 128), 1) < 64

    def project(first, queries, count=256):
        to = slice(128 * first, 128 * first + count)
        rows = tok[to, :]
        made = dot(rows, w_all[...] if queries else w_all[:, 384:1152])
        keys = made[:, made.shape[1] - 768 : made.shape[1] - 384]
        values = made[:, made.shape[1] - 384 :] + shift_v
        low_keys = keys.astype(BF16)
        low_values = values.astype(BF16)
        for p in range(3):
            k_ext[p, to, 0:128] = low_keys[:, 128 * p : 128 * p + 128]
            val[p, to, :] = low_values[:, 128 * p : 128 * p + 128]
        k_t[:, to] = keys.T.astype(BF16)
        v_t[:, to] = values.T.astype(BF16)
        if queries:
            query = made[:, 0:384] + shift_q
            low_query = query.astype(BF16).astype(F32) * 0.125
            for h in range(6):
                p = h // 2
                mine = low_lane if h % 2 == 0 else jnp.logical_not(low_lane)
                masked = jnp.where(mine, low_query[:, 128 * p : 128 * p + 128], 0.0)
                q_ext[h, to, 0:128] = masked.astype(BF16)

    def attend(blocks, first_query, count):
        queries = slice(first_query, first_query + count)
        part_at = blocks[0] // 2
        starts_at = [128 * first for first in blocks]
        peaks, totals, outs = {}, {}, {}

        def scores(h, at):
            part = dot_nt(k_ext[h // 2, at : at + 256, :], q_ext[h, queries, :])
            s_buf[h % 2, at : at + 256, queries] = part
            peak = jnp.max(part, axis=0, keepdims=True)
            peaks[h] = jnp.maximum(peaks[h], peak) if h in peaks else peak

        def weights(h, at):
            weight = jnp.exp(s_buf[h % 2, at : at + 256, queries] - peaks[h])
            total = jnp.sum(weight, axis=0, keepdims=True)
            low_weight = weight.astype(BF16)
            probs[h, at : at + 256, queries] = low_weight
            out = dot(v_t[64 * h : 64 * h + 64, at : at + 256], low_weight)
            totals[h] = totals[h] + total if h in totals else total
            outs[h] = outs[h] + out if h in outs else out

        for at in starts_at:
            scores(0, at)
        for h in range(6):
            for at in starts_at:
                if h < 5:
                    scores(h + 1, at)
                weights(h, at)
            part_top[part_at, h, :, queries] = peaks[h]
            part_sum[part_at, h, :, queries] = totals[h]
            part_out[part_at, 64 * h : 64 * h + 64, queries] = outs[h]

    def combine(first_query, groups):
        queries = slice(first_query, first_query + 256)
        for h in range(6):
            rows_h = slice(64 * h, 64 * h + 64)
            parts = [group_of[0] // 2 for group_of in groups]
            tops = [part_top[k, h, :, queries] for k in parts]
            top = functools.reduce(jnp.maximum, tops)
            shares = [jnp.exp(one - top) for one in tops]
            total = functools.reduce(
                jnp.add, [w * part_sum[k, h, :, queries] for w, k in zip(shares, parts)]
            )
            inverse = 1.0 / total
            shares = [w * inverse for w in shares]
            att_t[rows_h, queries] = functools.reduce(
                jnp.add, [w * part_out[k, rows_h, queries] for w, k in zip(shares, parts)]
            )
            for w, group_of in zip(shares, groups):
                for first in group_of:
                    share[first // 2, h, :, queries] = w

    def rank_rows(first):
        to = slice(128 * first, 128 * first + 256)
        rank_in[to, :] = dot(tok[to, :], v_in[...]).astype(BF16)

    def pass_far():
        for k in range(PIECES):
            send_far[k].wait_recv()
            pass_far_near[k].start()
        pass_far_sib.start()

    def near_blocks():
        send_near.wait_recv()
        pass_near_sib.start()
        pass_near_sib.wait_recv()
        project(NEAR, False)

    def far_blocks():
        pass_far_sib.wait_recv()
        project(FAR, True)

    def pass_last_on():
        for k in range(PIECES):
            pass_far_near[k].wait_recv()
            pass_last[k].start()

    def last_blocks():
        project(NEAR_FAR, False, 128)
        for k in range(PIECES):
            pass_last[k].wait_recv()
        project(SIB_NEAR_FAR, False, 128)

    loads[0].wait()
    send_sib.wait_recv()
    project(OWN, True)
    rank_rows(OWN)
    pl.when(inner)(start_far)
    attend((OWN,), 0, 256)

    @pl.when(inner)
    def _():
        pass_far()
        far_blocks()
        attend((FAR,), 0, 256)
        attend((OWN, FAR), 256, 256)
        near_blocks()
        attend((NEAR,), 0, 512)
        rank_rows(NEAR)
        pass_last_on()
        send_og.start()
        last_blocks()
        attend((NEAR_FAR,), 0, 512)
        combine(0, ((OWN,), (FAR,), (NEAR,), (NEAR_FAR,)))
        combine(256, ((OWN, FAR), (NEAR,), (NEAR_FAR,)))

    @pl.when(outer)
    def _():
        near_blocks()
        attend((NEAR,), 0, 256)
        pass_far()
        rank_rows(NEAR)
        far_blocks()
        attend((FAR,), 0, 256)
        attend((OWN, FAR, NEAR), 256, 256)
        pass_last_on()
        send_og.start()
        last_blocks()
        attend((NEAR_FAR,), 0, 512)
        combine(0, ((OWN,), (FAR,), (NEAR,), (NEAR_FAR,)))
        combine(256, ((OWN, FAR, NEAR), (NEAR_FAR,)))

    swap_att = remote(17, att_send, att_recv, to_sib)
    for k, at in ((0, 128 * SIB), (128, 128 * SIB_FAR)):
        att_send[k : k + 128, :] = att_t[:, at : at + 128].T.astype(BF16)
    swap_att.start()

    def norm(values_in):
        centered = values_in - jnp.mean(values_in, axis=-1, keepdims=True)
        inverse = lax.rsqrt(jnp.mean(centered * centered, axis=-1, keepdims=True) + 1e-05)
        return centered * inverse, inverse

    def norm_back(grad_in, normed, inverse, gain_row):
        scaled = grad_in * gain_row
        return inverse * (
            scaled
            - jnp.mean(scaled, axis=-1, keepdims=True)
            - normed * jnp.mean(scaled * normed, axis=-1, keepdims=True)
        )

    loads[6].wait()
    attended_mine = jnp.concatenate([att_t[:, 0:128], att_t[:, 256:384]], axis=1).T
    token_rows = jnp.concatenate([tok[0:128, :], tok[256:384, :]], axis=0).astype(F32)
    branch = dot(attended_mine.astype(BF16), w_out[pl.ds(half, 384), :])
    rank_rows(FAR)
    rank_rows(NEAR_FAR)
    swap_att.wait_recv()
    branch = branch + dot(att_recv[...], w_out[pl.ds(other_half, 384), :]) + shifts[2:3, :]
    normed_one, inverse_one = norm(token_rows + branch)
    n_one[...] = normed_one
    hidden = normed_one * gains[0:1, :] + shifts[4:5, :]
    hid[...] = hidden
    low_rows[...] = hidden.astype(BF16)

    loads[7].wait()
    loads[8].wait()
    def slope(t):
        return s_buf.at[t // 2048, pl.ds(t % 2048 // 2, 256)]

    for t in range(0, 3072, 512):
        cols = slice(t, t + 512)
        inner = dot(low_rows[...], w_one[:, cols]) + ffn_bias[:, cols]
        phi = 0.5 * (1.0 + lax.erf(inner * 0.7071067811865476))
        density = 0.3989422804014327 * jnp.exp(-0.5 * inner * inner)
        slope(t)[...] = phi + inner * density
        wide[:, cols] = (inner * phi).astype(BF16)
    ffn_branch = dot(wide[...], w_two[...])
    normed_two, inverse_two = norm(hid[...] + ffn_branch + shifts[3:4, :])
    out_rows = (normed_two * gains[1:2, :] + shifts[5:6, :]).astype(BF16)
    lo_buf[...] = out_rows[128:256]
    send_lo = remote(18, lo_buf, layer_out.at[group], to_far)
    send_lo.start()
    layer_out[group] = out_rows[0:128]
    loads[9].wait()
    send_og.wait_recv()
    grad_two = norm_back(og[...].astype(F32), normed_two, inverse_two, gains[1:2, :])
    g_two[...] = grad_two
    low_rows[...] = grad_two.astype(BF16)
    for t in range(0, 3072, 512):
        cols = slice(t, t + 512)
        grad_act = dot_nt(low_rows[...], w_two[cols, :])
        wide[:, cols] = (grad_act * slope(t)[...]).astype(BF16)
    grad_hidden = g_two[...] + dot_nt(wide[...], w_one[...])
    grad_one = norm_back(grad_hidden, n_one[...], inverse_one, gains[0:1, :])
    g_one[...] = grad_one
    low_one = grad_one.astype(BF16)
    swap_ga = remote(19, ga_send, ga_recv, to_sib)
    ga_send[...] = dot_nt(low_one, w_out[pl.ds(other_half, 384), :]).astype(BF16)
    swap_ga.start()
    ga_mine[...] = dot_nt(low_one, w_out[pl.ds(half, 384), :]).astype(BF16)

    low_row = lax.broadcasted_iota(jnp.int32, (128, 128), 0) < 64
    low_col = lax.broadcasted_iota(jnp.int32, (128, 128), 1) < 64

    def spread(block_at, rows):
        to = slice(128 * block_at, 128 * block_at + 128)
        flipped = rows.T
        for p in range(3):
            cols = slice(128 * p, 128 * p + 128)
            for e in range(2):
                h = 2 * p + e
                rows_of = low_row if e == 0 else jnp.logical_not(low_row)
                cols_of = low_col if e == 0 else jnp.logical_not(low_col)
                go_m[h, to, :] = jnp.where(cols_of, rows[:, cols], 0.0).astype(BF16)
                mine = jnp.where(rows_of, flipped[cols, :], 0.0)
                go_t[h, :, to] = mine.astype(BF16)
                delta[h, :, to] = jnp.sum(mine * att_t[cols, to], axis=0, keepdims=True)

    spread(OWN, ga_mine[0:128, :].astype(F32))
    spread(FAR, ga_mine[128:256, :].astype(F32))
    swap_ga.wait_recv()
    spread(SIB, ga_recv[0:128, :].astype(F32))
    spread(SIB_FAR, ga_recv[128:256, :].astype(F32))

    dq_t = part_out.at[0]

    def backward(first, first_query, count, heads=range(6)):
        rows = slice(128 * first, 128 * first + 256)
        queries = slice(first_query, first_query + count)

        def value_dots(h):
            return dot(val[h // 2, rows, :], go_t[h, :, queries])

        grad_prob = value_dots(heads[0])
        for h in heads:
            following = value_dots(h + 1) if h + 1 in heads else None
            weight = probs[h, rows, queries].astype(F32) * share[first // 2, h, :, queries]
            grad_score = (weight * (grad_prob - delta[h, :, queries])).astype(BF16)
            value_part = dot(weight.astype(BF16), go_m[h, queries, :])
            key_part = dot(grad_score, q_ext[h, queries, 0:128])
            rows_h = slice(64 * h, 64 * h + 64)
            query_part = dot(k_t[rows_h, rows], grad_score)
            if first == NEAR_FAR:
                dq_t[rows_h, queries] = query_part
            else:
                dq_t[rows_h, queries] += query_part
            if h % 2 == 0:
                grad_values, grad_keys = value_part, key_part
            else:
                grad_values, grad_keys = grad_values + value_part, grad_keys + key_part
                cols = slice(64 * h - 64, 64 * h + 64)
                value_cols = slice(64 * h + 320, 64 * h + 448)
                if count == 512:
                    d_kv[rows, cols] = grad_keys.astype(BF16)
                    d_kv[rows, value_cols] = grad_values.astype(BF16)
                elif first_query == 256:
                    d_held[:, cols] = grad_keys
                    d_held[:, value_cols] = grad_values
                else:
                    d_kv[rows, cols] = (d_held[:, cols] + grad_keys).astype(BF16)
                    d_kv[rows, value_cols] = (d_held[:, value_cols] + grad_values).astype(BF16)
            grad_prob = following

    def token_terms(start):
        return dot_nt(d_kv[start : start + 256, :], w_all[:, 384:1152])

    swap_parts = [
        remote(20 + k, part_send.at[pl.ds(128 * k, 128)], part_recv.at[pl.ds(128 * k, 128)], to_sib)
        for k in range(4)
    ]
    send_parts = [
        remote(24 + k, tn_send.at[pl.ds(128 * k, 128)], tn_recv.at[pl.ds(128 * k, 128)], to_near)
        for k in range(2)
    ]

    def share_out(k, terms):
        part_send[128 * k : 128 * k + 128, :] = terms[128:256].astype(BF16)
        swap_parts[k].start()
        part_mine[128 * k : 128 * k + 128, :] = terms[0:128]

    def shared(k):
        swap_parts[k].wait_recv()
        rows = slice(128 * k, 128 * k + 128)
        return part_mine[rows, :] + part_recv[rows, :].astype(F32)

    def pass_on(k):
        tn_send[128 * k : 128 * k + 128, :] = shared(k).astype(BF16)
        send_parts[k].start()

    backward(NEAR_FAR, 0, 512)
    share_out(0, token_terms(128 * NEAR_FAR))
    backward(NEAR, 0, 512, range(0, 2))
    pass_on(0)
    backward(NEAR, 0, 512, range(2, 6))
    share_out(1, token_terms(128 * NEAR))
    backward(FAR, 0, 512)
    pass_on(1)
    far_terms[...] = token_terms(128 * FAR)
    backward(OWN, 256, 256)
    low_dq_far = (dq_t[:, 256:512] * 0.125).T.astype(BF16)
    share_out(2, far_terms[...] + dot_nt(low_dq_far, w_all[:, 0:384]))
    backward(OWN, 0, 256)
    far_part = shared(2) + g_one[128:256, :]
    send_parts[0].wait_recv()
    ig_buf[...] = (far_part + tn_recv[0:128, :].astype(F32)).astype(BF16)
    send_ig = remote(26, ig_buf, in_grad.at[group], to_far)
    send_ig.start()

    low_dq_t = (dq_t[...] * 0.125).astype(BF16)
    low_dv_t = d_kv[:, 384:768].astype(F32).T.astype(BF16)
    rank_parts, out_parts = [], []
    for row, product_map in (
        (0, dot(low_dq_t, rank_in[0:512, :])),
        (1, dot(low_dv_t, rank_in[...])),
    ):
        product_map = product_map * v_out_t[...].astype(F32)
        out_row = out_scale[pl.ds(row, 1), pl.ds(half, 384)]
        out_col = jnp.broadcast_to(out_row, (128, 384)).T[:, 0:1]
        rank_part = jnp.sum(product_map * out_col, axis=0, keepdims=True)
        rank_parts += [rank_part[:, 0:512], rank_part[:, 512:1024]]
        out_part = jnp.sum(product_map * rank_scale[pl.ds(row, 1), :], axis=1, keepdims=True)
        out_part = jnp.broadcast_to(out_part, (384, 128)).T[0:1, :]
        out_part = jnp.concatenate([out_part, jnp.zeros((1, 128), F32)], axis=1)
        out_parts += [jnp.where(core == 0, out_part, 0.0), jnp.where(core == 1, out_part, 0.0)]
    for k, part in enumerate(rank_parts + out_parts):
        sum_buf[k : k + 1, :] = part

    def exchange(k, stage, wheres):
        swaps = [
            remote(
                k + n,
                sum_buf.at[pl.ds(8 * stage, 8)],
                sum_recv.at[pl.ds(8 * (k - 27 + n), 8)],
                where,
            )
            for n, where in enumerate(wheres)
        ]
        for swap in swaps:
            swap.start()
        return swaps

    def received(k):
        return sum_recv[8 * k : 8 * k + 8, :]

    core_swaps = exchange(27, 0, (to_sib,))
    low_dq = (dq_t[:, 0:256] * 0.125).T.astype(BF16)
    share_out(3, token_terms(128 * OWN) + dot_nt(low_dq, w_all[:, 0:384]))
    core_swaps[0].wait_recv()
    sum_buf[8:16, :] = sum_buf[0:8, :] + received(0)
    plane_swaps = exchange(28, 1, (to_bx, to_by, to_bxy))
    own_part = shared(3) + g_one[0:128, :]
    for swap in plane_swaps:
        swap.wait_recv()
    sum_buf[16:24, :] = (sum_buf[8:16, :] + received(1)) + (received(2) + received(3))
    line_swaps = exchange(31, 2, (to_near, to_far, to_near_far))
    send_parts[1].wait_recv()
    in_grad[group] = (own_part + tn_recv[128:256, :].astype(F32)).astype(BF16)
    for swap in line_swaps:
        swap.wait_recv()
    sums[...] = (sum_buf[16:24, :] + received(4)) + (received(5) + received(6))

    send_lo.wait_recv()
    send_ig.wait_recv()
    for item in (
        *send_far,
        *pass_far_near,
        *pass_last,
        send_near,
        send_sib,
        pass_far_sib,
        pass_near_sib,
        send_og,
        swap_att,
        swap_ga,
        send_lo,
        *swap_parts,
        *send_parts,
        send_ig,
        *core_swaps,
        *plane_swaps,
        *line_swaps,
    ):
        item.wait_send()


def finish_kernel(layer_in, grad_in, sums, layer_out, in_grad, rank_total, out_total, norms):
    layer_out[...] = layer_in[...]
    in_grad[...] = grad_in[...]
    rank_rows = [jnp.concatenate([sums[k : k + 1], sums[k + 1 : k + 2]], axis=1) for k in (0, 2)]
    out_rows = [
        jnp.concatenate([sums[k : k + 1, 0:384], sums[k + 1 : k + 2, 0:384]], axis=1) for k in (4, 6)
    ]
    for k in range(2):
        rank_total[k : k + 1, :] = rank_rows[k]
        out_total[k : k + 1, :] = out_rows[k]
    for k, row in enumerate(rank_rows + out_rows):
        norms[k] = jnp.sqrt(jnp.sum(row * row, axis=1, keepdims=True))[0, 0]


def fast_body(
    tokens,
    attn_in_weight,
    out_weight,
    ffn_in_weight,
    ffn_out_weight,
    vera_in,
    vera_out,
    rank_scale,
    out_scale,
    gains,
    shifts,
    ffn_bias,
    splits,
    out_grad,
):
    hbm = pl.BlockSpec(memory_space=pl.ANY)
    vmem = pl.BlockSpec(memory_space=pltpu.VMEM)
    smem = pl.BlockSpec(memory_space=pltpu.SMEM)
    shape = tokens.shape
    small = (rank_scale, out_scale, gains, shifts, ffn_bias.reshape(1, -1))
    scratch = [
        ((1024, 768), BF16),
        ((256, 768), BF16),
        ((768, 1152), BF16),
        ((768, 768), BF16),
        ((768, 3072), BF16),
        ((3072, 768), BF16),
        ((768, 1024), BF16),
        ((1024, 384), BF16),
        ((384, 1024), BF16),
        ((1024, 1024), BF16),
        ((3, 1024, 256), BF16),
        ((6, 512, 256), BF16),
        ((3, 1024, 128), BF16),
        ((384, 1024), BF16),
        ((384, 1024), BF16),
        ((6, 1024, 512), BF16),
        ((2, 1024, 512), F32),
        ((384, 512), F32),
        ((4, 6, 1, 512), F32),
        ((4, 6, 1, 512), F32),
        ((4, 384, 512), F32),
        ((4, 6, 1, 512), F32),
        ((256, 384), BF16),
        ((256, 384), BF16),
        ((256, 768), F32),
        ((256, 768), F32),
        ((256, 3072), BF16),
        ((256, 768), BF16),
        ((256, 768), F32),
        ((256, 768), F32),
        ((128, 768), BF16),
        ((256, 384), BF16),
        ((256, 384), BF16),
        ((256, 384), BF16),
        ((6, 128, 512), BF16),
        ((6, 512, 128), BF16),
        ((6, 1, 512), F32),
        ((1024, 768), BF16),
        ((256, 768), F32),
        ((512, 768), BF16),
        ((512, 768), BF16),
        ((512, 768), F32),
        ((256, 768), F32),
        ((256, 768), BF16),
        ((256, 768), BF16),
        ((128, 768), BF16),
        ((24, 512), F32),
        ((56, 512), F32),
    ]
    rows_type = jax.ShapeDtypeStruct(shape, BF16)
    held_rows = pltpu.VMEM(shape, BF16)
    layer_rows, grad_rows, sums = pl.pallas_call(
        layer_kernel,
        out_shape=(held_rows, held_rows, pltpu.VMEM((8, 512), F32)),
        in_specs=[hbm] * 14,
        out_specs=(vmem, vmem, vmem),
        scratch_shapes=[pltpu.VMEM(item.shape, F32) for item in small]
        + [pltpu.SMEM(splits.shape, jnp.int32)]
        + [pltpu.VMEM(dims, kind) for dims, kind in scratch]
        + [
            pltpu.SemaphoreType.DMA((34,)),
            pltpu.SemaphoreType.DMA((34,)),
            pltpu.SemaphoreType.DMA((18,)),
        ],
        compiler_params=pltpu.CompilerParams(
            collective_id=0, has_side_effects=True, vmem_limit_bytes=60 * 2**20
        ),
        name="encoder_layer",
    )(
        tokens,
        attn_in_weight,
        out_weight,
        ffn_in_weight,
        ffn_out_weight,
        vera_in,
        vera_out,
        out_grad,
        *small,
        splits,
    )
    return pl.pallas_call(
        finish_kernel,
        out_shape=(
            rows_type,
            rows_type,
            jax.ShapeDtypeStruct(rank_scale.shape, F32),
            jax.ShapeDtypeStruct(out_scale.shape, F32),
            jax.ShapeDtypeStruct((4,), F32),
        ),
        in_specs=[vmem, vmem, vmem],
        out_specs=(vmem, vmem, vmem, vmem, smem),
        name="finish",
    )(*[pltpu.with_memory_space_constraint(x, pltpu.VMEM) for x in (layer_rows, grad_rows, sums)])


def solution(mesh):
    chosen = fast_body if fits(mesh) else body
    in_specs = (
        P("batch", "seq", None),
        P(),
        P(),
        P(),
        P(),
        P(),
        P(),
        P(),
        P(),
        P(),
        P(),
        P(),
        P("batch"),
        P("batch", "seq", None),
    )
    out_specs = (P("batch", "seq", None), P("batch", "seq", None), P(), P(), P())
    return jax.shard_map(chosen, mesh=mesh, in_specs=in_specs, out_specs=out_specs, check_vma=False)
```

```python
import functools

import jax
import jax.numpy as jnp
from jax import lax
from jax.experimental import pallas as pl
from jax.experimental.pallas import tpu as pltpu
from jax.sharding import PartitionSpec as P

HEADS = 12


masked_score = -1e30
key_block = 512


def product(left_side, right_side):
    return jnp.dot(left_side, right_side, preferred_element_type=jnp.float32)


def product_t(left_side, right_side):
    return lax.dot_general(
        left_side, right_side, (((1,), (1,)), ((), ())), preferred_element_type=jnp.float32
    )


def gelu_exact(inputs):
    return jax.nn.gelu(inputs, approximate=False)


def norm_forward(values_in, gain_row, shift_row):
    centered = values_in - jnp.mean(values_in, axis=-1, keepdims=True)
    inverse = lax.rsqrt(jnp.mean(centered * centered, axis=-1, keepdims=True) + 1e-05)
    normed = centered * inverse
    return (normed * gain_row + shift_row, normed, inverse)


def norm_backward(grad_in, normed, inverse, gain_row):
    scaled = grad_in * gain_row
    return inverse * (
        scaled
        - jnp.mean(scaled, axis=-1, keepdims=True)
        - normed * jnp.mean(scaled * normed, axis=-1, keepdims=True)
    )


def block_width():
    return key_block


def body(
    tokens,
    attn_in_weight,
    out_weight,
    ffn_in_weight,
    ffn_out_weight,
    vera_in,
    vera_out,
    rank_scale,
    out_scale,
    gains,
    shifts,
    ffn_bias,
    splits,
    out_grad,
):
    sequences, per_device, model_width = tokens.shape
    head_dim = model_width // HEADS
    score_scale = head_dim ** (-0.5)
    cycle_place = lax.axis_index("seq")
    token_rows = tokens.reshape(-1, model_width)
    token_float = token_rows.astype(jnp.float32)
    rank_in = product(token_rows, vera_in)
    rank_q = (rank_in * rank_scale[0]).astype(jnp.bfloat16)
    rank_v = (rank_in * rank_scale[1]).astype(jnp.bfloat16)
    wide_q = product(rank_q, vera_out)
    wide_v = product(rank_v, vera_out)
    projected = product(token_rows, attn_in_weight)
    query = projected[:, :model_width] + shifts[0] + out_scale[0] * wide_q
    keys = projected[:, model_width : 2 * model_width]
    values = projected[:, 2 * model_width :] + shifts[1] + out_scale[1] * wide_v
    query_low = query.astype(jnp.bfloat16).reshape(sequences, per_device, HEADS, head_dim)
    pair_low = (
        jnp.concatenate([keys, values], axis=-1)
        .astype(jnp.bfloat16)
        .reshape(sequences, per_device, 2 * model_width)
    )
    query_pos = cycle_place * per_device + jnp.arange(per_device, dtype=jnp.int32)
    query_side = query_pos[None, :] < splits[:, None]

    def block_scores(pair_piece, block_start):
        count_keys = pair_piece.shape[1]
        key_pos = block_start + jnp.arange(count_keys, dtype=jnp.int32)
        key_side = key_pos[None, :] < splits[:, None]
        allowed = (query_side[:, :, None] == key_side[:, None, :])[:, None]
        key_heads = pair_piece[:, :, :model_width].reshape(sequences, count_keys, HEADS, head_dim)
        value_heads = pair_piece[:, :, model_width:].reshape(sequences, count_keys, HEADS, head_dim)
        raw_scores = (
            jnp.einsum("sqhe,skhe->shqk", query_low, key_heads, preferred_element_type=jnp.float32)
            * score_scale
        )
        return (raw_scores, allowed, key_heads, value_heads)

    start_max = jnp.full((sequences, HEADS, per_device), masked_score, jnp.float32)
    start_sum = jnp.zeros((sequences, HEADS, per_device), jnp.float32)
    start_acc = jnp.zeros((sequences, per_device, HEADS, head_dim), jnp.float32)
    carry = (start_max, start_sum, start_acc)
    pair_piece = lax.all_gather(pair_low, "seq", axis=1, tiled=True)
    shard_start = jnp.int32(0)
    count_keys = pair_piece.shape[1]
    block_size = block_width()
    for absorb_block_index in range(count_keys // block_size):
        absorb_pair_piece = pair_piece[
            :, absorb_block_index * block_size : (absorb_block_index + 1) * block_size
        ]
        running_max, running_sum, absorb_accumulated = carry
        absorb_raw_scores, absorb_allowed, absorb_key_heads, absorb_value_heads = block_scores(
            absorb_pair_piece, shard_start + absorb_block_index * block_size
        )
        new_max = jnp.maximum(
            running_max,
            jnp.max(jnp.where(absorb_allowed, absorb_raw_scores, masked_score), axis=-1),
        )
        block_weights = jnp.where(
            absorb_allowed, jnp.exp(absorb_raw_scores - new_max[..., None]), 0.0
        )
        rescale = jnp.exp(running_max - new_max)
        running_sum = running_sum * rescale + jnp.sum(block_weights, axis=-1)
        added = jnp.einsum(
            "shqk,skhe->sqhe",
            block_weights.astype(jnp.bfloat16),
            absorb_value_heads,
            preferred_element_type=jnp.float32,
        )
        absorb_accumulated = (
            absorb_accumulated * jnp.transpose(rescale, (0, 2, 1))[..., None] + added
        )
        carry = (new_max, running_sum, absorb_accumulated)
    final_max, final_sum, accumulated = carry
    attended = accumulated / jnp.transpose(final_sum, (0, 2, 1))[..., None]
    log_total = final_max + jnp.log(final_sum)
    branch = product(attended.reshape(-1, model_width).astype(jnp.bfloat16), out_weight) + shifts[2]
    hidden, normed_one, inverse_one = norm_forward(token_float + branch, gains[0], shifts[4])
    inner = product(hidden.astype(jnp.bfloat16), ffn_in_weight) + ffn_bias
    activated, gelu_pull = jax.vjp(gelu_exact, inner)
    ffn_branch = product(activated.astype(jnp.bfloat16), ffn_out_weight) + shifts[3]
    layer_out, normed_two, inverse_two = norm_forward(hidden + ffn_branch, gains[1], shifts[5])
    grad_two = norm_backward(
        out_grad.reshape(-1, model_width).astype(jnp.float32), normed_two, inverse_two, gains[1]
    )
    grad_act = product_t(grad_two.astype(jnp.bfloat16), ffn_out_weight)
    grad_inner = gelu_pull(grad_act)[0].astype(jnp.bfloat16)
    grad_hidden = grad_two + product_t(grad_inner, ffn_in_weight)
    grad_one = norm_backward(grad_hidden, normed_one, inverse_one, gains[0])
    grad_att = (
        product_t(grad_one.astype(jnp.bfloat16), out_weight)
        .astype(jnp.bfloat16)
        .reshape(sequences, per_device, HEADS, head_dim)
    )
    delta = jnp.transpose(jnp.sum(grad_att.astype(jnp.float32) * attended, axis=-1), (0, 2, 1))
    grad_query = jnp.zeros((sequences, per_device, HEADS, head_dim), jnp.float32)
    whole_pairs = lax.all_gather(pair_low, "seq", axis=1, tiled=True)
    whole_len = whole_pairs.shape[1]
    block_size = block_width()
    key_terms = []
    for block_index in range(whole_len // block_size):
        block_pair_piece = whole_pairs[:, block_index * block_size : (block_index + 1) * block_size]
        block_raw_scores, block_allowed, block_key_heads, block_value_heads = block_scores(
            block_pair_piece, block_index * block_size
        )
        prob = jnp.where(block_allowed, jnp.exp(block_raw_scores - log_total[..., None]), 0.0)
        grad_prob = jnp.einsum(
            "sqhe,skhe->shqk", grad_att, block_value_heads, preferred_element_type=jnp.float32
        )
        grad_score = (prob * (grad_prob - delta[..., None])).astype(jnp.bfloat16)
        grad_value = jnp.einsum(
            "shqk,sqhe->skhe",
            prob.astype(jnp.bfloat16),
            grad_att,
            preferred_element_type=jnp.float32,
        )
        grad_key = (
            jnp.einsum("shqk,sqhe->skhe", grad_score, query_low, preferred_element_type=jnp.float32)
            * score_scale
        )
        query_part = (
            jnp.einsum(
                "shqk,skhe->sqhe", grad_score, block_key_heads, preferred_element_type=jnp.float32
            )
            * score_scale
        )
        block_count_keys = block_pair_piece.shape[1]
        pair_part = jnp.concatenate(
            [
                grad_key.reshape(sequences, block_count_keys, model_width),
                grad_value.reshape(sequences, block_count_keys, model_width),
            ],
            axis=-1,
        )
        query_part, pair_part = (query_part, pair_part)
        grad_query = grad_query + query_part
        key_terms.append(pair_part)
    pair_sum = lax.psum_scatter(
        jnp.concatenate(key_terms, axis=1), "seq", scatter_dimension=1, tiled=True
    )
    pair_grad_low = pair_sum.astype(jnp.bfloat16).reshape(-1, 2 * model_width)
    query_grad_low = grad_query.reshape(-1, model_width).astype(jnp.bfloat16)
    query_grad_float = query_grad_low.astype(jnp.float32)
    value_grad_float = pair_grad_low[:, model_width:].astype(jnp.float32)
    grad_wide_q = (query_grad_float * out_scale[0]).astype(jnp.bfloat16)
    grad_wide_v = (value_grad_float * out_scale[1]).astype(jnp.bfloat16)
    grad_rank_q = product_t(grad_wide_q, vera_out)
    grad_rank_v = product_t(grad_wide_v, vera_out)
    grad_rank_in = (grad_rank_q * rank_scale[0] + grad_rank_v * rank_scale[1]).astype(jnp.bfloat16)
    grad_tokens = (
        grad_one
        + product_t(jnp.concatenate([query_grad_low, pair_grad_low], axis=-1), attn_in_weight)
        + product_t(grad_rank_in, vera_in)
    )
    rank_terms = jnp.stack(
        [jnp.sum(grad_rank_q * rank_in, axis=0), jnp.sum(grad_rank_v * rank_in, axis=0)]
    )
    out_terms = jnp.stack(
        [jnp.sum(query_grad_float * wide_q, axis=0), jnp.sum(value_grad_float * wide_v, axis=0)]
    )
    rank_total, out_total = lax.psum((rank_terms, out_terms), ("batch", "seq"))
    scale_norms = jnp.concatenate(
        [
            jnp.sqrt(jnp.sum(rank_total * rank_total, axis=1)),
            jnp.sqrt(jnp.sum(out_total * out_total, axis=1)),
        ]
    )
    return (
        layer_out.astype(jnp.bfloat16).reshape(sequences, per_device, model_width),
        grad_tokens.astype(jnp.bfloat16).reshape(sequences, per_device, model_width),
        rank_total,
        out_total,
        scale_norms,
    )


MESH = pl.DeviceIdType.MESH
BIG = 1e30
F32 = jnp.float32
BF16 = jnp.bfloat16


def fits(mesh):
    return mesh.shape["seq"] == 8 and mesh.shape["batch"] == 4


def dot(left, right):
    return lax.dot_general(left, right, (((1,), (0,)), ((), ())), preferred_element_type=F32)


def dot_nt(left, right):
    return lax.dot_general(left, right, (((1,), (1,)), ((), ())), preferred_element_type=F32)


OWN, SIB, FAR, SIB_FAR, NEAR_FAR, SIB_NEAR_FAR, NEAR, SIB_NEAR = range(8)
PIECES = 4


def layer_kernel(
    tokens,
    attn_in,
    out_w,
    ffn_in,
    ffn_out,
    vera_in,
    vera_out,
    out_grad,
    rank_scale_in,
    out_scale_in,
    gains_in,
    shifts_in,
    ffn_bias_in,
    splits_in,
    layer_out,
    in_grad,
    sums,
    rank_scale,
    out_scale,
    gains,
    shifts,
    ffn_bias,
    splits,
    tok,
    og,
    w_all,
    w_out,
    w_one,
    w_two,
    v_in,
    v_out,
    v_out_t,
    rank_in,
    k_ext,
    q_ext,
    val,
    k_t,
    v_t,
    probs,
    s_buf,
    att_t,
    part_top,
    part_sum,
    part_out,
    share,
    att_send,
    att_recv,
    hid,
    n_one,
    wide,
    low_rows,
    g_two,
    g_one,
    lo_buf,
    ga_send,
    ga_recv,
    ga_mine,
    go_t,
    go_m,
    delta,
    d_kv,
    d_held,
    part_send,
    part_recv,
    part_mine,
    far_terms,
    tn_send,
    tn_recv,
    ig_buf,
    sum_buf,
    sum_recv,
    send_sem,
    recv_sem,
    load_sem,
):
    s = lax.axis_index("seq")
    b = lax.axis_index("batch")
    core = s % 2
    group = s // 4
    sib = s + 1 - 2 * core
    near = s + 2 - 4 * ((s // 2) % 2)
    far = s + 4 - 8 * group
    bx = b + 1 - 2 * (b % 2)
    by = b + 2 - 4 * (b // 2)
    half = pl.multiple_of(core * 384, 384)
    other_half = pl.multiple_of(384 - core * 384, 384)

    def remote(k, src, dst, where):
        return pltpu.make_async_remote_copy(
            src_ref=src,
            dst_ref=dst,
            send_sem=send_sem.at[k],
            recv_sem=recv_sem.at[k],
            device_id=where,
            device_id_type=MESH,
        )

    def local(k, src, dst):
        return pltpu.make_async_copy(src, dst, load_sem.at[k])

    def block(ref, k, n=1):
        return ref.at[pl.ds(128 * k, 128 * n)]

    near_far = far + near - s
    to_sib, to_near, to_far = {"seq": sib}, {"seq": near}, {"seq": far}
    to_near_far = {"seq": near_far}
    to_bx, to_by, to_bxy = {"batch": bx}, {"batch": by}, {"batch": bx + by - b}

    barrier = pltpu.get_barrier_semaphore()
    for where in (to_sib, to_near, to_far, to_near_far, to_bx, to_by, to_bxy):
        pl.semaphore_signal(barrier, inc=1, device_id=where, device_id_type=MESH)

    loads = [
        local(0, tokens.at[group], block(tok, OWN)),
        local(1, vera_in, v_in),
        local(2, vera_out.at[:, pl.ds(half, 384)], v_out),
        local(3, attn_in.at[:, pl.ds(half, 384)], w_all.at[:, pl.ds(0, 384)]),
        local(4, attn_in.at[:, pl.ds(768 + half, 384)], w_all.at[:, pl.ds(384, 384)]),
        local(5, attn_in.at[:, pl.ds(1536 + half, 384)], w_all.at[:, pl.ds(768, 384)]),
        local(6, out_w, w_out),
        local(7, ffn_in, w_one),
        local(8, ffn_out, w_two),
        local(9, out_grad.at[group], og.at[pl.ds(0, 128)]),
    ]
    small_loads = [
        local(12, rank_scale_in, rank_scale),
        local(13, out_scale_in, out_scale),
        local(14, gains_in, gains),
        local(15, shifts_in, shifts),
        local(16, ffn_bias_in, ffn_bias),
        local(17, splits_in, splits),
    ]
    for item in (*loads[1:6], *small_loads, loads[0]):
        item.start()
    pl.semaphore_wait(barrier, 7)

    piece = 128 // PIECES
    send_far, pass_far_near, pass_last = [], [], []
    for k in range(PIECES):
        part = pl.ds(128 * FAR + piece * k, piece)
        near_part = pl.ds(128 * NEAR_FAR + piece * k, piece)
        last_part = pl.ds(128 * SIB_NEAR_FAR + piece * k, piece)
        send_far.append(
            remote(k, tokens.at[1 - group, pl.ds(piece * k, piece)], tok.at[part], to_far)
        )
        pass_far_near.append(remote(PIECES + k, tok.at[part], tok.at[near_part], to_near))
        pass_last.append(remote(2 * PIECES + k, tok.at[near_part], tok.at[last_part], to_sib))
    send_near = remote(12, tokens.at[group], block(tok, NEAR), to_near)
    send_sib = remote(13, tokens.at[group], block(tok, SIB), to_sib)
    pass_far_sib = remote(14, block(tok, FAR), block(tok, SIB_FAR), to_sib)
    pass_near_sib = remote(15, block(tok, NEAR), block(tok, SIB_NEAR), to_sib)
    send_og = remote(16, out_grad.at[1 - group], og.at[pl.ds(128, 128)], to_far)
    outer = (s // 2) % 2 == group
    inner = jnp.logical_not(outer)

    def start_far():
        for item in send_far:
            item.start()

    pl.when(outer)(start_far)
    pl.when(inner)(send_near.start)
    send_sib.start()

    for item in (*small_loads, *loads[1:6]):
        item.wait()
    for item in loads[6:10]:
        item.start()
    for row, at in ((0, 0), (1, 768)):
        scale_row = rank_scale[pl.ds(row, 1), :]
        out_row = out_scale[pl.ds(row, 1), pl.ds(half, 384)]

        def effective(t, _, at=at, scale_row=scale_row, out_row=out_row):
            rows = pl.ds(pl.multiple_of(t * 256, 256), 256)
            scaled = (v_in[rows, :].astype(F32) * scale_row).astype(BF16)
            wide = dot(scaled, v_out[...]) * out_row
            w_all[rows, at : at + 384] = (w_all[rows, at : at + 384].astype(F32) + wide).astype(BF16)
            return 0

        lax.fori_loop(0, 3, effective, 0)
    v_out_t[...] = v_out[...].astype(F32).T.astype(BF16)

    split = splits[group]
    lane = lax.broadcasted_iota(jnp.int32, (128, 128), 1)
    row_at = lax.broadcasted_iota(jnp.int32, (128, 128), 0)
    flip_one, flip_two, flip_four = sib - s, near - s, far - s
    starts = (
        s,
        s + flip_one,
        s + flip_four,
        s + flip_four + flip_one,
        s + flip_two + flip_four,
        s + flip_two + flip_four + flip_one,
        s + flip_two,
        s + flip_two + flip_one,
    )
    for k in range(8):
        first = (starts[k] * 128 + row_at < split).astype(F32)
        second = 1.0 - first
        key_side = jnp.where(lane == 0, first, jnp.where(lane == 1, second, 0.0)).astype(BF16)
        for p in range(3):
            k_ext[p, 128 * k : 128 * k + 128, 128:256] = key_side
        if k < 4:
            query_side = (
                jnp.where(lane == 0, second, jnp.where(lane == 1, first, 0.0)) * (-BIG)
            ).astype(BF16)
            for h in range(6):
                q_ext[h, 128 * k : 128 * k + 128, 128:256] = query_side

    pl.when(outer)(send_near.start)

    shift_q = shifts[0:1, pl.ds(half, 384)]
    shift_v = shifts[1:2, pl.ds(half, 384)]
    low_lane = lax.broadcasted_iota(jnp.int32, (256, 128), 1) < 64

    def project(first, queries, count=256):
        to = slice(128 * first, 128 * first + count)
        rows = tok[to, :]
        made = dot(rows, w_all[...] if queries else w_all[:, 384:1152])
        keys = made[:, made.shape[1] - 768 : made.shape[1] - 384]
        values = made[:, made.shape[1] - 384 :] + shift_v
        low_keys = keys.astype(BF16)
        low_values = values.astype(BF16)
        for p in range(3):
            k_ext[p, to, 0:128] = low_keys[:, 128 * p : 128 * p + 128]
            val[p, to, :] = low_values[:, 128 * p : 128 * p + 128]
        k_t[:, to] = keys.T.astype(BF16)
        v_t[:, to] = values.T.astype(BF16)
        if queries:
            query = made[:, 0:384] + shift_q
            low_query = query.astype(BF16).astype(F32) * 0.125
            for h in range(6):
                p = h // 2
                mine = low_lane if h % 2 == 0 else jnp.logical_not(low_lane)
                masked = jnp.where(mine, low_query[:, 128 * p : 128 * p + 128], 0.0)
                q_ext[h, to, 0:128] = masked.astype(BF16)

    def attend(blocks, first_query, count):
        queries = slice(first_query, first_query + count)
        part_at = blocks[0] // 2
        starts_at = [128 * first for first in blocks]
        peaks, totals, outs = {}, {}, {}

        def scores(h, at):
            part = dot_nt(k_ext[h // 2, at : at + 256, :], q_ext[h, queries, :])
            s_buf[h % 2, at : at + 256, queries] = part
            peak = jnp.max(part, axis=0, keepdims=True)
            peaks[h] = jnp.maximum(peaks[h], peak) if h in peaks else peak

        def weights(h, at):
            weight = jnp.exp(s_buf[h % 2, at : at + 256, queries] - peaks[h])
            total = jnp.sum(weight, axis=0, keepdims=True)
            low_weight = weight.astype(BF16)
            probs[h, at : at + 256, queries] = low_weight
            out = dot(v_t[64 * h : 64 * h + 64, at : at + 256], low_weight)
            totals[h] = totals[h] + total if h in totals else total
            outs[h] = outs[h] + out if h in outs else out

        for at in starts_at:
            scores(0, at)
        for h in range(6):
            for at in starts_at:
                if h < 5:
                    scores(h + 1, at)
                weights(h, at)
            part_top[part_at, h, :, queries] = peaks[h]
            part_sum[part_at, h, :, queries] = totals[h]
            part_out[part_at, 64 * h : 64 * h + 64, queries] = outs[h]

    def combine(first_query, groups):
        queries = slice(first_query, first_query + 256)
        for h in range(6):
            rows_h = slice(64 * h, 64 * h + 64)
            parts = [group_of[0] // 2 for group_of in groups]
            tops = [part_top[k, h, :, queries] for k in parts]
            top = functools.reduce(jnp.maximum, tops)
            shares = [jnp.exp(one - top) for one in tops]
            total = functools.reduce(
                jnp.add, [w * part_sum[k, h, :, queries] for w, k in zip(shares, parts)]
            )
            inverse = 1.0 / total
            shares = [w * inverse for w in shares]
            att_t[rows_h, queries] = functools.reduce(
                jnp.add, [w * part_out[k, rows_h, queries] for w, k in zip(shares, parts)]
            )
            for w, group_of in zip(shares, groups):
                for first in group_of:
                    share[first // 2, h, :, queries] = w

    def rank_rows(first):
        to = slice(128 * first, 128 * first + 256)
        rank_in[to, :] = dot(tok[to, :], v_in[...]).astype(BF16)

    def pass_far():
        for k in range(PIECES):
            send_far[k].wait_recv()
            pass_far_near[k].start()
        pass_far_sib.start()

    def near_blocks():
        send_near.wait_recv()
        pass_near_sib.start()
        pass_near_sib.wait_recv()
        project(NEAR, False)

    def far_blocks():
        pass_far_sib.wait_recv()
        project(FAR, True)

    def pass_last_on():
        for k in range(PIECES):
            pass_far_near[k].wait_recv()
            pass_last[k].start()

    def last_blocks():
        project(NEAR_FAR, False, 128)
        for k in range(PIECES):
            pass_last[k].wait_recv()
        project(SIB_NEAR_FAR, False, 128)

    loads[0].wait()
    send_sib.wait_recv()
    project(OWN, True)
    rank_rows(OWN)
    pl.when(inner)(start_far)
    attend((OWN,), 0, 256)

    @pl.when(inner)
    def _():
        pass_far()
        far_blocks()
        attend((FAR,), 0, 256)
        attend((OWN, FAR), 256, 256)
        near_blocks()
        attend((NEAR,), 0, 512)
        send_og.start()
        rank_rows(NEAR)
        pass_last_on()
        last_blocks()
        attend((NEAR_FAR,), 0, 512)
        combine(0, ((OWN,), (FAR,), (NEAR,), (NEAR_FAR,)))
        combine(256, ((OWN, FAR), (NEAR,), (NEAR_FAR,)))

    @pl.when(outer)
    def _():
        near_blocks()
        attend((NEAR,), 0, 256)
        pass_far()
        rank_rows(NEAR)
        far_blocks()
        attend((FAR,), 0, 256)
        attend((OWN, FAR, NEAR), 256, 256)
        send_og.start()
        pass_last_on()
        last_blocks()
        attend((NEAR_FAR,), 0, 512)
        combine(0, ((OWN,), (FAR,), (NEAR,), (NEAR_FAR,)))
        combine(256, ((OWN, FAR, NEAR), (NEAR_FAR,)))

    swap_att = remote(17, att_send, att_recv, to_sib)
    for k, at in ((0, 128 * SIB), (128, 128 * SIB_FAR)):
        att_send[k : k + 128, :] = att_t[:, at : at + 128].T.astype(BF16)
    swap_att.start()

    def norm(values_in):
        centered = values_in - jnp.mean(values_in, axis=-1, keepdims=True)
        inverse = lax.rsqrt(jnp.mean(centered * centered, axis=-1, keepdims=True) + 1e-05)
        return centered * inverse, inverse

    def norm_back(grad_in, normed, inverse, gain_row):
        scaled = grad_in * gain_row
        return inverse * (
            scaled
            - jnp.mean(scaled, axis=-1, keepdims=True)
            - normed * jnp.mean(scaled * normed, axis=-1, keepdims=True)
        )

    loads[6].wait()
    attended_mine = jnp.concatenate([att_t[:, 0:128], att_t[:, 256:384]], axis=1).T
    token_rows = jnp.concatenate([tok[0:128, :], tok[256:384, :]], axis=0).astype(F32)
    branch = dot(attended_mine.astype(BF16), w_out[pl.ds(half, 384), :])
    rank_rows(FAR)
    rank_rows(NEAR_FAR)
    swap_att.wait_recv()
    branch = branch + dot(att_recv[...], w_out[pl.ds(other_half, 384), :]) + shifts[2:3, :]
    normed_one, inverse_one = norm(token_rows + branch)
    n_one[...] = normed_one
    hidden = normed_one * gains[0:1, :] + shifts[4:5, :]
    hid[...] = hidden
    low_rows[...] = hidden.astype(BF16)

    loads[7].wait()
    loads[8].wait()
    def slope(t):
        return s_buf.at[t // 2048, pl.ds(t % 2048 // 2, 256)]

    for t in range(0, 3072, 512):
        cols = slice(t, t + 512)
        inner = dot(low_rows[...], w_one[:, cols]) + ffn_bias[:, cols]
        phi = 0.5 * (1.0 + lax.erf(inner * 0.7071067811865476))
        density = 0.3989422804014327 * jnp.exp(-0.5 * inner * inner)
        slope(t)[...] = phi + inner * density
        wide[:, cols] = (inner * phi).astype(BF16)
    ffn_branch = dot(wide[...], w_two[...])
    normed_two, inverse_two = norm(hid[...] + ffn_branch + shifts[3:4, :])
    out_rows = (normed_two * gains[1:2, :] + shifts[5:6, :]).astype(BF16)
    lo_buf[...] = out_rows[128:256]
    send_lo = remote(18, lo_buf, layer_out.at[group], to_far)
    send_lo.start()
    layer_out[group] = out_rows[0:128]
    loads[9].wait()
    send_og.wait_recv()
    grad_two = norm_back(og[...].astype(F32), normed_two, inverse_two, gains[1:2, :])
    g_two[...] = grad_two
    low_rows[...] = grad_two.astype(BF16)
    for t in range(0, 3072, 512):
        cols = slice(t, t + 512)
        grad_act = dot_nt(low_rows[...], w_two[cols, :])
        wide[:, cols] = (grad_act * slope(t)[...]).astype(BF16)
    grad_hidden = g_two[...] + dot_nt(wide[...], w_one[...])
    grad_one = norm_back(grad_hidden, n_one[...], inverse_one, gains[0:1, :])
    g_one[...] = grad_one
    low_one = grad_one.astype(BF16)
    swap_ga = remote(19, ga_send, ga_recv, to_sib)
    ga_send[...] = dot_nt(low_one, w_out[pl.ds(other_half, 384), :]).astype(BF16)
    swap_ga.start()
    ga_mine[...] = dot_nt(low_one, w_out[pl.ds(half, 384), :]).astype(BF16)

    low_row = lax.broadcasted_iota(jnp.int32, (128, 128), 0) < 64
    low_col = lax.broadcasted_iota(jnp.int32, (128, 128), 1) < 64

    def spread(block_at, rows):
        to = slice(128 * block_at, 128 * block_at + 128)
        flipped = rows.T
        for p in range(3):
            cols = slice(128 * p, 128 * p + 128)
            for e in range(2):
                h = 2 * p + e
                rows_of = low_row if e == 0 else jnp.logical_not(low_row)
                cols_of = low_col if e == 0 else jnp.logical_not(low_col)
                go_m[h, to, :] = jnp.where(cols_of, rows[:, cols], 0.0).astype(BF16)
                mine = jnp.where(rows_of, flipped[cols, :], 0.0)
                go_t[h, :, to] = mine.astype(BF16)
                delta[h, :, to] = jnp.sum(mine * att_t[cols, to], axis=0, keepdims=True)

    spread(OWN, ga_mine[0:128, :].astype(F32))
    spread(FAR, ga_mine[128:256, :].astype(F32))
    swap_ga.wait_recv()
    spread(SIB, ga_recv[0:128, :].astype(F32))
    spread(SIB_FAR, ga_recv[128:256, :].astype(F32))

    dq_t = part_out.at[0]

    def backward(first, first_query, count, heads=range(6)):
        rows = slice(128 * first, 128 * first + 256)
        queries = slice(first_query, first_query + count)

        def value_dots(h):
            return dot(val[h // 2, rows, :], go_t[h, :, queries])

        grad_prob = value_dots(heads[0])
        for h in heads:
            following = value_dots(h + 1) if h + 1 in heads else None
            weight = probs[h, rows, queries].astype(F32) * share[first // 2, h, :, queries]
            grad_score = (weight * (grad_prob - delta[h, :, queries])).astype(BF16)
            value_part = dot(weight.astype(BF16), go_m[h, queries, :])
            key_part = dot(grad_score, q_ext[h, queries, 0:128])
            rows_h = slice(64 * h, 64 * h + 64)
            query_part = dot(k_t[rows_h, rows], grad_score)
            if first == NEAR_FAR:
                dq_t[rows_h, queries] = query_part
            else:
                dq_t[rows_h, queries] += query_part
            if h % 2 == 0:
                grad_values, grad_keys = value_part, key_part
            else:
                grad_values, grad_keys = grad_values + value_part, grad_keys + key_part
                cols = slice(64 * h - 64, 64 * h + 64)
                value_cols = slice(64 * h + 320, 64 * h + 448)
                if count == 512:
                    d_kv[rows, cols] = grad_keys.astype(BF16)
                    d_kv[rows, value_cols] = grad_values.astype(BF16)
                elif first_query == 256:
                    d_held[:, cols] = grad_keys
                    d_held[:, value_cols] = grad_values
                else:
                    d_kv[rows, cols] = (d_held[:, cols] + grad_keys).astype(BF16)
                    d_kv[rows, value_cols] = (d_held[:, value_cols] + grad_values).astype(BF16)
            grad_prob = following

    def token_terms(start):
        return dot_nt(d_kv[start : start + 256, :], w_all[:, 384:1152])

    swap_parts = [
        remote(20 + k, part_send.at[pl.ds(128 * k, 128)], part_recv.at[pl.ds(128 * k, 128)], to_sib)
        for k in range(4)
    ]
    send_parts = [
        remote(24 + k, tn_send.at[pl.ds(128 * k, 128)], tn_recv.at[pl.ds(128 * k, 128)], to_near)
        for k in range(2)
    ]

    def share_out(k, terms):
        part_send[128 * k : 128 * k + 128, :] = terms[128:256].astype(BF16)
        swap_parts[k].start()
        part_mine[128 * k : 128 * k + 128, :] = terms[0:128]

    def shared(k):
        swap_parts[k].wait_recv()
        rows = slice(128 * k, 128 * k + 128)
        return part_mine[rows, :] + part_recv[rows, :].astype(F32)

    def pass_on(k):
        tn_send[128 * k : 128 * k + 128, :] = shared(k).astype(BF16)
        send_parts[k].start()

    backward(NEAR_FAR, 0, 512)
    share_out(0, token_terms(128 * NEAR_FAR))
    backward(NEAR, 0, 512, range(0, 2))
    pass_on(0)
    backward(NEAR, 0, 512, range(2, 6))
    share_out(1, token_terms(128 * NEAR))
    backward(FAR, 0, 512)
    pass_on(1)
    far_terms[...] = token_terms(128 * FAR)
    backward(OWN, 256, 256)
    low_dq_far = (dq_t[:, 256:512] * 0.125).T.astype(BF16)
    share_out(2, far_terms[...] + dot_nt(low_dq_far, w_all[:, 0:384]))
    backward(OWN, 0, 256)
    far_part = shared(2) + g_one[128:256, :]
    send_parts[0].wait_recv()
    ig_buf[...] = (far_part + tn_recv[0:128, :].astype(F32)).astype(BF16)
    send_ig = remote(26, ig_buf, in_grad.at[group], to_far)
    send_ig.start()

    low_dq_t = (dq_t[...] * 0.125).astype(BF16)
    low_dv_t = d_kv[:, 384:768].astype(F32).T.astype(BF16)
    rank_parts, out_parts = [], []
    for row, product_map in (
        (0, dot(low_dq_t, rank_in[0:512, :])),
        (1, dot(low_dv_t, rank_in[...])),
    ):
        product_map = product_map * v_out_t[...].astype(F32)
        out_row = out_scale[pl.ds(row, 1), pl.ds(half, 384)]
        out_col = jnp.broadcast_to(out_row, (128, 384)).T[:, 0:1]
        rank_part = jnp.sum(product_map * out_col, axis=0, keepdims=True)
        rank_parts += [rank_part[:, 0:512], rank_part[:, 512:1024]]
        out_part = jnp.sum(product_map * rank_scale[pl.ds(row, 1), :], axis=1, keepdims=True)
        out_part = jnp.broadcast_to(out_part, (384, 128)).T[0:1, :]
        out_part = jnp.concatenate([out_part, jnp.zeros((1, 128), F32)], axis=1)
        out_parts += [jnp.where(core == 0, out_part, 0.0), jnp.where(core == 1, out_part, 0.0)]
    for k, part in enumerate(rank_parts + out_parts):
        sum_buf[k : k + 1, :] = part

    def exchange(k, stage, wheres):
        swaps = [
            remote(
                k + n,
                sum_buf.at[pl.ds(8 * stage, 8)],
                sum_recv.at[pl.ds(8 * (k - 27 + n), 8)],
                where,
            )
            for n, where in enumerate(wheres)
        ]
        for swap in swaps:
            swap.start()
        return swaps

    def received(k):
        return sum_recv[8 * k : 8 * k + 8, :]

    core_swaps = exchange(27, 0, (to_sib,))
    low_dq = (dq_t[:, 0:256] * 0.125).T.astype(BF16)
    share_out(3, token_terms(128 * OWN) + dot_nt(low_dq, w_all[:, 0:384]))
    core_swaps[0].wait_recv()
    sum_buf[8:16, :] = sum_buf[0:8, :] + received(0)
    plane_swaps = exchange(28, 1, (to_bx, to_by, to_bxy))
    own_part = shared(3) + g_one[0:128, :]
    for swap in plane_swaps:
        swap.wait_recv()
    sum_buf[16:24, :] = (sum_buf[8:16, :] + received(1)) + (received(2) + received(3))
    line_swaps = exchange(31, 2, (to_near, to_far, to_near_far))
    send_parts[1].wait_recv()
    in_grad[group] = (own_part + tn_recv[128:256, :].astype(F32)).astype(BF16)
    for swap in line_swaps:
        swap.wait_recv()
    sums[...] = (sum_buf[16:24, :] + received(4)) + (received(5) + received(6))

    send_lo.wait_recv()
    send_ig.wait_recv()
    for item in (
        *send_far,
        *pass_far_near,
        *pass_last,
        send_near,
        send_sib,
        pass_far_sib,
        pass_near_sib,
        send_og,
        swap_att,
        swap_ga,
        send_lo,
        *swap_parts,
        *send_parts,
        send_ig,
        *core_swaps,
        *plane_swaps,
        *line_swaps,
    ):
        item.wait_send()


def finish_kernel(layer_in, grad_in, sums, layer_out, in_grad, rank_total, out_total, norms):
    layer_out[...] = layer_in[...]
    in_grad[...] = grad_in[...]
    rank_rows = [jnp.concatenate([sums[k : k + 1], sums[k + 1 : k + 2]], axis=1) for k in (0, 2)]
    out_rows = [
        jnp.concatenate([sums[k : k + 1, 0:384], sums[k + 1 : k + 2, 0:384]], axis=1) for k in (4, 6)
    ]
    for k in range(2):
        rank_total[k : k + 1, :] = rank_rows[k]
        out_total[k : k + 1, :] = out_rows[k]
    for k, row in enumerate(rank_rows + out_rows):
        norms[k] = jnp.sqrt(jnp.sum(row * row, axis=1, keepdims=True))[0, 0]


def fast_body(
    tokens,
    attn_in_weight,
    out_weight,
    ffn_in_weight,
    ffn_out_weight,
    vera_in,
    vera_out,
    rank_scale,
    out_scale,
    gains,
    shifts,
    ffn_bias,
    splits,
    out_grad,
):
    hbm = pl.BlockSpec(memory_space=pl.ANY)
    vmem = pl.BlockSpec(memory_space=pltpu.VMEM)
    smem = pl.BlockSpec(memory_space=pltpu.SMEM)
    shape = tokens.shape
    small = (rank_scale, out_scale, gains, shifts, ffn_bias.reshape(1, -1))
    scratch = [
        ((1024, 768), BF16),
        ((256, 768), BF16),
        ((768, 1152), BF16),
        ((768, 768), BF16),
        ((768, 3072), BF16),
        ((3072, 768), BF16),
        ((768, 1024), BF16),
        ((1024, 384), BF16),
        ((384, 1024), BF16),
        ((1024, 1024), BF16),
        ((3, 1024, 256), BF16),
        ((6, 512, 256), BF16),
        ((3, 1024, 128), BF16),
        ((384, 1024), BF16),
        ((384, 1024), BF16),
        ((6, 1024, 512), BF16),
        ((2, 1024, 512), F32),
        ((384, 512), F32),
        ((4, 6, 1, 512), F32),
        ((4, 6, 1, 512), F32),
        ((4, 384, 512), F32),
        ((4, 6, 1, 512), F32),
        ((256, 384), BF16),
        ((256, 384), BF16),
        ((256, 768), F32),
        ((256, 768), F32),
        ((256, 3072), BF16),
        ((256, 768), BF16),
        ((256, 768), F32),
        ((256, 768), F32),
        ((128, 768), BF16),
        ((256, 384), BF16),
        ((256, 384), BF16),
        ((256, 384), BF16),
        ((6, 128, 512), BF16),
        ((6, 512, 128), BF16),
        ((6, 1, 512), F32),
        ((1024, 768), BF16),
        ((256, 768), F32),
        ((512, 768), BF16),
        ((512, 768), BF16),
        ((512, 768), F32),
        ((256, 768), F32),
        ((256, 768), BF16),
        ((256, 768), BF16),
        ((128, 768), BF16),
        ((24, 512), F32),
        ((56, 512), F32),
    ]
    rows_type = jax.ShapeDtypeStruct(shape, BF16)
    held_rows = pltpu.VMEM(shape, BF16)
    layer_rows, grad_rows, sums = pl.pallas_call(
        layer_kernel,
        out_shape=(held_rows, held_rows, pltpu.VMEM((8, 512), F32)),
        in_specs=[hbm] * 14,
        out_specs=(vmem, vmem, vmem),
        scratch_shapes=[pltpu.VMEM(item.shape, F32) for item in small]
        + [pltpu.SMEM(splits.shape, jnp.int32)]
        + [pltpu.VMEM(dims, kind) for dims, kind in scratch]
        + [
            pltpu.SemaphoreType.DMA((34,)),
            pltpu.SemaphoreType.DMA((34,)),
            pltpu.SemaphoreType.DMA((18,)),
        ],
        compiler_params=pltpu.CompilerParams(
            collective_id=0, has_side_effects=True, vmem_limit_bytes=60 * 2**20
        ),
        name="encoder_layer",
    )(
        tokens,
        attn_in_weight,
        out_weight,
        ffn_in_weight,
        ffn_out_weight,
        vera_in,
        vera_out,
        out_grad,
        *small,
        splits,
    )
    return pl.pallas_call(
        finish_kernel,
        out_shape=(
            rows_type,
            rows_type,
            jax.ShapeDtypeStruct(rank_scale.shape, F32),
            jax.ShapeDtypeStruct(out_scale.shape, F32),
            jax.ShapeDtypeStruct((4,), F32),
        ),
        in_specs=[vmem, vmem, vmem],
        out_specs=(vmem, vmem, vmem, vmem, smem),
        name="finish",
    )(*[pltpu.with_memory_space_constraint(x, pltpu.VMEM) for x in (layer_rows, grad_rows, sums)])


def solution(mesh):
    chosen = fast_body if fits(mesh) else body
    in_specs = (
        P("batch", "seq", None),
        P(),
        P(),
        P(),
        P(),
        P(),
        P(),
        P(),
        P(),
        P(),
        P(),
        P(),
        P("batch"),
        P("batch", "seq", None),
    )
    out_specs = (P("batch", "seq", None), P("batch", "seq", None), P(), P(), P())
    return jax.shard_map(chosen, mesh=mesh, in_specs=in_specs, out_specs=out_specs, check_vma=False)
```
